32 devices in a mesh: dp: 8 (over z, y), fsdp: 4 (over x, core).
Axes of the slice: x: 2, y: 2, z: 4, core: 2. Of those that a mesh axis runs over, the one named last changes fastest.
Arguments:
- tokens: bfloat16 [16384, 1024], P(('dp', 'fsdp')), may hold values from -6 to 6
- lengths: int32 [32, 4], P(('dp', 'fsdp')), may hold values from 0 to 512, as said below
- w_qkv: bfloat16 [1024, 3072], P(('dp', 'fsdp')), may hold values from -0.1875 to 0.1875
- w_out: bfloat16 [1024, 1024], P(('dp', 'fsdp')), may hold values from -0.75 to 0.75
- w_up: bfloat16 [1024, 4096], P(('dp', 'fsdp')), may hold values from -0.1875 to 0.1875
- w_down: bfloat16 [4096, 1024], P(('dp', 'fsdp')), may hold values from -0.09375 to 0.09375
- gain_attn: bfloat16 [1024], P(('dp', 'fsdp')), may hold values from 0.099609375 to 1.8984375
- gain_mlp: bfloat16 [1024], P(('dp', 'fsdp')), may hold values from 0.099609375 to 1.8984375
- cotangent: bfloat16 [16384, 1024], P(('dp', 'fsdp')), may hold values from -6 to 6
Outputs:
- output: bfloat16 [16384, 1024], P(('dp', 'fsdp'))
- grad_tokens: bfloat16 [16384, 1024], P(('dp', 'fsdp'))
- grad_w_qkv: float32 [1024, 3072], P(('dp', 'fsdp'))
- grad_w_out: float32 [1024, 1024], P(('dp', 'fsdp'))
- grad_w_up: float32 [1024, 4096], P(('dp', 'fsdp'))
- grad_w_down: float32 [4096, 1024], P(('dp', 'fsdp'))
- grad_gain_attn: float32 [1024], P(('dp', 'fsdp'))
- grad_gain_mlp: float32 [1024], P(('dp', 'fsdp'))
The draws below stay inside these ranges and needn't reach their ends.
Inputs may be any that keep to these rules, and one draw needn't show every extreme that they name: Row b gives the lengths of the items of bucket b in order; empty slots hold 0 and follow the used ones; each row sums to 512; in every draw some bucket holds a single item of 512 frames.
All inputs are finite; a program needn't handle non-finite values.
Results may differ from the reference program's by a relative error of at most 0.012.
Values may be sent and summed in bfloat16 or wider, within the bound.
A program may use at most 192 MiB of HBM per device.

```python
import math
import jax
import jax.numpy as jnp
from jax import lax

D = 1024
H = 16
HD = 64
FF = 4096
ROWS = 512
SLOTS = 4
TOKENS = 16384
DEVICES = 32


def draw_lengths(key, part):
    key = jax.random.fold_in(key, 11)
    key_count, key_cut, key_whole = jax.random.split(key, 3)
    counts = jax.random.randint(key_count, (DEVICES, 1), 1, SLOTS + 1)
    single = jax.random.randint(key_whole, (), 0, DEVICES)
    counts = jnp.where(jnp.arange(DEVICES)[:, None] == single, 1, counts)
    cut_points = jnp.sort(jax.random.randint(key_cut, (DEVICES, SLOTS - 1), 1, ROWS), axis=1)
    slot_index = jnp.arange(SLOTS - 1)[None, :]
    cut_points = jnp.where(slot_index < counts - 1, cut_points, ROWS)
    bounds = jnp.concatenate([jnp.zeros((DEVICES, 1), jnp.int32), cut_points.astype(jnp.int32), jnp.full((DEVICES, 1), ROWS, jnp.int32)], axis=1)
    return (bounds[:, 1:] - bounds[:, :-1]).astype(jnp.int32)


def block_scale(own_key, dims, cuts, least, largest):
    def one(dim, parts):
        heights = jax.random.uniform(jax.random.fold_in(jax.random.fold_in(own_key, 6), dim), (parts,), jnp.float32, least / len(cuts), largest / len(cuts))
        return jnp.repeat(jnp.exp(heights), dims[dim] // parts).reshape((-1,) + (1,) * (len(dims) - dim - 1))

    level = one(*cuts[0])
    for cut in cuts[1:]:
        level = level * one(*cut)
    return level


def centred(own_key, dims, deviation, most, cuts=(), kind=jnp.bfloat16):
    level = block_scale(own_key, dims, cuts, -0.22, 0.18) if cuts else 1.0
    entries = jax.random.normal(own_key, dims, jnp.float32) * deviation * level
    return jnp.minimum(jnp.maximum(entries, -most), most).astype(kind)


def setup_inputs(seed: int = 0) -> dict:
    streams_of = jax.random.split(jax.random.key(seed), 10)
    return {
        "tokens": centred(streams_of[0], (TOKENS, D), 1.0, 6.0, ((0, 32),)),
        "lengths": draw_lengths(jax.random.fold_in(streams_of[9], 71), 0),
        "w_qkv": centred(streams_of[2], (D, 3 * D), D ** -0.5, 0.1875, ((0, 32),)),
        "w_out": centred(streams_of[3], (D, D), (D // 16) ** -0.5, 0.75, ((0, 32),)),
        "w_up": centred(streams_of[4], (D, FF), D ** -0.5, 0.1875, ((0, 32),)),
        "w_down": centred(streams_of[5], (FF, D), FF ** -0.5, 0.09375, ((0, 32),)),
        "gain_attn": jnp.clip(1.0 + 0.18 * jax.random.normal(streams_of[6], (D,), jnp.float32), 0.099609375, 1.8984375).astype(jnp.bfloat16),
        "gain_mlp": jnp.clip(1.0 + 0.18 * jax.random.normal(streams_of[7], (D,), jnp.float32), 0.099609375, 1.8984375).astype(jnp.bfloat16),
        "cotangent": centred(streams_of[8], (TOKENS, D), 1.0, 6.0, ((0, 32),)),
    }


@jax.custom_vjp
def low(v):
    return lax.optimization_barrier(v.astype(jnp.bfloat16)).astype(jnp.float32)

@jax.custom_vjp
def low_back(v):
    return v

def low_keep(v):
    return (low(v), None)

def low_pass(kept, grad):
    return (grad,)

def back_keep(v):
    return (v, None)

def back_low(kept, grad):
    return (low(grad),)
low.defvjp(low_keep, low_pass)
low_back.defvjp(back_keep, back_low)
epsilon = 1e-05
highest = lax.Precision.HIGHEST

def normalize(values, gain):
    return values * lax.rsqrt(lax.optimization_barrier(jnp.mean(values * values, axis=-1, keepdims=True)) + epsilon) * gain

def attend(inputs):
    queries, keys_all, values_all, segment = inputs
    raw = jnp.einsum('qhd,khd->hqk', queries, keys_all, precision=highest)
    logits = low_back(raw) * (1.0 / math.sqrt(HD))
    places = jnp.arange(ROWS, dtype=jnp.int32)
    allowed = (segment[:, None] == segment[None, :]) & (places[:, None] >= places[None, :])
    logits = jnp.where(allowed[None], logits, -1e+30)
    shifted = logits - lax.optimization_barrier(jnp.max(logits, axis=-1, keepdims=True))
    raised = jnp.exp(shifted)
    attn_prob = raised / lax.optimization_barrier(jnp.sum(raised, axis=-1, keepdims=True))
    return jnp.einsum('hqk,khd->qhd', low(attn_prob), values_all, precision=highest)

def reference(tokens, lengths, w_qkv, w_out, w_up, w_down, gain_attn, gain_mlp, cotangent):
    ends = jnp.cumsum(lengths, axis=1)
    places = jnp.arange(ROWS, dtype=jnp.int32)
    segments = lax.optimization_barrier(jnp.sum((places[None, :, None] >= ends[:, None, :]).astype(jnp.int32), axis=2)).astype(jnp.int32)

    def forward(tokens_f, w_qkv_f, w_out_f, w_up_f, w_down_f, gain_attn_f, gain_mlp_f):
        normed = low(normalize(tokens_f, gain_attn_f))
        mixed = low_back(low(jnp.dot(normed, w_qkv_f, precision=highest)))
        split = mixed.reshape(DEVICES, ROWS, 3, H, HD)
        context = lax.map(jax.checkpoint(attend), (split[:, :, 0], split[:, :, 1], split[:, :, 2], segments))
        merged = low_back(low(context.reshape(TOKENS, D)))
        middle = tokens_f + low_back(jnp.dot(merged, w_out_f, precision=highest))
        second = low(normalize(middle, gain_mlp_f))
        hidden = low_back(jnp.dot(second, w_up_f, precision=highest))
        active = low(jax.nn.gelu(hidden, approximate=True))
        return middle + jnp.dot(active, w_down_f, precision=highest)
    result, pullback = jax.vjp(forward, tokens.astype(jnp.float32), w_qkv.astype(jnp.float32), w_out.astype(jnp.float32), w_up.astype(jnp.float32), w_down.astype(jnp.float32), gain_attn.astype(jnp.float32), gain_mlp.astype(jnp.float32))
    grads = pullback(cotangent.astype(jnp.float32))
    return (result.astype(jnp.bfloat16), grads[0].astype(jnp.bfloat16), grads[1], grads[2], grads[3], grads[4], grads[5], grads[6])
```

```python
import functools
import math

import jax
import jax.numpy as jnp
from jax import lax
from jax.experimental import pallas as pl
from jax.experimental.pallas import tpu as pltpu
from jax.sharding import PartitionSpec as P

H = 16
HD = 64
MESH = pl.DeviceIdType.MESH
AXES = ("dp", "fsdp")


epsilon = 1e-05


def normalize(values, gain):
    scale_row = lax.rsqrt(jnp.mean(values * values, axis=-1, keepdims=True) + epsilon)
    return (values * scale_row * gain, scale_row)


def norm_back(grad_normed, values, scale_row, gain):
    scaled = grad_normed * gain
    grad_gain = jnp.sum(grad_normed * values * scale_row, axis=0)
    cubed = scale_row * scale_row * scale_row
    grad_values = scale_row * scaled - values * cubed * jnp.mean(
        scaled * values, axis=-1, keepdims=True
    )
    return (grad_values, grad_gain)


def block_logits(query_block, key_rows, segment):
    block_rows = query_block.shape[0]
    key_limit = key_rows.shape[0]
    raw = jnp.einsum("qhd,khd->hqk", query_block, key_rows, preferred_element_type=jnp.float32)
    query_place = jnp.arange(block_rows, dtype=jnp.int32)
    key_place = jnp.arange(key_limit, dtype=jnp.int32)
    allowed = (segment[:, None] == segment[None, :]) & (query_place[:, None] >= key_place[None, :])
    return jnp.where(allowed[None], raw * (1.0 / math.sqrt(HD)), -1e30)


def attend_forward(queries, keys_all, values_all, segment):
    logits = block_logits(queries, keys_all, segment)
    peak = jnp.max(logits, axis=-1, keepdims=True)
    raised = jnp.exp(logits - peak)
    totals = jnp.sum(raised, axis=-1, keepdims=True)
    attn_prob = (raised / totals).astype(jnp.bfloat16)
    contexts = jnp.einsum("hqk,khd->qhd", attn_prob, values_all, preferred_element_type=jnp.float32)
    log_sums = (peak + jnp.log(totals))[:, :, 0]
    return (contexts, log_sums)


def attend_backward(queries, keys_all, values_all, segment, log_sums, grad_context):
    logits = block_logits(queries, keys_all, segment)
    attn_prob = jnp.exp(logits - log_sums[:, :, None])
    rounded = attn_prob.astype(jnp.bfloat16)
    grad_prob = jnp.einsum(
        "qhd,khd->hqk", grad_context, values_all, preferred_element_type=jnp.float32
    )
    inner = jnp.sum(attn_prob * grad_prob, axis=-1, keepdims=True)
    grad_logit = (1.0 / math.sqrt(HD) * attn_prob * (grad_prob - inner)).astype(jnp.bfloat16)
    grad_queries = jnp.einsum(
        "hqk,khd->qhd", grad_logit, keys_all, preferred_element_type=jnp.float32
    )
    grad_keys = jnp.einsum("hqk,qhd->khd", grad_logit, queries, preferred_element_type=jnp.float32)
    grad_values = jnp.einsum(
        "hqk,qhd->khd", rounded, grad_context, preferred_element_type=jnp.float32
    )
    return (grad_queries, grad_keys, grad_values)


def gather_any(*weights):
    return tuple(lax.all_gather(w, AXES, axis=0, tiled=True) for w in weights)


def sum_any(*grads):
    return tuple(lax.psum_scatter(g, AXES, scatter_dimension=0, tiled=True) for g in grads)


NZ = 4


def coords():
    a, b = lax.axis_index("dp"), lax.axis_index("fsdp")
    return a // 2, a % 2, b // 2, b % 2


def device(z, y, x, c):
    return (z * 2 + y, x * 2 + c)


def owner(z, y, x, c):
    return ((z * 2 + y) * 2 + x) * 2 + c


def all_peers(z, y, x, c):
    peers = []
    for d in range(NZ):
        for m in range(2):
            for l in range(2):
                for s in range(2):
                    if d + m + l + s:
                        peers.append(
                            device(
                                lax.rem(z + d, NZ),
                                1 - y if m else y,
                                1 - x if l else x,
                                1 - c if s else c,
                            )
                        )
    return peers


def greet(peers):
    sem = pltpu.get_barrier_semaphore()
    for peer in peers:
        pl.semaphore_signal(sem, inc=1, device_id=peer, device_id_type=MESH)
    pl.semaphore_wait(sem, len(peers))


def remote(src, dst, send_sem, recv_sem, peer):
    return pltpu.make_async_remote_copy(
        src_ref=src, dst_ref=dst, send_sem=send_sem, recv_sem=recv_sem,
        device_id=peer, device_id_type=MESH,
    )


def gather_kernel(nw, *refs):
    ins, outs = refs[:nw], refs[nw : 2 * nw]
    gain_in, gain_out = refs[2 * nw], refs[2 * nw + 1]
    lsem, ssem, rsem, gs, gr = refs[2 * nw + 2 :]
    z, y, x, c = coords()
    zfrom = [lax.rem(z + NZ - d, NZ) for d in range(NZ)]
    ypeer, xpeer, speer = device(z, 1 - y, x, c), device(z, y, 1 - x, c), device(z, y, x, 1 - c)
    zpeers = [device(lax.rem(z + d, NZ), y, x, c) for d in range(1, NZ)]
    peers = all_peers(z, y, x, c)
    greet(peers)
    pend = []
    me = owner(z, y, x, c)
    gain_copies = []
    for j, peer in enumerate(peers):
        cp = remote(gain_in, gain_out.at[j + 1], gs.at[j], gr.at[j], peer)
        cp.start()
        gain_copies.append(cp)
    own_gain = pltpu.make_async_copy(gain_in, gain_out.at[0], lsem.at[nw])
    own_gain.start()

    def rows(w, p, o):
        r = ins[w].shape[0] // 2
        return pl.ds(pl.multiple_of(o * (2 * r) + p * r, r), r)

    def send(w, p, o, k, peer, own=False):
        r = ins[w].shape[0] // 2
        dst = outs[w].at[rows(w, p, o)]
        src = ins[w].at[pl.ds(p * r, r)] if own else dst
        cp = remote(src, dst, ssem.at[w, p, k], rsem.at[w, p, k], peer)
        cp.start()
        pend.append(cp)

    def wait(w, p, o, k):
        ref = outs[w].at[rows(w, p, o)]
        remote(ref, ref, ssem.at[w, p, k], rsem.at[w, p, k], speer).wait_recv()

    def sib(w, p, o, i, own=False):
        send(w, p, o, 15 + i, speer, own)

    def whose(p, d, m, l, core):
        sy, sx = (m, l) if p == 0 else (l, m)
        return owner(zfrom[d], (1 - y) if sy else y, (1 - x) if sx else x, core)

    second, third = [ypeer, xpeer], [xpeer, ypeer]
    local = [own_gain]

    def start(w):
        for p in range(2):
            o = whose(p, 0, 0, 0, c)
            send(w, p, o, 3, second[p], True)
            send(w, p, o, 7, third[p], True)
            for d in range(1, NZ):
                send(w, p, o, d - 1, zpeers[d - 1], True)
            sib(w, p, o, 0, True)
        n = ins[w].shape[0]
        cp = pltpu.make_async_copy(
            ins[w], outs[w].at[pl.ds(pl.multiple_of(me * n, n), n)], lsem.at[w]
        )
        cp.start()
        local.append(cp)

    def from_z(w):
        for d in (1, 3, 2):
            for p in range(2):
                o = whose(p, d, 0, 0, c)
                wait(w, p, o, d - 1)
                send(w, p, o, 3 + d, second[p])
                send(w, p, o, 7 + d, third[p])
                sib(w, p, o, d)

    def from_second(w):
        for d in (0, 1, 3, 2):
            for p in range(2):
                o = whose(p, d, 1, 0, c)
                wait(w, p, o, 3 + d)
                send(w, p, o, 11 + d, third[p])
                sib(w, p, o, 4 + d)

    def from_third(w):
        for m in (0, 1):
            for d in (0, 1, 3, 2):
                for p in range(2):
                    o = whose(p, d, m, 1, c)
                    wait(w, p, o, 7 + m * 4 + d)
                    sib(w, p, o, 8 + m * 4 + d)

    def from_core(w):
        for p in range(2):
            for l in (0, 1):
                for m in (0, 1):
                    for d in range(4):
                        wait(w, p, whose(p, d, m, l, 1 - c), 15 + l * 8 + m * 4 + d)

    for t in range(nw + 4):
        for step, lag in ((start, 0), (from_z, 1), (from_second, 2), (from_third, 3), (from_core, 4)):
            if 0 <= t - lag < nw:
                step(t - lag)
    for cp in gain_copies:
        cp.wait()
    for cp in pend:
        cp.wait_send()
    for cp in local:
        cp.wait()


def gather(weights, gains):
    nw = len(weights)
    hbm = pl.BlockSpec(memory_space=pl.ANY)
    out = pl.pallas_call(
        functools.partial(gather_body, nw),
        out_shape=[jax.ShapeDtypeStruct((w.shape[0] * 32, w.shape[1]), w.dtype) for w in weights]
        + [jax.ShapeDtypeStruct((32, 8, 128), jnp.float32)],
        in_specs=[hbm] * (nw + 1),
        out_specs=[hbm] * (nw + 1),
        scratch_shapes=[
            pltpu.SemaphoreType.DMA((nw + 1,)),
            pltpu.SemaphoreType.DMA((nw, 2, 31)),
            pltpu.SemaphoreType.DMA((nw, 2, 31)),
            pltpu.SemaphoreType.DMA((31,)),
            pltpu.SemaphoreType.DMA((31,)),
        ],
        compiler_params=pltpu.CompilerParams(collective_id=0, has_side_effects=True),
    )(*weights, gains)
    return out[:nw], out[nw]


def gather_body(nw, *refs):
    ins, gain_in = refs[:nw], refs[nw]
    outs, gain_out = refs[nw + 1 : 2 * nw + 1], refs[2 * nw + 1]
    gather_kernel(nw, *ins, *outs, gain_in, gain_out, *refs[2 * nw + 2 :])


UNITS = ((0, 0, 1024), (1, 0, 4096), (2, 0, 1024), (3, 0, 1024), (3, 1024, 1024), (3, 2048, 1024))


def scatter_kernel(dims, *refs):
    nu = len(UNITS)
    grads, gain_in = refs[:4], refs[4]
    outs, gain_out = refs[5:9], refs[9]
    refs = refs[10:]
    mine, got0, got1, got2, got3, res = (refs[i * nu : (i + 1) * nu] for i in range(6))
    got_gain, ssem, rsem, lsem, osem, gs, gr = refs[6 * nu :]
    z, y, x, c = coords()
    ypeer, xpeer, speer = device(z, 1 - y, x, c), device(z, y, 1 - x, c), device(z, y, x, 1 - c)
    zof = [lax.rem(z + d, NZ) for d in range(NZ)]
    zpeers = [device(zof[d], y, x, c) for d in range(NZ)]
    peers = all_peers(z, y, x, c)
    greet(peers)
    pend = []

    def send(u, k, src, dst, peer):
        cp = remote(src, dst, ssem.at[u, k], rsem.at[u, k], peer)
        cp.start()
        pend.append(cp)

    def wait(u, k, ref):
        remote(ref, ref, ssem.at[u, k], rsem.at[u, k], speer).wait_recv()

    def add(dst, src):
        dst[...] = (dst[...].astype(jnp.float32) + src[...].astype(jnp.float32)).astype(dst.dtype)

    def stage0(u):
        w, col, width = UNITS[u]
        src = grads[w].at[:, :, :, :, :, pl.ds(col, width)]
        send(u, 0, src.at[:, :, :, 1 - c], got0[u], speer)
        cp = pltpu.make_async_copy(src.at[:, :, :, c], mine[u], lsem.at[u])
        cp.start()

    def stage1(u):
        w, col, width = UNITS[u]
        src = grads[w].at[:, :, :, c, :, pl.ds(col, width)]
        h = mine[u].shape[3] // 2
        pltpu.make_async_copy(src, mine[u], lsem.at[u]).wait()
        wait(u, 0, got0[u])
        lo, hi = pl.ds(0, h), pl.ds(h, h)
        for far in (True, False):
            xx, yy = (1 - x, 1 - y) if far else (x, y)

            @pl.loop(0, NZ)
            def _(k):
                for j in range(2):
                    add(mine[u].at[k, j, xx, lo], got0[u].at[k, j, xx, lo])
                    add(mine[u].at[k, yy, j, hi], got0[u].at[k, yy, j, hi])

            if far:
                send(u, 1, mine[u].at[:, :, xx, lo], got1[u].at[0], xpeer)
                send(u, 2, mine[u].at[:, yy, :, hi], got1[u].at[1], ypeer)

    def stage2(u):
        h = mine[u].shape[3] // 2
        lo, hi = pl.ds(0, h), pl.ds(h, h)
        wait(u, 1, got1[u].at[0])
        wait(u, 2, got1[u].at[1])
        for far in (True, False):
            xx, yy = (1 - x, 1 - y) if far else (x, y)

            @pl.loop(0, NZ)
            def _(k):
                add(mine[u].at[k, yy, x, lo], got1[u].at[0, k, yy])
                add(mine[u].at[k, y, xx, hi], got1[u].at[1, k, xx])

            if far:
                send(u, 3, mine[u].at[:, yy, x, lo], got2[u].at[0], ypeer)
                send(u, 4, mine[u].at[:, y, xx, hi], got2[u].at[1], xpeer)

    def stage3(u):
        h = mine[u].shape[3] // 2
        lo, hi = pl.ds(0, h), pl.ds(h, h)
        wait(u, 3, got2[u].at[0])
        wait(u, 4, got2[u].at[1])

        @pl.loop(0, NZ)
        def _(k):
            add(mine[u].at[k, y, x, lo], got2[u].at[0, k])
            add(mine[u].at[k, y, x, hi], got2[u].at[1, k])

        for d in range(1, NZ):
            send(u, 4 + d, mine[u].at[zof[d], y, x], got3[u].at[d - 1], zpeers[d])

    def stage4(u):
        w, col, width = UNITS[u]
        for d in range(1, NZ):
            wait(u, 4 + d, got3[u].at[d - 1])
        total = mine[u][z, y, x].astype(jnp.float32)
        for d in range(1, NZ):
            total = total + got3[u][d - 1].astype(jnp.float32)
        res[u][...] = total
        cp = pltpu.make_async_copy(res[u], outs[w].at[:, pl.ds(col, width)], osem.at[u])
        cp.start()
        finals.append(cp)

    finals = []
    gain_copies = []
    for j, (peer, o) in enumerate(zip(peers, peers)):
        block = (o[0] * 4 + o[1]) // 4
        cp = remote(gain_in.at[block], got_gain.at[j + 1], gs.at[j], gr.at[j], peer)
        cp.start()
        gain_copies.append(cp)
    for t in range(nu + 4):
        for step, lag in ((stage4, 4), (stage3, 3), (stage2, 2), (stage1, 1), (stage0, 0)):
            if 0 <= t - lag < nu:
                step(t - lag)
    for cp in gain_copies:
        cp.wait()
    got_gain[0] = gain_in[owner(z, y, x, c) // 4]
    total = got_gain[0]
    for j in range(1, 32):
        total = total + got_gain[j]
    gain_out[...] = total
    for cp in pend:
        cp.wait_send()
    for cp in finals:
        cp.wait()


def scatter(grads, gains):
    hbm = pl.BlockSpec(memory_space=pl.ANY)
    vmem = pl.BlockSpec(memory_space=pltpu.VMEM)
    dims = [(g.shape[4], g.shape[5]) for g in grads]
    scratch = []
    per = [(dims[w][0], width) for w, col, width in UNITS]
    for r, n in per:
        scratch.append(pltpu.VMEM((4, 2, 2, r, n), jnp.bfloat16))
    for r, n in per:
        scratch.append(pltpu.VMEM((4, 2, 2, r, n), jnp.bfloat16))
    for r, n in per:
        scratch.append(pltpu.VMEM((2, 4, 2, r // 2, n), jnp.bfloat16))
    for r, n in per:
        scratch.append(pltpu.VMEM((2, 4, r // 2, n), jnp.bfloat16))
    for r, n in per:
        scratch.append(pltpu.VMEM((3, r, n), jnp.bfloat16))
    for r, n in per:
        scratch.append(pltpu.VMEM((r, n), jnp.float32))
    nu = len(UNITS)
    scratch += [
        pltpu.VMEM((32, 8, 128), jnp.float32),
        pltpu.SemaphoreType.DMA((nu, 8)),
        pltpu.SemaphoreType.DMA((nu, 8)),
        pltpu.SemaphoreType.DMA((nu,)),
        pltpu.SemaphoreType.DMA((nu,)),
        pltpu.SemaphoreType.DMA((31,)),
        pltpu.SemaphoreType.DMA((31,)),
    ]
    return pl.pallas_call(
        functools.partial(scatter_kernel, dims),
        out_shape=[jax.ShapeDtypeStruct(d, jnp.float32) for d in dims]
        + [jax.ShapeDtypeStruct((8, 128), jnp.float32)],
        in_specs=[hbm] * 4 + [vmem],
        out_specs=[hbm] * 4 + [vmem],
        scratch_shapes=scratch,
        compiler_params=pltpu.CompilerParams(
            collective_id=1, has_side_effects=True, vmem_limit_bytes=60 << 20
        ),
    )(*grads, gains)


def project_input(inputs, w_qkv, gain):
    normed, scale_one = normalize(inputs, gain)
    normed_low = normed.astype(jnp.bfloat16)
    mixed = jnp.dot(normed_low, w_qkv, preferred_element_type=jnp.float32).astype(jnp.bfloat16)
    split = mixed.reshape(inputs.shape[0], 3, H, HD)
    return (normed_low, scale_one, split[:, 0], split[:, 1], split[:, 2])


def feed_inputs(inputs, context, w_out, w_up, gain):
    middle = inputs + jnp.dot(context, w_out, preferred_element_type=jnp.float32)
    second, scale_two = normalize(middle, gain)
    second_low = second.astype(jnp.bfloat16)
    hidden = jnp.dot(second_low, w_up, preferred_element_type=jnp.float32)
    active = jax.nn.gelu(hidden, approximate=True).astype(jnp.bfloat16)
    return (middle, scale_two, second_low, hidden, active)


def layer(tokens, lengths, w_qkv, w_out, w_up, w_down, gain_attn, gain_mlp, cotangent, low_type):
    total_rows = tokens.shape[0]
    ends = jnp.cumsum(lengths[0])
    places = jnp.arange(total_rows, dtype=jnp.int32)
    segment = jnp.sum((places[:, None] >= ends[None, :]).astype(jnp.int32), axis=1)
    inputs = tokens.astype(jnp.float32)
    gain_attn, gain_mlp = gain_attn.astype(jnp.float32), gain_mlp.astype(jnp.float32)
    normed_low, scale_one, queries, keys_all, values_all = project_input(inputs, w_qkv, gain_attn)
    context_full, log_sums = attend_forward(queries, keys_all, values_all, segment)
    context = context_full.reshape(total_rows, H * HD).astype(jnp.bfloat16)
    middle, scale_two, second_low, hidden, active = feed_inputs(
        inputs, context, w_out, w_up, gain_mlp
    )
    output = (middle + jnp.dot(active, w_down, preferred_element_type=jnp.float32)).astype(
        jnp.bfloat16
    )
    grad_down = jnp.einsum("rf,rd->fd", active, cotangent, preferred_element_type=low_type)
    grad_active = jnp.einsum("rd,fd->rf", cotangent, w_down, preferred_element_type=jnp.float32)
    unused, gelu_pull = jax.vjp(lambda values: jax.nn.gelu(values, approximate=True), hidden)
    grad_hidden = gelu_pull(grad_active)[0].astype(jnp.bfloat16)
    grad_up = jnp.einsum("rd,rf->df", second_low, grad_hidden, preferred_element_type=low_type)
    grad_second = jnp.einsum("rf,df->rd", grad_hidden, w_up, preferred_element_type=jnp.float32)
    grad_mid_norm, grad_gain_m = norm_back(grad_second, middle, scale_two, gain_mlp)
    grad_middle = cotangent.astype(jnp.float32) + grad_mid_norm
    grad_mid_low = grad_middle.astype(jnp.bfloat16)
    grad_out = jnp.einsum("rc,rd->cd", context, grad_mid_low, preferred_element_type=low_type)
    grad_context = jnp.einsum("rd,cd->rc", grad_mid_low, w_out, preferred_element_type=jnp.float32)
    grad_context = grad_context.astype(jnp.bfloat16).reshape(total_rows, H, HD)
    grad_queries, grad_keys, grad_values = attend_backward(
        queries, keys_all, values_all, segment, log_sums, grad_context
    )
    grad_mixed = (
        jnp.stack([grad_queries, grad_keys, grad_values], axis=1)
        .reshape(total_rows, 3 * H * HD)
        .astype(jnp.bfloat16)
    )
    grad_qkv = jnp.einsum("rd,re->de", normed_low, grad_mixed, preferred_element_type=low_type)
    grad_normed = jnp.einsum("re,de->rd", grad_mixed, w_qkv, preferred_element_type=jnp.float32)
    grad_in_norm, grad_gain_a = norm_back(grad_normed, inputs, scale_one, gain_attn)
    grad_tokens = (grad_middle + grad_in_norm).astype(jnp.bfloat16)
    return (output, grad_tokens, grad_qkv, grad_out, grad_up, grad_down, grad_gain_a, grad_gain_m)


def shards_any(tokens, lengths, w_qkv, w_out, w_up, w_down, gain_attn, gain_mlp, cotangent):
    whole = gather_any(w_qkv, w_out, w_up, w_down, gain_attn, gain_mlp)
    out = layer(tokens, lengths, *whole, cotangent, jnp.float32)
    return out[:2] + sum_any(*out[2:])


def shards(tokens, lengths, w_qkv, w_out, w_up, w_down, gain_attn, gain_mlp, cotangent):
    me = lax.axis_index("dp") * 4 + lax.axis_index("fsdp")
    lanes = lax.rem(me, 4) * 32
    pair = jnp.stack([gain_attn, gain_mlp]).astype(jnp.float32)
    spot = lax.dynamic_update_slice(jnp.zeros((8, 128), jnp.float32), pair, (0, lanes))
    (f_qkv, f_out, f_up, f_down), gains = gather((w_qkv, w_out, w_up, w_down), spot)
    z, y, x, c = coords()
    order = jnp.stack([me] + [o[0] * 4 + o[1] for o in all_peers_from(z, y, x, c)])
    whole = jnp.zeros((32, 8, 128), jnp.float32).at[order].set(gains)
    whole = whole.reshape(8, 4, 8, 128).sum(axis=1)
    f_ga, f_gm = whole[:, 0].reshape(1024), whole[:, 1].reshape(1024)
    out = layer(tokens, lengths, f_qkv, f_out, f_up, f_down, f_ga, f_gm, cotangent, jnp.bfloat16)
    grad_gain = jnp.stack([out[6].reshape(8, 128), out[7].reshape(8, 128)], axis=1)
    grad_gain = jnp.pad(grad_gain, ((0, 0), (0, 6), (0, 0)))
    split = lambda g: g.reshape(4, 2, 2, 2, g.shape[0] // 32, g.shape[1])
    g_down, g_up, g_out, g_qkv, g_gain = scatter(
        (split(out[5]), split(out[4]), split(out[3]), split(out[2])), grad_gain
    )
    own = lax.dynamic_slice(g_gain, (0, lanes), (2, 32))
    return (out[0], out[1], g_qkv, g_out, g_up, g_down, own[0], own[1])


def all_peers_from(z, y, x, c):
    peers = []
    for d in range(NZ):
        for m in range(2):
            for l in range(2):
                for s in range(2):
                    if d + m + l + s:
                        peers.append(
                            device(
                                lax.rem(z + NZ - d, NZ),
                                1 - y if m else y,
                                1 - x if l else x,
                                1 - c if s else c,
                            )
                        )
    return peers


def solution(mesh):
    rows, flat = P(AXES, None), P(AXES)
    known = dict(mesh.shape) == {"dp": 8, "fsdp": 4}
    return jax.shard_map(
        shards if known else shards_any,
        mesh=mesh,
        in_specs=(rows, rows, rows, rows, rows, rows, flat, flat, rows),
        out_specs=(rows, rows, rows, rows, rows, rows, flat, flat),
        check_vma=False,
    )
```

```python
import functools
import math

import jax
import jax.numpy as jnp
from jax import lax
from jax.experimental import pallas as pl
from jax.experimental.pallas import tpu as pltpu
from jax.sharding import PartitionSpec as P

H = 16
HD = 64
MESH = pl.DeviceIdType.MESH
AXES = ("dp", "fsdp")


epsilon = 1e-05


def normalize(values, gain):
    scale_row = lax.rsqrt(jnp.mean(values * values, axis=-1, keepdims=True) + epsilon)
    return (values * scale_row * gain, scale_row)


def norm_back(grad_normed, values, scale_row, gain):
    scaled = grad_normed * gain
    grad_gain = jnp.sum(grad_normed * values * scale_row, axis=0)
    cubed = scale_row * scale_row * scale_row
    grad_values = scale_row * scaled - values * cubed * jnp.mean(
        scaled * values, axis=-1, keepdims=True
    )
    return (grad_values, grad_gain)


def block_logits(query_block, key_rows, segment):
    block_rows = query_block.shape[0]
    key_limit = key_rows.shape[0]
    raw = jnp.einsum("qhd,khd->hqk", query_block, key_rows, preferred_element_type=jnp.float32)
    query_place = jnp.arange(block_rows, dtype=jnp.int32)
    key_place = jnp.arange(key_limit, dtype=jnp.int32)
    allowed = (segment[:, None] == segment[None, :]) & (query_place[:, None] >= key_place[None, :])
    return jnp.where(allowed[None], raw * (1.0 / math.sqrt(HD)), -1e30)


def attend_forward(queries, keys_all, values_all, segment):
    logits = block_logits(queries, keys_all, segment)
    peak = jnp.max(logits, axis=-1, keepdims=True)
    raised = jnp.exp(logits - peak)
    totals = jnp.sum(raised, axis=-1, keepdims=True)
    attn_prob = (raised / totals).astype(jnp.bfloat16)
    contexts = jnp.einsum("hqk,khd->qhd", attn_prob, values_all, preferred_element_type=jnp.float32)
    log_sums = (peak + jnp.log(totals))[:, :, 0]
    return (contexts, log_sums)


def attend_backward(queries, keys_all, values_all, segment, log_sums, grad_context):
    logits = block_logits(queries, keys_all, segment)
    attn_prob = jnp.exp(logits - log_sums[:, :, None])
    rounded = attn_prob.astype(jnp.bfloat16)
    grad_prob = jnp.einsum(
        "qhd,khd->hqk", grad_context, values_all, preferred_element_type=jnp.float32
    )
    inner = jnp.sum(attn_prob * grad_prob, axis=-1, keepdims=True)
    grad_logit = (1.0 / math.sqrt(HD) * attn_prob * (grad_prob - inner)).astype(jnp.bfloat16)
    grad_queries = jnp.einsum(
        "hqk,khd->qhd", grad_logit, keys_all, preferred_element_type=jnp.float32
    )
    grad_keys = jnp.einsum("hqk,qhd->khd", grad_logit, queries, preferred_element_type=jnp.float32)
    grad_values = jnp.einsum(
        "hqk,qhd->khd", rounded, grad_context, preferred_element_type=jnp.float32
    )
    return (grad_queries, grad_keys, grad_values)


def gather_any(*weights):
    return tuple(lax.all_gather(w, AXES, axis=0, tiled=True) for w in weights)


def sum_any(*grads):
    return tuple(lax.psum_scatter(g, AXES, scatter_dimension=0, tiled=True) for g in grads)


NZ = 4


def coords():
    a, b = lax.axis_index("dp"), lax.axis_index("fsdp")
    return a // 2, a % 2, b // 2, b % 2


def device(z, y, x, c):
    return (z * 2 + y, x * 2 + c)


def owner(z, y, x, c):
    return ((z * 2 + y) * 2 + x) * 2 + c


def all_peers(z, y, x, c):
    peers = []
    for d in range(NZ):
        for m in range(2):
            for l in range(2):
                for s in range(2):
                    if d + m + l + s:
                        peers.append(
                            device(
                                lax.rem(z + d, NZ),
                                1 - y if m else y,
                                1 - x if l else x,
                                1 - c if s else c,
                            )
                        )
    return peers


def greet(peers):
    sem = pltpu.get_barrier_semaphore()
    for peer in peers:
        pl.semaphore_signal(sem, inc=1, device_id=peer, device_id_type=MESH)
    pl.semaphore_wait(sem, len(peers))


def remote(src, dst, send_sem, recv_sem, peer):
    return pltpu.make_async_remote_copy(
        src_ref=src, dst_ref=dst, send_sem=send_sem, recv_sem=recv_sem,
        device_id=peer, device_id_type=MESH,
    )


FORWARD = 512
SHARDS = ((32, 3072), (32, 1024), (32, 4096), (128, 1024))
PARTS = (
    (0, 0, 16, 0, 3072, "zyx"),
    (0, 16, 16, 0, 3072, "zxy"),
    (1, 0, 16, 0, 1024, "zyx"),
    (1, 16, 16, 0, 1024, "zxy"),
    (2, 0, 32, 0, 1792, "zyx"),
    (2, 0, 32, 1792, 1792, "zxy"),
    (2, 0, 32, 3584, 512, "xyz"),
    (3, 0, 48, 0, 1024, "zyx"),
    (3, 48, 48, 0, 1024, "zxy"),
    (3, 96, 32, 0, 1024, "yxz"),
)
GROUPS = ((0, 1), (2, 3), (4, 5, 6), (7, 8, 9))


def hops(dim):
    return (1, 3, 2) if dim == "z" else (1,)


def moved(rel, dim, e):
    d, m, l = rel
    if dim == "z":
        return ((d + e) % NZ, m, l)
    return (d, 1 - m, l) if dim == "y" else (d, m, 1 - l)


def routes(stages):
    hold, arrivals, slot = [(0, 0, 0)], [], {}
    for s, dim in enumerate(stages):
        new = []
        for rel in hold:
            for e in hops(dim):
                slot[(rel, s, e)] = len(arrivals)
                arrivals.append((moved(rel, dim, e), s))
                new.append(arrivals[-1][0])
        hold = hold + new
    return arrivals, slot


class Gather:
    def __init__(self, ins, outs, sems, here):
        self.ins, self.outs, (self.ssem, self.rsem) = ins, outs, sems
        z, y, x, c = here
        self.core = c
        self.zfrom = [lax.rem(z + NZ - d, NZ) for d in range(NZ)]
        self.ys, self.xs = (y, 1 - y), (x, 1 - x)
        self.peer = {("z", e): device(lax.rem(z + e, NZ), y, x, c) for e in range(1, NZ)}
        self.peer["y", 1] = device(z, 1 - y, x, c)
        self.peer["x", 1] = device(z, y, 1 - x, c)
        self.other = device(z, y, x, 1 - c)
        self.plan = [routes(p[5]) for p in PARTS]
        self.sent = []

    def place(self, part, rel, core):
        w, r0, nr, c0, nc, stages = PARTS[part]
        o = owner(self.zfrom[rel[0]], self.ys[rel[1]], self.xs[rel[2]], core)
        n = SHARDS[w][0]
        return self.outs[w].at[pl.ds(pl.multiple_of(o * n + r0, 16), nr), pl.ds(c0, nc)]

    def send(self, part, rel, k, peer, own):
        w, r0, nr, c0, nc, stages = PARTS[part]
        dst = self.place(part, rel, self.core)
        src = self.ins[w].at[pl.ds(r0, nr), pl.ds(c0, nc)] if own else dst
        cp = remote(src, dst, self.ssem.at[part, k], self.rsem.at[part, k], peer)
        cp.start()
        self.sent.append(cp)

    def wait(self, part, rel, core, k):
        ref = self.place(part, rel, core)
        remote(ref, ref, self.ssem.at[part, k], self.rsem.at[part, k], self.other).wait_recv()

    def forward(self, part, rel, s, i):
        stages, slot = PARTS[part][5], self.plan[part][1]
        for t in range(s + 1, 3):
            for e in hops(stages[t]):
                self.send(part, rel, slot[rel, t, e], self.peer[stages[t], e], s < 0)
        self.send(part, rel, 15 + i, self.other, s < 0)

    def start(self, group):
        for part in group:
            self.forward(part, (0, 0, 0), -1, 0)

    def arrive(self, group, s):
        ks = [[k for k, a in enumerate(self.plan[p][0]) if a[1] == s] for p in group]
        steps = []
        for j in range(max(map(len, ks))):
            steps.append([(p, k[j]) for p, k in zip(group, ks) if j < len(k)])

        def one(step):
            for part, k in step:
                rel = self.plan[part][0][k][0]
                self.wait(part, rel, self.core, k)
                self.forward(part, rel, s, 1 + k)

        return [functools.partial(one, step) for step in steps]

    def halves(self, group):
        for part in group:
            for i, rel in enumerate([(0, 0, 0)] + [a[0] for a in self.plan[part][0]]):
                self.wait(part, rel, 1 - self.core, 15 + i)


def dot(a, b, ca, cb):
    return lax.dot_general(
        a, b, (((ca,), (cb,)), ((), ())), preferred_element_type=jnp.float32
    )


def scale_of(values):
    return lax.rsqrt(jnp.mean(values * values, axis=-1, keepdims=True) + epsilon)


def rows_loop(step):
    @pl.loop(0, 8)
    def _(i):
        step(pl.ds(pl.multiple_of(i * 64, 64), 64))


LOG2E = math.log2(math.e)
SCALE2 = LOG2E / math.sqrt(HD)


def write_bias(lengths, bias):
    ends, total = [], jnp.int32(0)
    for j in range(lengths.shape[1]):
        total = total + lengths[0, j]
        ends.append(total)
    key = lax.broadcasted_iota(jnp.int32, (1, 512), 1)
    seg_key = sum((key >= e).astype(jnp.int32) for e in ends)

    @pl.loop(0, 8)
    def _(i):
        query = lax.broadcasted_iota(jnp.int32, (64, 1), 0) + i * 64
        seg_query = sum((query >= e).astype(jnp.int32) for e in ends)
        ok = (seg_query == seg_key) & (query >= key)
        bias[pl.ds(pl.multiple_of(i * 64, 64), 64), :] = jnp.where(ok, 0.0, -1e30)


def attend_pair(pair, qkv, bias, context, lse):
    lane = lax.broadcasted_iota(jnp.int32, (1, 128), 1)
    low = lane < HD
    col = pl.multiple_of(pair * 128, 128)
    q = qkv[:, pl.ds(col, 128)]
    k = qkv[:, pl.ds(1024 + col, 128)]
    v = qkv[:, pl.ds(2048 + col, 128)]
    parts, sums = [], lse[...]
    for h in range(2):
        qh = jnp.where(low if h == 0 else ~low, q, jnp.zeros_like(q))
        logits = dot(qh, k, 1, 1) * SCALE2 + bias[...]
        peak = jnp.max(logits, axis=1, keepdims=True)
        raised = jnp.exp2(logits - peak)
        total = jnp.sum(raised, axis=1, keepdims=True)
        parts.append(dot(raised.astype(jnp.bfloat16), v, 1, 0) * (1.0 / total))
        sums = jnp.where(lane == pair * 2 + h, peak + jnp.log2(total), sums)
    context[:, pl.ds(col, 128)] = jnp.where(low, parts[0], parts[1]).astype(jnp.bfloat16)
    lse[...] = sums


GELU_A = math.sqrt(2.0 / math.pi)


def forward_kernel(*refs):
    ins, gain_in, lengths, tokens, cotangent = refs[:4], *refs[4:8]
    outs = refs[8:12]
    o_gain, o_qkv, o_context, o_lse, o_middle, o_second, o_hidden, o_grad = refs[12:20]
    w_qkv, w_out, w_up, normed, qkv, bias, context, lse, middle, second = refs[20:30]
    hid, act, grad, gains, gain_row = refs[30:35]
    lsem, wsem, hsem, gsem, ssem, rsem, gs, gr = refs[35:]
    here = coords()
    z, y, x, c = here
    peers = all_peers(*here)
    me = owner(*here)
    greet(peers)
    g = Gather(ins, outs, (ssem, rsem), here)
    g.start(GROUPS[0])
    gain_copies = []
    for j, peer in enumerate(peers):
        cp = remote(gain_in, gains.at[me], gs.at[j], gr.at[j], peer)
        cp.start()
        gain_copies.append(cp)
    for w in range(4):
        n = SHARDS[w][0]
        cp = pltpu.make_async_copy(
            ins[w], outs[w].at[pl.ds(pl.multiple_of(me * n, n), n)], lsem.at[w]
        )
        cp.start()
    own = [
        pltpu.make_async_copy(
            ins[w],
            outs[w].at[pl.ds(pl.multiple_of(me * SHARDS[w][0], SHARDS[w][0]), SHARDS[w][0])],
            lsem.at[w],
        )
        for w in range(4)
    ]
    gains[me] = gain_in[...]
    g.start(GROUPS[1])
    g.start(GROUPS[2])
    write_bias(lengths, bias)
    saves = []

    def save(src, dst, k):
        cp = pltpu.make_async_copy(src, dst, lsem.at[k])
        cp.start()
        saves.append(cp)

    def gain_rows():
        for cp in gain_copies:
            cp.wait()
        for b in range(8):
            total = gains[4 * b] + gains[4 * b + 1] + gains[4 * b + 2] + gains[4 * b + 3]
            gain_row[:, b * 128 : (b + 1) * 128] = total
        save(gain_row, o_gain, 4)

    def norm_one():
        def step(r):
            v = tokens[r, :].astype(jnp.float32)
            normed[r, :] = (v * scale_of(v) * gain_row[0:1, :]).astype(jnp.bfloat16)

        rows_loop(step)

    def load(w, dst, n):
        width = SHARDS[w][1] // n
        g.halves(GROUPS[w])
        own[w].wait()
        for i in range(n):
            s = pl.ds(i * width, width)
            pltpu.make_async_copy(outs[w].at[:, s], dst.at[:, s], wsem.at[w, i]).start()

    def loaded(w, dst, n, i):
        s = pl.ds(i * (SHARDS[w][1] // n), SHARDS[w][1] // n)
        pltpu.make_async_copy(outs[w].at[:, s], dst.at[:, s], wsem.at[w, i]).wait()

    def project(i):
        loaded(0, w_qkv, 6, i)
        s = slice(i * 512, (i + 1) * 512)
        qkv[:, s] = dot(normed[...], w_qkv[:, s], 1, 0).astype(jnp.bfloat16)

    def attend(i):
        @pl.loop(0, 2)
        def _(j):
            attend_pair(i * 2 + j, qkv, bias, context, lse)

    def attended():
        save(qkv, o_qkv, 5)
        save(context, o_context, 6)
        save(lse, o_lse, 7)

    def add_out(i):
        loaded(1, w_out, 2, i)
        s = slice(i * 512, (i + 1) * 512)
        middle[:, s] = tokens[:, s].astype(jnp.float32) + dot(context[...], w_out[:, s], 1, 0)

    def norm_two():
        save(middle, o_middle, 8)

        def step(r):
            v = middle[r, :]
            second[r, :] = (v * scale_of(v) * gain_row[1:2, :]).astype(jnp.bfloat16)

        rows_loop(step)
        save(second, o_second, 9)

    hid_copies, grad_copies = [], []

    def feed(i):
        loaded(2, w_up, 8, i)
        s = slice(i * 512, (i + 1) * 512)
        slot = i % 2
        if i >= 2:
            hid_copies[i - 2].wait()
        hid[slot] = dot(second[...], w_up[:, s], 1, 0)
        cp = pltpu.make_async_copy(hid.at[slot], o_hidden.at[:, s], hsem.at[slot])
        cp.start()
        hid_copies.append(cp)

        def step(r):
            v = hid[slot, r, :]
            t = jnp.tanh(GELU_A * (v + 0.044715 * v * v * v))
            act[r, :] = (0.5 * v * (1.0 + t)).astype(jnp.bfloat16)

        rows_loop(step)
        if i >= 2:
            grad_copies[i - 2].wait()
        grad[slot] = dot(act[...], cotangent[...], 0, 0).astype(jnp.bfloat16)
        cp = pltpu.make_async_copy(grad.at[slot], o_grad.at[s, :], gsem.at[slot])
        cp.start()
        grad_copies.append(cp)

    events = []
    for t in range(1, 7):
        if t == 1:
            events += [functools.partial(g.start, GROUPS[3])]
        for s in (0, 1, 2):
            if 0 <= t - s - 1 < 4:
                events += g.arrive(GROUPS[t - s - 1], s)
                if s == 2:
                    events.append("whole%d" % (t - s - 1))
    F = functools.partial
    work = {
        None: [gain_rows, norm_one],
        0: [F(project, i) for i in range(6)] + [F(attend, i) for i in range(4)] + [attended],
        1: [F(add_out, i) for i in range(2)] + [norm_two],
        2: [F(feed, i) for i in range(8)],
    }
    ready, since = list(work[None]), 0
    n_load = {0: (w_qkv, 6), 1: (w_out, 2), 2: (w_up, 8)}
    lse[...] = jnp.zeros_like(lse)
    for e in events:
        if isinstance(e, str):
            w = int(e[5:])
            if w in n_load:
                ready.append(F(load, w, *n_load[w]))
                ready += work[w]
            continue
        e()
        since += 1
        if ready and since >= EVERY:
            ready.pop(0)()
            since = 0
    for step in ready:
        step()
    g.halves(GROUPS[3])
    own[3].wait()
    for cp in hid_copies[-2:] + grad_copies[-2:] + saves:
        cp.wait()
    for cp in g.sent:
        cp.wait_send()


EVERY = 1


def forward(weights, gains, lengths, tokens, cotangent):
    hbm = pl.BlockSpec(memory_space=pl.ANY)
    vmem = pl.BlockSpec(memory_space=pltpu.VMEM)
    smem = pl.BlockSpec(memory_space=pltpu.SMEM)
    bf, f32 = jnp.bfloat16, jnp.float32
    saved = [
        ((8, 1024), f32),
        ((512, 3072), bf),
        ((512, 1024), bf),
        ((512, 128), f32),
        ((512, 1024), f32),
        ((512, 1024), bf),
        ((512, 4096), f32),
        ((4096, 1024), bf),
    ]
    scratch = [
        ((1024, 3072), bf),
        ((1024, 1024), bf),
        ((1024, 4096), bf),
        ((512, 1024), bf),
        ((512, 3072), bf),
        ((512, 512), f32),
        ((512, 1024), bf),
        ((512, 128), f32),
        ((512, 1024), f32),
        ((512, 1024), bf),
        ((2, 512, 512), f32),
        ((512, 512), bf),
        ((2, 512, 1024), bf),
        ((32, 8, 128), f32),
        ((8, 1024), f32),
    ]
    dma = pltpu.SemaphoreType.DMA
    out = pl.pallas_call(
        forward_kernel,
        out_shape=[jax.ShapeDtypeStruct((w.shape[0] * 32, w.shape[1]), w.dtype) for w in weights]
        + [jax.ShapeDtypeStruct(*s) for s in saved],
        in_specs=[hbm] * 4 + [vmem, smem, vmem, vmem],
        out_specs=[hbm] * 12,
        scratch_shapes=[pltpu.VMEM(*s) for s in scratch]
        + [
            dma((10,)),
            dma((3, 8)),
            dma((2,)),
            dma((2,)),
            dma((len(PARTS), 31)),
            dma((len(PARTS), 31)),
            dma((31,)),
            dma((31,)),
        ],
        compiler_params=pltpu.CompilerParams(
            collective_id=0, has_side_effects=True, vmem_limit_bytes=60 << 20
        ),
    )(*weights, gains, lengths, tokens, cotangent)
    return out[:4], out[4:]


UNITS = ((0, 0, 1024), (1, 0, 4096), (2, 0, 1024), (3, 0, 1024), (3, 1024, 1024), (3, 2048, 1024))


def scatter_kernel(dims, *refs):
    nu = len(UNITS)
    grads, gain_in = refs[:4], refs[4]
    outs, gain_out = refs[5:9], refs[9]
    refs = refs[10:]
    mine, got0, got1, got2, got3, res = (refs[i * nu : (i + 1) * nu] for i in range(6))
    got_gain, ssem, rsem, lsem, osem, gs, gr = refs[6 * nu :]
    z, y, x, c = coords()
    ypeer, xpeer, speer = device(z, 1 - y, x, c), device(z, y, 1 - x, c), device(z, y, x, 1 - c)
    zof = [lax.rem(z + d, NZ) for d in range(NZ)]
    zpeers = [device(zof[d], y, x, c) for d in range(NZ)]
    peers = all_peers(z, y, x, c)
    greet(peers)
    pend = []

    def send(u, k, src, dst, peer):
        cp = remote(src, dst, ssem.at[u, k], rsem.at[u, k], peer)
        cp.start()
        pend.append(cp)

    def wait(u, k, ref):
        remote(ref, ref, ssem.at[u, k], rsem.at[u, k], speer).wait_recv()

    def add(dst, src):
        dst[...] = (dst[...].astype(jnp.float32) + src[...].astype(jnp.float32)).astype(dst.dtype)

    def stage0(u):
        w, col, width = UNITS[u]
        src = grads[w].at[:, :, :, :, :, pl.ds(col, width)]
        send(u, 0, src.at[:, :, :, 1 - c], got0[u], speer)
        cp = pltpu.make_async_copy(src.at[:, :, :, c], mine[u], lsem.at[u])
        cp.start()

    def stage1(u):
        w, col, width = UNITS[u]
        src = grads[w].at[:, :, :, c, :, pl.ds(col, width)]
        h = mine[u].shape[3] // 2
        pltpu.make_async_copy(src, mine[u], lsem.at[u]).wait()
        wait(u, 0, got0[u])
        lo, hi = pl.ds(0, h), pl.ds(h, h)
        for far in (True, False):
            xx, yy = (1 - x, 1 - y) if far else (x, y)

            @pl.loop(0, NZ)
            def _(k):
                for j in range(2):
                    add(mine[u].at[k, j, xx, lo], got0[u].at[k, j, xx, lo])
                    add(mine[u].at[k, yy, j, hi], got0[u].at[k, yy, j, hi])

            if far:
                send(u, 1, mine[u].at[:, :, xx, lo], got1[u].at[0], xpeer)
                send(u, 2, mine[u].at[:, yy, :, hi], got1[u].at[1], ypeer)

    def stage2(u):
        h = mine[u].shape[3] // 2
        lo, hi = pl.ds(0, h), pl.ds(h, h)
        wait(u, 1, got1[u].at[0])
        wait(u, 2, got1[u].at[1])
        for far in (True, False):
            xx, yy = (1 - x, 1 - y) if far else (x, y)

            @pl.loop(0, NZ)
            def _(k):
                add(mine[u].at[k, yy, x, lo], got1[u].at[0, k, yy])
                add(mine[u].at[k, y, xx, hi], got1[u].at[1, k, xx])

            if far:
                send(u, 3, mine[u].at[:, yy, x, lo], got2[u].at[0], ypeer)
                send(u, 4, mine[u].at[:, y, xx, hi], got2[u].at[1], xpeer)

    def stage3(u):
        h = mine[u].shape[3] // 2
        lo, hi = pl.ds(0, h), pl.ds(h, h)
        wait(u, 3, got2[u].at[0])
        wait(u, 4, got2[u].at[1])

        @pl.loop(0, NZ)
        def _(k):
            add(mine[u].at[k, y, x, lo], got2[u].at[0, k])
            add(mine[u].at[k, y, x, hi], got2[u].at[1, k])

        for d in range(1, NZ):
            send(u, 4 + d, mine[u].at[zof[d], y, x], got3[u].at[d - 1], zpeers[d])

    def stage4(u):
        w, col, width = UNITS[u]
        for d in range(1, NZ):
            wait(u, 4 + d, got3[u].at[d - 1])
        total = mine[u][z, y, x].astype(jnp.float32)
        for d in range(1, NZ):
            total = total + got3[u][d - 1].astype(jnp.float32)
        res[u][...] = total
        cp = pltpu.make_async_copy(res[u], outs[w].at[:, pl.ds(col, width)], osem.at[u])
        cp.start()
        finals.append(cp)

    finals = []
    gain_copies = []
    for j, (peer, o) in enumerate(zip(peers, peers)):
        block = (o[0] * 4 + o[1]) // 4
        cp = remote(gain_in.at[block], got_gain.at[j + 1], gs.at[j], gr.at[j], peer)
        cp.start()
        gain_copies.append(cp)
    for t in range(nu + 4):
        for step, lag in ((stage4, 4), (stage3, 3), (stage2, 2), (stage1, 1), (stage0, 0)):
            if 0 <= t - lag < nu:
                step(t - lag)
    for cp in gain_copies:
        cp.wait()
    got_gain[0] = gain_in[owner(z, y, x, c) // 4]
    total = got_gain[0]
    for j in range(1, 32):
        total = total + got_gain[j]
    gain_out[...] = total
    for cp in pend:
        cp.wait_send()
    for cp in finals:
        cp.wait()


def scatter(grads, gains):
    hbm = pl.BlockSpec(memory_space=pl.ANY)
    vmem = pl.BlockSpec(memory_space=pltpu.VMEM)
    dims = [(g.shape[4], g.shape[5]) for g in grads]
    scratch = []
    per = [(dims[w][0], width) for w, col, width in UNITS]
    for r, n in per:
        scratch.append(pltpu.VMEM((4, 2, 2, r, n), jnp.bfloat16))
    for r, n in per:
        scratch.append(pltpu.VMEM((4, 2, 2, r, n), jnp.bfloat16))
    for r, n in per:
        scratch.append(pltpu.VMEM((2, 4, 2, r // 2, n), jnp.bfloat16))
    for r, n in per:
        scratch.append(pltpu.VMEM((2, 4, r // 2, n), jnp.bfloat16))
    for r, n in per:
        scratch.append(pltpu.VMEM((3, r, n), jnp.bfloat16))
    for r, n in per:
        scratch.append(pltpu.VMEM((r, n), jnp.float32))
    nu = len(UNITS)
    scratch += [
        pltpu.VMEM((32, 8, 128), jnp.float32),
        pltpu.SemaphoreType.DMA((nu, 8)),
        pltpu.SemaphoreType.DMA((nu, 8)),
        pltpu.SemaphoreType.DMA((nu,)),
        pltpu.SemaphoreType.DMA((nu,)),
        pltpu.SemaphoreType.DMA((31,)),
        pltpu.SemaphoreType.DMA((31,)),
    ]
    return pl.pallas_call(
        functools.partial(scatter_kernel, dims),
        out_shape=[jax.ShapeDtypeStruct(d, jnp.float32) for d in dims]
        + [jax.ShapeDtypeStruct((8, 128), jnp.float32)],
        in_specs=[hbm] * 4 + [vmem],
        out_specs=[hbm] * 4 + [vmem],
        scratch_shapes=scratch,
        compiler_params=pltpu.CompilerParams(
            collective_id=1, has_side_effects=True, vmem_limit_bytes=60 << 20
        ),
    )(*grads, gains)


def project_input(inputs, w_qkv, gain):
    normed, scale_one = normalize(inputs, gain)
    normed_low = normed.astype(jnp.bfloat16)
    mixed = jnp.dot(normed_low, w_qkv, preferred_element_type=jnp.float32).astype(jnp.bfloat16)
    split = mixed.reshape(inputs.shape[0], 3, H, HD)
    return (normed_low, scale_one, split[:, 0], split[:, 1], split[:, 2])


def feed_inputs(inputs, context, w_out, w_up, gain):
    middle = inputs + jnp.dot(context, w_out, preferred_element_type=jnp.float32)
    second, scale_two = normalize(middle, gain)
    second_low = second.astype(jnp.bfloat16)
    hidden = jnp.dot(second_low, w_up, preferred_element_type=jnp.float32)
    active = jax.nn.gelu(hidden, approximate=True).astype(jnp.bfloat16)
    return (middle, scale_two, second_low, hidden, active)


def layer(tokens, lengths, w_qkv, w_out, w_up, w_down, gain_attn, gain_mlp, cotangent, low_type):
    total_rows = tokens.shape[0]
    ends = jnp.cumsum(lengths[0])
    places = jnp.arange(total_rows, dtype=jnp.int32)
    segment = jnp.sum((places[:, None] >= ends[None, :]).astype(jnp.int32), axis=1)
    inputs = tokens.astype(jnp.float32)
    gain_attn, gain_mlp = gain_attn.astype(jnp.float32), gain_mlp.astype(jnp.float32)
    normed_low, scale_one, queries, keys_all, values_all = project_input(inputs, w_qkv, gain_attn)
    context_full, log_sums = attend_forward(queries, keys_all, values_all, segment)
    context = context_full.reshape(total_rows, H * HD).astype(jnp.bfloat16)
    middle, scale_two, second_low, hidden, active = feed_inputs(
        inputs, context, w_out, w_up, gain_mlp
    )
    output = (middle + jnp.dot(active, w_down, preferred_element_type=jnp.float32)).astype(
        jnp.bfloat16
    )
    grad_down = jnp.einsum("rf,rd->fd", active, cotangent, preferred_element_type=low_type)
    grad_active = jnp.einsum("rd,fd->rf", cotangent, w_down, preferred_element_type=jnp.float32)
    unused, gelu_pull = jax.vjp(lambda values: jax.nn.gelu(values, approximate=True), hidden)
    grad_hidden = gelu_pull(grad_active)[0].astype(jnp.bfloat16)
    grad_up = jnp.einsum("rd,rf->df", second_low, grad_hidden, preferred_element_type=low_type)
    grad_second = jnp.einsum("rf,df->rd", grad_hidden, w_up, preferred_element_type=jnp.float32)
    grad_mid_norm, grad_gain_m = norm_back(grad_second, middle, scale_two, gain_mlp)
    grad_middle = cotangent.astype(jnp.float32) + grad_mid_norm
    grad_mid_low = grad_middle.astype(jnp.bfloat16)
    grad_out = jnp.einsum("rc,rd->cd", context, grad_mid_low, preferred_element_type=low_type)
    grad_context = jnp.einsum("rd,cd->rc", grad_mid_low, w_out, preferred_element_type=jnp.float32)
    grad_context = grad_context.astype(jnp.bfloat16).reshape(total_rows, H, HD)
    grad_queries, grad_keys, grad_values = attend_backward(
        queries, keys_all, values_all, segment, log_sums, grad_context
    )
    grad_mixed = (
        jnp.stack([grad_queries, grad_keys, grad_values], axis=1)
        .reshape(total_rows, 3 * H * HD)
        .astype(jnp.bfloat16)
    )
    grad_qkv = jnp.einsum("rd,re->de", normed_low, grad_mixed, preferred_element_type=low_type)
    grad_normed = jnp.einsum("re,de->rd", grad_mixed, w_qkv, preferred_element_type=jnp.float32)
    grad_in_norm, grad_gain_a = norm_back(grad_normed, inputs, scale_one, gain_attn)
    grad_tokens = (grad_middle + grad_in_norm).astype(jnp.bfloat16)
    return (output, grad_tokens, grad_qkv, grad_out, grad_up, grad_down, grad_gain_a, grad_gain_m)


def shards_any(tokens, lengths, w_qkv, w_out, w_up, w_down, gain_attn, gain_mlp, cotangent):
    whole = gather_any(w_qkv, w_out, w_up, w_down, gain_attn, gain_mlp)
    out = layer(tokens, lengths, *whole, cotangent, jnp.float32)
    return out[:2] + sum_any(*out[2:])


def shards(tokens, lengths, w_qkv, w_out, w_up, w_down, gain_attn, gain_mlp, cotangent):
    me = lax.axis_index("dp") * 4 + lax.axis_index("fsdp")
    lanes = lax.rem(me, 4) * 32
    pair = jnp.stack([gain_attn, gain_mlp]).astype(jnp.float32)
    spot = lax.dynamic_update_slice(jnp.zeros((8, 128), jnp.float32), pair, (0, lanes))
    whole, saved = forward((w_qkv, w_out, w_up, w_down), spot, lengths, tokens, cotangent)
    w_qkv, w_out, w_up, w_down = whole
    gains, mixed, context, lse, middle, second_low, hidden, grad_down = saved
    gain_attn, gain_mlp = gains[0], gains[1]
    total_rows = tokens.shape[0]
    ends = jnp.cumsum(lengths[0])
    places = jnp.arange(total_rows, dtype=jnp.int32)
    segment = jnp.sum((places[:, None] >= ends[None, :]).astype(jnp.int32), axis=1)
    inputs = tokens.astype(jnp.float32)
    normed, scale_one = normalize(inputs, gain_attn)
    normed_low = normed.astype(jnp.bfloat16)
    split = mixed.reshape(total_rows, 3, H, HD)
    queries, keys_all, values_all = split[:, 0], split[:, 1], split[:, 2]
    log_sums = lse[:, :H].T / LOG2E
    unused, scale_two = normalize(middle, gain_mlp)
    low_type = jnp.bfloat16
    active, gelu_pull = jax.vjp(lambda values: jax.nn.gelu(values, approximate=True), hidden)
    output = (
        middle + jnp.dot(active.astype(low_type), w_down, preferred_element_type=jnp.float32)
    ).astype(jnp.bfloat16)
    grad_active = jnp.einsum("rd,fd->rf", cotangent, w_down, preferred_element_type=jnp.float32)
    grad_hidden = gelu_pull(grad_active)[0].astype(jnp.bfloat16)
    grad_up = jnp.einsum("rd,rf->df", second_low, grad_hidden, preferred_element_type=low_type)
    grad_second = jnp.einsum("rf,df->rd", grad_hidden, w_up, preferred_element_type=jnp.float32)
    grad_mid_norm, grad_gain_m = norm_back(grad_second, middle, scale_two, gain_mlp)
    grad_middle = cotangent.astype(jnp.float32) + grad_mid_norm
    grad_mid_low = grad_middle.astype(jnp.bfloat16)
    grad_out = jnp.einsum("rc,rd->cd", context, grad_mid_low, preferred_element_type=low_type)
    grad_context = jnp.einsum("rd,cd->rc", grad_mid_low, w_out, preferred_element_type=jnp.float32)
    grad_context = grad_context.astype(jnp.bfloat16).reshape(total_rows, H, HD)
    grad_queries, grad_keys, grad_values = attend_backward(
        queries, keys_all, values_all, segment, log_sums, grad_context
    )
    grad_mixed = (
        jnp.stack([grad_queries, grad_keys, grad_values], axis=1)
        .reshape(total_rows, 3 * H * HD)
        .astype(jnp.bfloat16)
    )
    grad_qkv = jnp.einsum("rd,re->de", normed_low, grad_mixed, preferred_element_type=low_type)
    grad_normed = jnp.einsum("re,de->rd", grad_mixed, w_qkv, preferred_element_type=jnp.float32)
    grad_in_norm, grad_gain_a = norm_back(grad_normed, inputs, scale_one, gain_attn)
    grad_tokens = (grad_middle + grad_in_norm).astype(jnp.bfloat16)
    grad_gain = jnp.stack([grad_gain_a.reshape(8, 128), grad_gain_m.reshape(8, 128)], axis=1)
    grad_gain = jnp.pad(grad_gain, ((0, 0), (0, 6), (0, 0)))
    split = lambda g: g.reshape(4, 2, 2, 2, g.shape[0] // 32, g.shape[1])
    g_down, g_up, g_out, g_qkv, g_gain = scatter(
        (split(grad_down), split(grad_up), split(grad_out), split(grad_qkv)), grad_gain
    )
    own = lax.dynamic_slice(g_gain, (0, lanes), (2, 32))
    return (output, grad_tokens, g_qkv, g_out, g_up, g_down, own[0], own[1])


def solution(mesh):
    rows, flat = P(AXES, None), P(AXES)
    known = dict(mesh.shape) == {"dp": 8, "fsdp": 4}
    return jax.shard_map(
        shards if known else shards_any,
        mesh=mesh,
        in_specs=(rows, rows, rows, rows, rows, rows, flat, flat, rows),
        out_specs=(rows, rows, rows, rows, rows, rows, flat, flat),
        check_vma=False,
    )
```

```python
import functools
import math

import jax
import jax.numpy as jnp
from jax import lax
from jax.experimental import pallas as pl
from jax.experimental.pallas import tpu as pltpu
from jax.sharding import PartitionSpec as P

H = 16
HD = 64
MESH = pl.DeviceIdType.MESH
AXES = ("dp", "fsdp")


epsilon = 1e-05


def normalize(values, gain):
    scale_row = lax.rsqrt(jnp.mean(values * values, axis=-1, keepdims=True) + epsilon)
    return (values * scale_row * gain, scale_row)


def norm_back(grad_normed, values, scale_row, gain):
    scaled = grad_normed * gain
    grad_gain = jnp.sum(grad_normed * values * scale_row, axis=0)
    cubed = scale_row * scale_row * scale_row
    grad_values = scale_row * scaled - values * cubed * jnp.mean(
        scaled * values, axis=-1, keepdims=True
    )
    return (grad_values, grad_gain)


def block_logits(query_block, key_rows, segment):
    block_rows = query_block.shape[0]
    key_limit = key_rows.shape[0]
    raw = jnp.einsum("qhd,khd->hqk", query_block, key_rows, preferred_element_type=jnp.float32)
    query_place = jnp.arange(block_rows, dtype=jnp.int32)
    key_place = jnp.arange(key_limit, dtype=jnp.int32)
    allowed = (segment[:, None] == segment[None, :]) & (query_place[:, None] >= key_place[None, :])
    return jnp.where(allowed[None], raw * (1.0 / math.sqrt(HD)), -1e30)


def attend_forward(queries, keys_all, values_all, segment):
    logits = block_logits(queries, keys_all, segment)
    peak = jnp.max(logits, axis=-1, keepdims=True)
    raised = jnp.exp(logits - peak)
    totals = jnp.sum(raised, axis=-1, keepdims=True)
    attn_prob = (raised / totals).astype(jnp.bfloat16)
    contexts = jnp.einsum("hqk,khd->qhd", attn_prob, values_all, preferred_element_type=jnp.float32)
    log_sums = (peak + jnp.log(totals))[:, :, 0]
    return (contexts, log_sums)


def attend_backward(queries, keys_all, values_all, segment, log_sums, grad_context):
    logits = block_logits(queries, keys_all, segment)
    attn_prob = jnp.exp(logits - log_sums[:, :, None])
    rounded = attn_prob.astype(jnp.bfloat16)
    grad_prob = jnp.einsum(
        "qhd,khd->hqk", grad_context, values_all, preferred_element_type=jnp.float32
    )
    inner = jnp.sum(attn_prob * grad_prob, axis=-1, keepdims=True)
    grad_logit = (1.0 / math.sqrt(HD) * attn_prob * (grad_prob - inner)).astype(jnp.bfloat16)
    grad_queries = jnp.einsum(
        "hqk,khd->qhd", grad_logit, keys_all, preferred_element_type=jnp.float32
    )
    grad_keys = jnp.einsum("hqk,qhd->khd", grad_logit, queries, preferred_element_type=jnp.float32)
    grad_values = jnp.einsum(
        "hqk,qhd->khd", rounded, grad_context, preferred_element_type=jnp.float32
    )
    return (grad_queries, grad_keys, grad_values)


def gather_any(*weights):
    return tuple(lax.all_gather(w, AXES, axis=0, tiled=True) for w in weights)


def sum_any(*grads):
    return tuple(lax.psum_scatter(g, AXES, scatter_dimension=0, tiled=True) for g in grads)


NZ = 4


def coords():
    a, b = lax.axis_index("dp"), lax.axis_index("fsdp")
    return a // 2, a % 2, b // 2, b % 2


def device(z, y, x, c):
    return (z * 2 + y, x * 2 + c)


def owner(z, y, x, c):
    return ((z * 2 + y) * 2 + x) * 2 + c


def all_peers(z, y, x, c):
    peers = []
    for d in range(NZ):
        for m in range(2):
            for l in range(2):
                for s in range(2):
                    if d + m + l + s:
                        peers.append(
                            device(
                                lax.rem(z + d, NZ),
                                1 - y if m else y,
                                1 - x if l else x,
                                1 - c if s else c,
                            )
                        )
    return peers


def greet(peers):
    sem = pltpu.get_barrier_semaphore()
    for peer in peers:
        pl.semaphore_signal(sem, inc=1, device_id=peer, device_id_type=MESH)
    pl.semaphore_wait(sem, len(peers))


def remote(src, dst, send_sem, recv_sem, peer):
    return pltpu.make_async_remote_copy(
        src_ref=src, dst_ref=dst, send_sem=send_sem, recv_sem=recv_sem,
        device_id=peer, device_id_type=MESH,
    )


FORWARD = 512
SHARDS = ((32, 3072), (32, 1024), (32, 4096), (128, 1024))
PARTS = (
    (0, 0, 16, 0, 3072, "zyx"),
    (0, 16, 16, 0, 3072, "zxy"),
    (1, 0, 16, 0, 1024, "zyx"),
    (1, 16, 16, 0, 1024, "zxy"),
    (2, 0, 32, 0, 1792, "zyx"),
    (2, 0, 32, 1792, 1792, "zxy"),
    (2, 0, 32, 3584, 512, "xyz"),
    (3, 0, 48, 0, 1024, "zyx"),
    (3, 48, 48, 0, 1024, "zxy"),
    (3, 96, 32, 0, 1024, "yxz"),
)
GROUPS = ((0, 1), (2, 3), (4, 5, 6), (7, 8, 9))


def hops(dim):
    return (1, 3, 2) if dim == "z" else (1,)


def moved(rel, dim, e):
    d, m, l = rel
    if dim == "z":
        return ((d + e) % NZ, m, l)
    return (d, 1 - m, l) if dim == "y" else (d, m, 1 - l)


def routes(stages):
    hold, arrivals, slot = [(0, 0, 0)], [], {}
    for s, dim in enumerate(stages):
        new = []
        for rel in hold:
            for e in hops(dim):
                slot[(rel, s, e)] = len(arrivals)
                arrivals.append((moved(rel, dim, e), s))
                new.append(arrivals[-1][0])
        hold = hold + new
    return arrivals, slot


class Gather:
    def __init__(self, ins, outs, sems, here):
        self.ins, self.outs, (self.ssem, self.rsem) = ins, outs, sems
        z, y, x, c = here
        self.core = c
        self.zfrom = [lax.rem(z + NZ - d, NZ) for d in range(NZ)]
        self.ys, self.xs = (y, 1 - y), (x, 1 - x)
        self.peer = {("z", e): device(lax.rem(z + e, NZ), y, x, c) for e in range(1, NZ)}
        self.peer["y", 1] = device(z, 1 - y, x, c)
        self.peer["x", 1] = device(z, y, 1 - x, c)
        self.other = device(z, y, x, 1 - c)
        self.plan = [routes(p[5]) for p in PARTS]
        self.sent = []

    def place(self, part, rel, core):
        w, r0, nr, c0, nc, stages = PARTS[part]
        o = owner(self.zfrom[rel[0]], self.ys[rel[1]], self.xs[rel[2]], core)
        n = SHARDS[w][0]
        return self.outs[w].at[pl.ds(pl.multiple_of(o * n + r0, 16), nr), pl.ds(c0, nc)]

    def send(self, part, rel, k, peer, own):
        w, r0, nr, c0, nc, stages = PARTS[part]
        dst = self.place(part, rel, self.core)
        src = self.ins[w].at[pl.ds(r0, nr), pl.ds(c0, nc)] if own else dst
        cp = remote(src, dst, self.ssem.at[part, k], self.rsem.at[part, k], peer)
        cp.start()
        self.sent.append(cp)

    def wait(self, part, rel, core, k):
        ref = self.place(part, rel, core)
        remote(ref, ref, self.ssem.at[part, k], self.rsem.at[part, k], self.other).wait_recv()

    def forward(self, part, rel, s, i):
        stages, slot = PARTS[part][5], self.plan[part][1]
        for t in range(s + 1, 3):
            for e in hops(stages[t]):
                self.send(part, rel, slot[rel, t, e], self.peer[stages[t], e], s < 0)
        self.send(part, rel, 15 + i, self.other, s < 0)

    def start(self, group):
        for part in group:
            self.forward(part, (0, 0, 0), -1, 0)

    def arrive(self, group, s):
        ks = [[k for k, a in enumerate(self.plan[p][0]) if a[1] == s] for p in group]
        steps = []
        for j in range(max(map(len, ks))):
            steps.append([(p, k[j]) for p, k in zip(group, ks) if j < len(k)])

        def one(step):
            for part, k in step:
                rel = self.plan[part][0][k][0]
                self.wait(part, rel, self.core, k)
                self.forward(part, rel, s, 1 + k)

        return [functools.partial(one, step) for step in steps]

    def halves(self, group):
        for part in group:
            for i, rel in enumerate([(0, 0, 0)] + [a[0] for a in self.plan[part][0]]):
                self.wait(part, rel, 1 - self.core, 15 + i)


def dot(a, b, ca, cb):
    return lax.dot_general(
        a, b, (((ca,), (cb,)), ((), ())), preferred_element_type=jnp.float32
    )


def scale_of(values):
    return lax.rsqrt(jnp.mean(values * values, axis=-1, keepdims=True) + epsilon)


def rows_loop(step):
    @pl.loop(0, 8)
    def _(i):
        step(pl.ds(pl.multiple_of(i * 64, 64), 64))


LOG2E = math.log2(math.e)
SCALE2 = LOG2E / math.sqrt(HD)


def write_bias(lengths, bias):
    ends, total = [], jnp.int32(0)
    for j in range(lengths.shape[1]):
        total = total + lengths[0, j]
        ends.append(total)
    key = lax.broadcasted_iota(jnp.int32, (1, 512), 1)
    seg_key = sum((key >= e).astype(jnp.int32) for e in ends)

    @pl.loop(0, 8)
    def _(i):
        query = lax.broadcasted_iota(jnp.int32, (64, 1), 0) + i * 64
        seg_query = sum((query >= e).astype(jnp.int32) for e in ends)
        ok = (seg_query == seg_key) & (query >= key)
        bias[pl.ds(pl.multiple_of(i * 64, 64), 64), :] = jnp.where(ok, 0.0, -1e30)


def attend_pair(pair, qkv, bias, context, lse):
    lane = lax.broadcasted_iota(jnp.int32, (1, 128), 1)
    low = lane < HD
    col = pl.multiple_of(pair * 128, 128)
    q = qkv[:, pl.ds(col, 128)]
    k = qkv[:, pl.ds(1024 + col, 128)]
    v = qkv[:, pl.ds(2048 + col, 128)]
    parts, sums = [], lse[...]
    for h in range(2):
        qh = jnp.where(low if h == 0 else ~low, q, jnp.zeros_like(q))
        logits = dot(qh, k, 1, 1) * SCALE2 + bias[...]
        peak = jnp.max(logits, axis=1, keepdims=True)
        raised = jnp.exp2(logits - peak)
        total = jnp.sum(raised, axis=1, keepdims=True)
        parts.append(dot(raised.astype(jnp.bfloat16), v, 1, 0) * (1.0 / total))
        sums = jnp.where(lane == pair * 2 + h, peak + jnp.log2(total), sums)
    context[:, pl.ds(col, 128)] = jnp.where(low, parts[0], parts[1]).astype(jnp.bfloat16)
    lse[...] = sums


GELU_A = math.sqrt(2.0 / math.pi)


def forward_kernel(*refs):
    ins, gain_in, lengths, tokens, cotangent = refs[:4], *refs[4:8]
    outs = refs[8:12]
    o_gain, o_qkv, o_context, o_lse, o_middle, o_second, o_hidden, o_grad = refs[12:20]
    w_qkv, w_out, w_up, normed, qkv, bias, context, lse, middle, second = refs[20:30]
    hid, act, grad, gains, gain_row = refs[30:35]
    lsem, wsem, hsem, gsem, ssem, rsem, gs, gr = refs[35:]
    here = coords()
    z, y, x, c = here
    peers = all_peers(*here)
    me = owner(*here)
    greet(peers)
    g = Gather(ins, outs, (ssem, rsem), here)
    g.start(GROUPS[0])
    gain_copies = []
    for j, peer in enumerate(peers):
        cp = remote(gain_in, gains.at[me], gs.at[j], gr.at[j], peer)
        cp.start()
        gain_copies.append(cp)
    for w in range(4):
        n = SHARDS[w][0]
        cp = pltpu.make_async_copy(
            ins[w], outs[w].at[pl.ds(pl.multiple_of(me * n, n), n)], lsem.at[w]
        )
        cp.start()
    own = [
        pltpu.make_async_copy(
            ins[w],
            outs[w].at[pl.ds(pl.multiple_of(me * SHARDS[w][0], SHARDS[w][0]), SHARDS[w][0])],
            lsem.at[w],
        )
        for w in range(4)
    ]
    gains[me] = gain_in[...]
    g.start(GROUPS[1])
    g.start(GROUPS[2])
    write_bias(lengths, bias)
    saves = []

    def save(src, dst, k):
        cp = pltpu.make_async_copy(src, dst, lsem.at[k])
        cp.start()
        saves.append(cp)

    def gain_rows():
        for cp in gain_copies:
            cp.wait()
        for b in range(8):
            total = gains[4 * b] + gains[4 * b + 1] + gains[4 * b + 2] + gains[4 * b + 3]
            gain_row[:, b * 128 : (b + 1) * 128] = total
        save(gain_row, o_gain, 4)

    def norm_one():
        def step(r):
            v = tokens[r, :].astype(jnp.float32)
            normed[r, :] = (v * scale_of(v) * gain_row[0:1, :]).astype(jnp.bfloat16)

        rows_loop(step)

    def load(w, dst, n):
        width = SHARDS[w][1] // n
        g.halves(GROUPS[w])
        own[w].wait()
        for i in range(n):
            s = pl.ds(i * width, width)
            pltpu.make_async_copy(outs[w].at[:, s], dst.at[:, s], wsem.at[w, i]).start()

    def loaded(w, dst, n, i):
        s = pl.ds(i * (SHARDS[w][1] // n), SHARDS[w][1] // n)
        pltpu.make_async_copy(outs[w].at[:, s], dst.at[:, s], wsem.at[w, i]).wait()

    def project(i):
        loaded(0, w_qkv, 6, i)
        s = slice(i * 512, (i + 1) * 512)
        qkv[:, s] = dot(normed[...], w_qkv[:, s], 1, 0).astype(jnp.bfloat16)

    def attend(i):
        @pl.loop(0, 2)
        def _(j):
            attend_pair(i * 2 + j, qkv, bias, context, lse)

    def attended():
        save(qkv, o_qkv, 5)
        save(context, o_context, 6)
        save(lse, o_lse, 7)

    def add_out(i):
        loaded(1, w_out, 2, i)
        s = slice(i * 512, (i + 1) * 512)
        middle[:, s] = tokens[:, s].astype(jnp.float32) + dot(context[...], w_out[:, s], 1, 0)

    def norm_two():
        save(middle, o_middle, 8)

        def step(r):
            v = middle[r, :]
            second[r, :] = (v * scale_of(v) * gain_row[1:2, :]).astype(jnp.bfloat16)

        rows_loop(step)
        save(second, o_second, 9)

    hid_copies, grad_copies = [], []

    def feed(i):
        loaded(2, w_up, 8, i)
        s = slice(i * 512, (i + 1) * 512)
        slot = i % 2
        if i >= 2:
            hid_copies[i - 2].wait()
        hid[slot] = dot(second[...], w_up[:, s], 1, 0)
        cp = pltpu.make_async_copy(hid.at[slot], o_hidden.at[:, s], hsem.at[slot])
        cp.start()
        hid_copies.append(cp)

        def step(r):
            v = hid[slot, r, :]
            t = jnp.tanh(GELU_A * (v + 0.044715 * v * v * v))
            act[r, :] = (0.5 * v * (1.0 + t)).astype(jnp.bfloat16)

        rows_loop(step)
        if i >= 2:
            grad_copies[i - 2].wait()
        grad[slot] = dot(act[...], cotangent[...], 0, 0).astype(jnp.bfloat16)
        cp = pltpu.make_async_copy(grad.at[slot], o_grad.at[s, :], gsem.at[slot])
        cp.start()
        grad_copies.append(cp)

    events = []
    for t in range(1, 7):
        if t == 1:
            events += [functools.partial(g.start, GROUPS[3])]
        for s in (0, 1, 2):
            if 0 <= t - s - 1 < 4:
                events += g.arrive(GROUPS[t - s - 1], s)
                if s == 2:
                    events.append("whole%d" % (t - s - 1))
    F = functools.partial
    work = {
        None: [gain_rows, norm_one],
        0: [F(project, i) for i in range(6)] + [F(attend, i) for i in range(4)] + [attended],
        1: [F(add_out, i) for i in range(2)] + [norm_two],
        2: [F(feed, i) for i in range(8)],
    }
    ready, since = list(work[None]), 0
    n_load = {0: (w_qkv, 6), 1: (w_out, 2), 2: (w_up, 8)}
    lse[...] = jnp.zeros_like(lse)
    for e in events:
        if isinstance(e, str):
            w = int(e[5:])
            if w in n_load:
                ready.append(F(load, w, *n_load[w]))
                ready += work[w]
            continue
        e()
        since += 1
        if ready and since >= EVERY:
            ready.pop(0)()
            since = 0
    for step in ready:
        step()
    g.halves(GROUPS[3])
    own[3].wait()
    for cp in hid_copies[-2:] + grad_copies[-2:] + saves:
        cp.wait()
    for cp in g.sent:
        cp.wait_send()


EVERY = 1


def forward(weights, gains, lengths, tokens, cotangent):
    hbm = pl.BlockSpec(memory_space=pl.ANY)
    vmem = pl.BlockSpec(memory_space=pltpu.VMEM)
    smem = pl.BlockSpec(memory_space=pltpu.SMEM)
    bf, f32 = jnp.bfloat16, jnp.float32
    saved = [
        ((8, 1024), f32),
        ((512, 3072), bf),
        ((512, 1024), bf),
        ((512, 128), f32),
        ((512, 1024), f32),
        ((512, 1024), bf),
        ((512, 4096), f32),
        ((4096, 1024), bf),
    ]
    scratch = [
        ((1024, 3072), bf),
        ((1024, 1024), bf),
        ((1024, 4096), bf),
        ((512, 1024), bf),
        ((512, 3072), bf),
        ((512, 512), f32),
        ((512, 1024), bf),
        ((512, 128), f32),
        ((512, 1024), f32),
        ((512, 1024), bf),
        ((2, 512, 512), f32),
        ((512, 512), bf),
        ((2, 512, 1024), bf),
        ((32, 8, 128), f32),
        ((8, 1024), f32),
    ]
    dma = pltpu.SemaphoreType.DMA
    out = pl.pallas_call(
        forward_kernel,
        out_shape=[jax.ShapeDtypeStruct((w.shape[0] * 32, w.shape[1]), w.dtype) for w in weights]
        + [jax.ShapeDtypeStruct(*s) for s in saved],
        in_specs=[hbm] * 4 + [vmem, smem, vmem, vmem],
        out_specs=[hbm] * 12,
        scratch_shapes=[pltpu.VMEM(*s) for s in scratch]
        + [
            dma((10,)),
            dma((3, 8)),
            dma((2,)),
            dma((2,)),
            dma((len(PARTS), 31)),
            dma((len(PARTS), 31)),
            dma((31,)),
            dma((31,)),
        ],
        compiler_params=pltpu.CompilerParams(
            collective_id=0, has_side_effects=True, vmem_limit_bytes=60 << 20
        ),
    )(*weights, gains, lengths, tokens, cotangent)
    return out[:4], out[4:]


UNITS = ("d0", "d1", "u0", "u1", "o", "q", "k", "v")
SHAPE = {"d0": (32, 1024), "d1": (32, 1024), "u0": (16, 2048), "u1": (16, 2048)}
NEAR = (
    "c0", "d0.1", "c1", "d1.1", "c2", "c3", "u0.0", "d0.2", "c4", "u0.1", "c5", "d1.2", "c6", "c7",
    "u1.0", "d0.3", "nb", "u1.1",
)
LATE = (
    "go0", "go1", "o.0", "dc0", "dc1", "o.1", "a0", "a1", "u0.2", "a2", "d0.4", "a3", "d1.3", "a4",
    "a5", "d1.4", "a6", "a7", "free", "gq0", "gq1", "q.0", "gk0", "gk1", "k.0", "gv0", "gv1", "v.0",
    "q.1", "u1.2", "k.1", "v.1", "u0.3", "dn0", "dn1", "dn2", "o.2", "u0.4", "dn3", "dn4", "dn5",
    "u1.3", "nf", "gs", "q.2", "o.3", "u1.4", "k.2", "q.3", "v.2", "o.4", "k.3", "q.4", "v.3",
    "k.4", "v.4",
)


def unit_shape(u):
    return SHAPE.get(u, (16, 1024))


def backward_kernel(*refs):
    f_qkv, f_out, f_up, f_down, h_qkv, h_context, h_lse, h_middle, h_second, h_hidden, h_grad = refs[:11]
    h_gain, h_tokens, h_cot, lengths = refs[11:15]
    o_output, o_tokens, o_gqkv, o_gout, o_gup, o_gdown, o_gain = refs[15:22]
    refs = refs[22:]
    nu = len(UNITS)
    got1, got2, got3, res = (dict(zip(UNITS, refs[i * nu : (i + 1) * nu])) for i in range(4))
    refs = refs[4 * nu :]
    m_d, g_u0, g_u1, g_o, g_v, got0_d, got0_u0, got0_u1 = refs[:8]
    cot, middle, dmid, rows_buf, cols_buf, second, low, context, dcontext = refs[8:17]
    gains, gain_sum, gain_send, got_gain = refs[17:21]
    ssem, rsem, lsem, osem, rsems, csems, hsems, gs, gr, credit = refs[21:]
    here = coords()
    z, y, x, c = here
    me = owner(*here)
    ypeer, xpeer, speer = device(z, 1 - y, x, c), device(z, y, 1 - x, c), device(z, y, x, 1 - c)
    zof = [lax.rem(z + d, NZ) for d in range(NZ)]
    zpeers = [device(zof[d], y, x, c) for d in range(NZ)]
    peers = all_peers(*here)
    greet(peers)
    index = {u: i for i, u in enumerate(UNITS)}
    sent = {u: [] for u in UNITS}

    def core_rows(core, base, n):
        return pl.ds(pl.multiple_of(base + core * 32, 32), n)

    def mine(u, k, yy, xx, lo, n):
        if u in ("d0", "d1"):
            return m_d.at[k, yy, xx, pl.ds((64 if u == "d1" else 0) + lo, n)]
        buf, base = {"u0": (g_u0, 0), "u1": (g_u1, 0), "o": (g_o, 0), "v": (g_v, 0),
                     "q": (m_d, 0), "k": (m_d, 64)}[u]
        return buf.at[k, yy, xx, core_rows(c, base + lo, n)] if lo % 32 == 0 else buf.at[
            k, yy, xx, pl.ds(pl.multiple_of(base + lo + c * 32, 16), n)
        ]

    def first(u):
        if u in ("d0", "d1"):
            return got0_d.at[:, :, :, pl.ds(64 if u == "d1" else 0, 64)]
        if u in ("u0", "u1"):
            return got0_u0 if u == "u0" else got0_u1
        return got0_d.at[:, :, :, pl.ds("oqkv".index(u) * 32, 32)]

    def send(u, k, make, peer):
        def copy():
            src, dst = make()
            return remote(src, dst, ssem.at[index[u], k], rsem.at[index[u], k], peer)

        copy().start()
        sent[u].append(copy)

    def wait(u, k, ref):
        remote(ref, ref, ssem.at[index[u], k], rsem.at[index[u], k], speer).wait_recv()

    def add(dst, src):
        dst[...] = dst[...] + src[...]

    def own_down(u):
        n = 64 if u == "d1" else 0
        k = 8 if u == "d1" else 7
        src = h_grad.at[:, :, :, c, pl.ds(n, 64)]
        return pltpu.make_async_copy(src, m_d.at[:, :, :, pl.ds(n, 64)], lsem.at[k])

    def stage0(u):
        if u in ("d0", "d1"):
            n = 64 if u == "d1" else 0
            send(u, 0, lambda: (h_grad.at[:, :, :, 1 - c, pl.ds(n, 64)], first(u)), speer)
            own_down(u).start()
            return
        if u == "o":
            pl.semaphore_wait(credit, 1)
        buf, base = {"u0": (g_u0, 0), "u1": (g_u1, 0), "o": (g_o, 0), "v": (g_v, 0),
                     "q": (m_d, 0), "k": (m_d, 64)}[u]
        send(u, 0, lambda: (buf.at[:, :, :, core_rows(1 - c, base, 32)], first(u)), speer)

    def stage1(u):
        h, n = unit_shape(u)
        got = first(u)
        if u in ("d0", "d1"):
            own_down(u).wait()
        wait(u, 0, got)
        for far in (True, False):
            xx, yy = (1 - x, 1 - y) if far else (x, y)

            @pl.loop(0, NZ)
            def _(k):
                for j in range(2):
                    add(mine(u, k, j, xx, 0, h), got.at[k, j, xx, pl.ds(0, h)])
                    add(mine(u, k, yy, j, h, h), got.at[k, yy, j, pl.ds(h, h)])

            if far:
                every = slice(None)
                send(u, 1, lambda: (mine(u, every, every, 1 - x, 0, h), got1[u].at[0]), xpeer)
                send(u, 2, lambda: (mine(u, every, 1 - y, every, h, h), got1[u].at[1]), ypeer)
        if u == "d1":
            pl.semaphore_signal(credit, inc=1, device_id=speer, device_id_type=MESH)

    def stage2(u):
        h, n = unit_shape(u)
        wait(u, 1, got1[u].at[0])
        wait(u, 2, got1[u].at[1])
        for far in (True, False):
            xx, yy = (1 - x, 1 - y) if far else (x, y)

            @pl.loop(0, NZ)
            def _(k):
                add(mine(u, k, yy, x, 0, h), got1[u].at[0, k, yy])
                add(mine(u, k, y, xx, h, h), got1[u].at[1, k, xx])

            if far:
                every = slice(None)
                send(u, 3, lambda: (mine(u, every, 1 - y, x, 0, h), got2[u].at[0]), ypeer)
                send(u, 4, lambda: (mine(u, every, y, 1 - x, h, h), got2[u].at[1]), xpeer)

    def stage3(u):
        h, n = unit_shape(u)
        wait(u, 3, got2[u].at[0])
        wait(u, 4, got2[u].at[1])

        @pl.loop(0, NZ)
        def _(k):
            add(mine(u, k, y, x, 0, h), got2[u].at[0, k])
            add(mine(u, k, y, x, h, h), got2[u].at[1, k])

        for d in range(1, NZ):

            def make(d=d):
                return mine(u, zof[d], y, x, 0, 2 * h), got3[u].at[d - 1]

            send(u, 4 + d, make, zpeers[d])

    finals = []

    def stage4(u):
        h, n = unit_shape(u)
        for d in range(1, NZ):
            wait(u, 4 + d, got3[u].at[d - 1])
        total = mine(u, z, y, x, 0, 2 * h)[...].astype(jnp.float32)
        for d in range(1, NZ):
            total = total + got3[u][d - 1].astype(jnp.float32)
        res[u][...] = total
        result(u).start()
        finals.append(u)

    def result(u):
        dst = {
            "d0": o_gdown.at[pl.ds(0, 64)],
            "d1": o_gdown.at[pl.ds(64, 64)],
            "u0": o_gup.at[:, pl.ds(0, 2048)],
            "u1": o_gup.at[:, pl.ds(2048, 2048)],
            "o": o_gout,
            "q": o_gqkv.at[:, pl.ds(0, 1024)],
            "k": o_gqkv.at[:, pl.ds(1024, 1024)],
            "v": o_gqkv.at[:, pl.ds(2048, 1024)],
        }[u]
        return pltpu.make_async_copy(res[u], dst, osem.at[index[u]])

    stages = (stage0, stage1, stage2, stage3, stage4)
    stage0("d0")
    stage0("d1")

    def local(src, dst, k):
        cp = pltpu.make_async_copy(src, dst, lsem.at[k])
        cp.start()
        return cp

    row_steps = [(f_down, i) for i in range(8)] + [(f_out, i) for i in range(2)]
    col_steps = [(f_up, i) for i in range(8)] + [(f_qkv, i) for i in range(6)]

    def row_copy(j):
        ref, i = row_steps[j]
        return pltpu.make_async_copy(ref.at[pl.ds(i * 512, 512)], rows_buf.at[j % 2], rsems.at[j % 2])

    def col_copy(j):
        ref, i = col_steps[j]
        return pltpu.make_async_copy(ref.at[:, pl.ds(i * 512, 512)], cols_buf.at[j % 2], csems.at[j % 2])

    for j in range(2):
        row_copy(j).start()
        col_copy(j).start()
    early = [
        local(h_cot, cot, 0),
        local(h_middle, middle, 1),
        local(h_second, second, 2),
        local(h_gain, gains, 3),
        local(h_context, context, 4),
    ]

    def next_row(j):
        if j + 2 < len(row_steps):
            row_copy(j + 2).start()

    def next_col(j):
        if j + 2 < len(col_steps):
            col_copy(j + 2).start()

    def split(v):
        return v.astype(jnp.bfloat16).reshape(4, 2, 2, 64, v.shape[-1])

    def run(order, work):
        for name in order:
            if "." in name:
                u, k = name.split(".")
                stages[int(k)](u)
            else:
                for cut in range(len(name), 0, -1):
                    if name[:cut] in work:
                        rest = name[cut:]
                        work[name[:cut]](*([int(rest)] if rest else []))
                        break
                else:
                    raise KeyError(name)

    def phase_one(out_sum, hid, dact, act, dhid):
        def hid_copy(i):
            return pltpu.make_async_copy(
                h_hidden.at[:, pl.ds(i * 512, 512)], hid.at[i % 2], hsems.at[i % 2]
            )

        hid_copy(0).start()
        hid_copy(1).start()
        for cp in early:
            cp.wait()

        def chunk(i):
            slot = i % 2
            row_copy(i).wait()
            dact[...] = dot(cot[...], rows_buf[slot], 1, 1)
            hid_copy(i).wait()

            def step(r):
                v = hid[slot, r, :]
                sq = v * v
                t = jnp.tanh(GELU_A * (v + 0.044715 * v * sq))
                half = 0.5 * (1.0 + t)
                act[r, :] = (v * half).astype(jnp.bfloat16)
                slope = half + 0.5 * v * (1.0 - t * t) * (GELU_A * (1.0 + 3 * 0.044715 * sq))
                dhid[r, :] = (dact[r, :] * slope).astype(jnp.bfloat16)

            rows_loop(step)
            if i + 2 < 8:
                hid_copy(i + 2).start()
            base = middle if i == 0 else out_sum
            out_sum[...] = base[...] + dot(act[...], rows_buf[slot], 1, 0)
            next_row(i)
            g_u = g_u0 if i < 4 else g_u1
            s = slice((i % 4) * 512, (i % 4 + 1) * 512)
            g_u[:, :, :, :, s] = split(dot(second[...], dhid[...], 0, 0))
            col_copy(i).wait()
            part = dot(dhid[...], cols_buf[slot], 1, 1)
            dmid[...] = part if i == 0 else dmid[...] + part
            next_col(i)

        def norm_back_two():
            gain_sum[...] = jnp.zeros_like(gain_sum)

            def step(r):
                v, dn = middle[r, :], dmid[r, :]
                sc = scale_of(v)
                gain_sum[1:2, :] += jnp.sum(dn * v * sc, axis=0, keepdims=True)
                scaled = dn * gains[1:2, :]
                inner = jnp.mean(scaled * v, axis=-1, keepdims=True)
                total = cot[r, :].astype(jnp.float32) + (sc * scaled - v * (sc * sc * sc) * inner)
                dmid[r, :] = total
                low[r, :] = total.astype(jnp.bfloat16)
                dcontext[r, :] = out_sum[r, :].astype(jnp.bfloat16)

            rows_loop(step)

        run(NEAR, {"c": chunk, "nb": norm_back_two})

    f32, bf = jnp.float32, jnp.bfloat16
    pl.run_scoped(
        phase_one,
        pltpu.VMEM((512, 1024), f32),
        pltpu.VMEM((2, 512, 512), f32),
        pltpu.VMEM((512, 512), f32),
        pltpu.VMEM((512, 512), bf),
        pltpu.VMEM((512, 512), bf),
    )

    def phase_two(qkv, dqkv, bias, lse, dk_sum, dv_sum):
        out_copy = local(dcontext, o_output, 0)
        load_qkv = local(h_qkv, qkv, 1)
        load_lse = local(h_lse, lse, 3)
        load_tokens = local(h_tokens, second, 2)
        write_bias(lengths, bias)
        late = []

        def grad_out(i):
            s = slice(i * 512, (i + 1) * 512)
            g_o[:, :, :, :, s] = split(dot(context[...], low[:, s], 0, 0))

        def grad_context(i):
            if i == 0:
                out_copy.wait()
            j = 8 + i
            row_copy(j).wait()
            s = slice(i * 512, (i + 1) * 512)
            dcontext[:, s] = dot(low[...], rows_buf[j % 2], 1, 1).astype(bf)

        def attend_back(pair):
            if pair == 0:
                load_qkv.wait()
                load_lse.wait()
            lane = lax.broadcasted_iota(jnp.int32, (1, 128), 1)
            lower = lane < HD
            col = pair * 128
            for r0 in (256, 0):
                limit = r0 + 256
                q = qkv[r0:limit, col : col + 128]
                do = dcontext[r0:limit, col : col + 128]
                k = qkv[0:limit, 1024 + col : 1152 + col]
                v = qkv[0:limit, 2048 + col : 2176 + col]
                parts, dk, dv = [], None, None
                for h in range(2):
                    keep = lower if h == 0 else ~lower
                    qh = jnp.where(keep, q, jnp.zeros_like(q))
                    dh = jnp.where(keep, do, jnp.zeros_like(do))
                    sums = jnp.where(lane == pair * 2 + h, lse[r0:limit, :], 0.0)
                    sums = jnp.sum(sums, axis=1, keepdims=True)
                    prob = jnp.exp2(dot(qh, k, 1, 1) * SCALE2 + bias[r0:limit, 0:limit] - sums)
                    scaled = prob * dot(dh, v, 1, 1)
                    inner = jnp.sum(scaled, axis=1, keepdims=True)
                    dlogit = (scaled - prob * inner).astype(bf)
                    parts.append(dot(dlogit, k, 1, 0))
                    dk_h = dot(dlogit, qh, 0, 0)
                    dv_h = dot(prob.astype(bf), dh, 0, 0)
                    dk = dk_h if dk is None else dk + dk_h
                    dv = dv_h if dv is None else dv + dv_h
                scale = 1.0 / math.sqrt(HD)
                dqkv[r0:limit, col : col + 128] = (
                    jnp.where(lower, parts[0], parts[1]) * scale
                ).astype(bf)
                if limit == 512:
                    dk_sum[...] = dk
                    dv_sum[...] = dv
                else:
                    dk_sum[0:limit] += dk
                    dv_sum[0:limit] += dv
            dqkv[:, 1024 + col : 1152 + col] = (dk_sum[...] * scale).astype(bf)
            dqkv[:, 2048 + col : 2176 + col] = dv_sum[...].astype(bf)

        def free():
            for u in ("d0", "d1"):
                for copy in sent[u]:
                    copy().wait_send()
                sent[u] = []
            load_tokens.wait()

            def step(r):
                v = second[r, :].astype(f32)
                context[r, :] = (v * scale_of(v) * gains[0:1, :]).astype(bf)

            rows_loop(step)

        def grad_qkv(j, i):
            s = slice(i * 512, (i + 1) * 512)
            t = slice(j * 1024 + i * 512, j * 1024 + (i + 1) * 512)
            total = split(dot(context[...], dqkv[:, t], 0, 0))
            if j == 2:
                g_v[:, :, :, :, s] = total
            else:
                m_d[:, :, :, j * 64 : (j + 1) * 64, s] = total

        def grad_normed(i):
            j = 8 + i
            col_copy(j).wait()
            t = slice(i * 512, (i + 1) * 512)
            part = dot(dqkv[:, t], cols_buf[j % 2], 1, 1)
            middle[...] = part if i == 0 else middle[...] + part
            next_col(j)

        def norm_final():
            def step(r):
                v, dn = second[r, :].astype(f32), middle[r, :]
                sc = scale_of(v)
                gain_sum[0:1, :] += jnp.sum(dn * v * sc, axis=0, keepdims=True)
                scaled = dn * gains[0:1, :]
                inner = jnp.mean(scaled * v, axis=-1, keepdims=True)
                total = dmid[r, :] + (sc * scaled - v * (sc * sc * sc) * inner)
                low[r, :] = total.astype(bf)

            rows_loop(step)
            late.append(local(low, o_tokens, 0))

        gain_copies = []

        def gain_start():
            for b in range(8):
                gain_send[b] = gain_sum[:, b * 128 : (b + 1) * 128]
            for j, peer in enumerate(peers):
                block = (peer[0] * 4 + peer[1]) // 4
                cp = remote(gain_send.at[block], got_gain.at[me], gs.at[j], gr.at[j], peer)
                cp.start()
                gain_copies.append(cp)
            got_gain[me] = gain_send[me // 4]

        F = functools.partial
        run(
            LATE,
            {
                "go": grad_out,
                "dc": grad_context,
                "a": attend_back,
                "free": free,
                "gq": F(grad_qkv, 0),
                "gk": F(grad_qkv, 1),
                "gv": F(grad_qkv, 2),
                "dn": grad_normed,
                "nf": norm_final,
                "gs": gain_start,
            },
        )
        for cp in gain_copies:
            cp.wait()
        total = got_gain[0]
        for j in range(1, 32):
            total = total + got_gain[j]
        o_gain[...] = total
        for cp in late:
            cp.wait()

    pl.run_scoped(
        phase_two,
        pltpu.VMEM((512, 3072), bf),
        pltpu.VMEM((512, 3072), bf),
        pltpu.VMEM((512, 512), f32),
        pltpu.VMEM((512, 128), f32),
        pltpu.VMEM((512, 128), f32),
        pltpu.VMEM((512, 128), f32),
    )
    for u in UNITS:
        for copy in sent[u]:
            copy().wait_send()
    for u in finals:
        result(u).wait()


def backward(whole, saved, tokens, cotangent, lengths):
    gains, qkv, context, lse, middle, second, hidden, grad_down = saved
    grad_down = grad_down.reshape(4, 2, 2, 2, 128, 1024)
    hbm = pl.BlockSpec(memory_space=pl.ANY)
    vmem = pl.BlockSpec(memory_space=pltpu.VMEM)
    smem = pl.BlockSpec(memory_space=pltpu.SMEM)
    bf, f32, dma = jnp.bfloat16, jnp.float32, pltpu.SemaphoreType.DMA
    per = [unit_shape(u) for u in UNITS]
    scratch = (
        [((2, 4, 2, h, n), bf) for h, n in per]
        + [((2, 4, h, n), bf) for h, n in per]
        + [((3, 2 * h, n), bf) for h, n in per]
        + [((2 * h, n), f32) for h, n in per]
        + [
            ((4, 2, 2, 128, 1024), bf),
            ((4, 2, 2, 64, 2048), bf),
            ((4, 2, 2, 64, 2048), bf),
            ((4, 2, 2, 64, 1024), bf),
            ((4, 2, 2, 64, 1024), bf),
            ((4, 2, 2, 128, 1024), bf),
            ((4, 2, 2, 32, 2048), bf),
            ((4, 2, 2, 32, 2048), bf),
            ((512, 1024), bf),
            ((512, 1024), f32),
            ((512, 1024), f32),
            ((2, 512, 1024), bf),
            ((2, 1024, 512), bf),
            ((512, 1024), bf),
            ((512, 1024), bf),
            ((512, 1024), bf),
            ((512, 1024), bf),
            ((8, 1024), f32),
            ((8, 1024), f32),
            ((8, 8, 128), f32),
            ((32, 8, 128), f32),
        ]
    )
    outs = [
        ((512, 1024), bf),
        ((512, 1024), bf),
        ((32, 3072), f32),
        ((32, 1024), f32),
        ((32, 4096), f32),
        ((128, 1024), f32),
        ((8, 128), f32),
    ]
    nu = len(UNITS)
    return pl.pallas_call(
        backward_kernel,
        out_shape=[jax.ShapeDtypeStruct(*o) for o in outs],
        in_specs=[hbm] * 14 + [smem],
        out_specs=[hbm] * 6 + [vmem],
        scratch_shapes=[pltpu.VMEM(*v) for v in scratch]
        + [
            dma((nu, 8)),
            dma((nu, 8)),
            dma((9,)),
            dma((nu,)),
            dma((2,)),
            dma((2,)),
            dma((2,)),
            dma((31,)),
            dma((31,)),
            pltpu.SemaphoreType.REGULAR,
        ],
        compiler_params=pltpu.CompilerParams(
            collective_id=1, has_side_effects=True, vmem_limit_bytes=63 << 20
        ),
    )(
        *whole, qkv, context, lse, middle, second, hidden, grad_down, gains, tokens, cotangent, lengths
    )


def project_input(inputs, w_qkv, gain):
    normed, scale_one = normalize(inputs, gain)
    normed_low = normed.astype(jnp.bfloat16)
    mixed = jnp.dot(normed_low, w_qkv, preferred_element_type=jnp.float32).astype(jnp.bfloat16)
    split = mixed.reshape(inputs.shape[0], 3, H, HD)
    return (normed_low, scale_one, split[:, 0], split[:, 1], split[:, 2])


def feed_inputs(inputs, context, w_out, w_up, gain):
    middle = inputs + jnp.dot(context, w_out, preferred_element_type=jnp.float32)
    second, scale_two = normalize(middle, gain)
    second_low = second.astype(jnp.bfloat16)
    hidden = jnp.dot(second_low, w_up, preferred_element_type=jnp.float32)
    active = jax.nn.gelu(hidden, approximate=True).astype(jnp.bfloat16)
    return (middle, scale_two, second_low, hidden, active)


def layer(tokens, lengths, w_qkv, w_out, w_up, w_down, gain_attn, gain_mlp, cotangent, low_type):
    total_rows = tokens.shape[0]
    ends = jnp.cumsum(lengths[0])
    places = jnp.arange(total_rows, dtype=jnp.int32)
    segment = jnp.sum((places[:, None] >= ends[None, :]).astype(jnp.int32), axis=1)
    inputs = tokens.astype(jnp.float32)
    gain_attn, gain_mlp = gain_attn.astype(jnp.float32), gain_mlp.astype(jnp.float32)
    normed_low, scale_one, queries, keys_all, values_all = project_input(inputs, w_qkv, gain_attn)
    context_full, log_sums = attend_forward(queries, keys_all, values_all, segment)
    context = context_full.reshape(total_rows, H * HD).astype(jnp.bfloat16)
    middle, scale_two, second_low, hidden, active = feed_inputs(
        inputs, context, w_out, w_up, gain_mlp
    )
    output = (middle + jnp.dot(active, w_down, preferred_element_type=jnp.float32)).astype(
        jnp.bfloat16
    )
    grad_down = jnp.einsum("rf,rd->fd", active, cotangent, preferred_element_type=low_type)
    grad_active = jnp.einsum("rd,fd->rf", cotangent, w_down, preferred_element_type=jnp.float32)
    unused, gelu_pull = jax.vjp(lambda values: jax.nn.gelu(values, approximate=True), hidden)
    grad_hidden = gelu_pull(grad_active)[0].astype(jnp.bfloat16)
    grad_up = jnp.einsum("rd,rf->df", second_low, grad_hidden, preferred_element_type=low_type)
    grad_second = jnp.einsum("rf,df->rd", grad_hidden, w_up, preferred_element_type=jnp.float32)
    grad_mid_norm, grad_gain_m = norm_back(grad_second, middle, scale_two, gain_mlp)
    grad_middle = cotangent.astype(jnp.float32) + grad_mid_norm
    grad_mid_low = grad_middle.astype(jnp.bfloat16)
    grad_out = jnp.einsum("rc,rd->cd", context, grad_mid_low, preferred_element_type=low_type)
    grad_context = jnp.einsum("rd,cd->rc", grad_mid_low, w_out, preferred_element_type=jnp.float32)
    grad_context = grad_context.astype(jnp.bfloat16).reshape(total_rows, H, HD)
    grad_queries, grad_keys, grad_values = attend_backward(
        queries, keys_all, values_all, segment, log_sums, grad_context
    )
    grad_mixed = (
        jnp.stack([grad_queries, grad_keys, grad_values], axis=1)
        .reshape(total_rows, 3 * H * HD)
        .astype(jnp.bfloat16)
    )
    grad_qkv = jnp.einsum("rd,re->de", normed_low, grad_mixed, preferred_element_type=low_type)
    grad_normed = jnp.einsum("re,de->rd", grad_mixed, w_qkv, preferred_element_type=jnp.float32)
    grad_in_norm, grad_gain_a = norm_back(grad_normed, inputs, scale_one, gain_attn)
    grad_tokens = (grad_middle + grad_in_norm).astype(jnp.bfloat16)
    return (output, grad_tokens, grad_qkv, grad_out, grad_up, grad_down, grad_gain_a, grad_gain_m)


def shards_any(tokens, lengths, w_qkv, w_out, w_up, w_down, gain_attn, gain_mlp, cotangent):
    whole = gather_any(w_qkv, w_out, w_up, w_down, gain_attn, gain_mlp)
    out = layer(tokens, lengths, *whole, cotangent, jnp.float32)
    return out[:2] + sum_any(*out[2:])


def shards(tokens, lengths, w_qkv, w_out, w_up, w_down, gain_attn, gain_mlp, cotangent):
    me = lax.axis_index("dp") * 4 + lax.axis_index("fsdp")
    lanes = lax.rem(me, 4) * 32
    pair = jnp.stack([gain_attn, gain_mlp]).astype(jnp.float32)
    spot = lax.dynamic_update_slice(jnp.zeros((8, 128), jnp.float32), pair, (0, lanes))
    whole, saved = forward((w_qkv, w_out, w_up, w_down), spot, lengths, tokens, cotangent)
    output, grad_tokens, g_qkv, g_out, g_up, g_down, g_gain = backward(
        whole, saved, tokens, cotangent, lengths
    )
    own = lax.dynamic_slice(g_gain, (0, lanes), (2, 32))
    return (output, grad_tokens, g_qkv, g_out, g_up, g_down, own[0], own[1])


def solution(mesh):
    rows, flat = P(AXES, None), P(AXES)
    known = dict(mesh.shape) == {"dp": 8, "fsdp": 4}
    return jax.shard_map(
        shards if known else shards_any,
        mesh=mesh,
        in_specs=(rows, rows, rows, rows, rows, rows, flat, flat, rows),
        out_specs=(rows, rows, rows, rows, rows, rows, flat, flat),
        check_vma=False,
    )
```

```python
import functools
import math

import jax
import jax.numpy as jnp
from jax import lax
from jax.experimental import pallas as pl
from jax.experimental.pallas import tpu as pltpu
from jax.sharding import PartitionSpec as P

H = 16
HD = 64
MESH = pl.DeviceIdType.MESH
AXES = ("dp", "fsdp")


epsilon = 1e-05


def normalize(values, gain):
    scale_row = lax.rsqrt(jnp.mean(values * values, axis=-1, keepdims=True) + epsilon)
    return (values * scale_row * gain, scale_row)


def norm_back(grad_normed, values, scale_row, gain):
    scaled = grad_normed * gain
    grad_gain = jnp.sum(grad_normed * values * scale_row, axis=0)
    cubed = scale_row * scale_row * scale_row
    grad_values = scale_row * scaled - values * cubed * jnp.mean(
        scaled * values, axis=-1, keepdims=True
    )
    return (grad_values, grad_gain)


def block_logits(query_block, key_rows, segment):
    block_rows = query_block.shape[0]
    key_limit = key_rows.shape[0]
    raw = jnp.einsum("qhd,khd->hqk", query_block, key_rows, preferred_element_type=jnp.float32)
    query_place = jnp.arange(block_rows, dtype=jnp.int32)
    key_place = jnp.arange(key_limit, dtype=jnp.int32)
    allowed = (segment[:, None] == segment[None, :]) & (query_place[:, None] >= key_place[None, :])
    return jnp.where(allowed[None], raw * (1.0 / math.sqrt(HD)), -1e30)


def attend_forward(queries, keys_all, values_all, segment):
    logits = block_logits(queries, keys_all, segment)
    peak = jnp.max(logits, axis=-1, keepdims=True)
    raised = jnp.exp(logits - peak)
    totals = jnp.sum(raised, axis=-1, keepdims=True)
    attn_prob = (raised / totals).astype(jnp.bfloat16)
    contexts = jnp.einsum("hqk,khd->qhd", attn_prob, values_all, preferred_element_type=jnp.float32)
    log_sums = (peak + jnp.log(totals))[:, :, 0]
    return (contexts, log_sums)


def attend_backward(queries, keys_all, values_all, segment, log_sums, grad_context):
    logits = block_logits(queries, keys_all, segment)
    attn_prob = jnp.exp(logits - log_sums[:, :, None])
    rounded = attn_prob.astype(jnp.bfloat16)
    grad_prob = jnp.einsum(
        "qhd,khd->hqk", grad_context, values_all, preferred_element_type=jnp.float32
    )
    inner = jnp.sum(attn_prob * grad_prob, axis=-1, keepdims=True)
    grad_logit = (1.0 / math.sqrt(HD) * attn_prob * (grad_prob - inner)).astype(jnp.bfloat16)
    grad_queries = jnp.einsum(
        "hqk,khd->qhd", grad_logit, keys_all, preferred_element_type=jnp.float32
    )
    grad_keys = jnp.einsum("hqk,qhd->khd", grad_logit, queries, preferred_element_type=jnp.float32)
    grad_values = jnp.einsum(
        "hqk,qhd->khd", rounded, grad_context, preferred_element_type=jnp.float32
    )
    return (grad_queries, grad_keys, grad_values)


def gather_any(*weights):
    return tuple(lax.all_gather(w, AXES, axis=0, tiled=True) for w in weights)


def sum_any(*grads):
    return tuple(lax.psum_scatter(g, AXES, scatter_dimension=0, tiled=True) for g in grads)


NZ = 4


def coords():
    a, b = lax.axis_index("dp"), lax.axis_index("fsdp")
    return a // 2, a % 2, b // 2, b % 2


def device(z, y, x, c):
    return (z * 2 + y, x * 2 + c)


def owner(z, y, x, c):
    return ((z * 2 + y) * 2 + x) * 2 + c


def all_peers(z, y, x, c):
    peers = []
    for d in range(NZ):
        for m in range(2):
            for l in range(2):
                for s in range(2):
                    if d + m + l + s:
                        peers.append(
                            device(
                                lax.rem(z + d, NZ),
                                1 - y if m else y,
                                1 - x if l else x,
                                1 - c if s else c,
                            )
                        )
    return peers


def greet(peers):
    sem = pltpu.get_barrier_semaphore()
    for peer in peers:
        pl.semaphore_signal(sem, inc=1, device_id=peer, device_id_type=MESH)
    pl.semaphore_wait(sem, len(peers))


def remote(src, dst, send_sem, recv_sem, peer):
    return pltpu.make_async_remote_copy(
        src_ref=src, dst_ref=dst, send_sem=send_sem, recv_sem=recv_sem,
        device_id=peer, device_id_type=MESH,
    )


FORWARD = 512
SHARDS = ((32, 3072), (32, 1024), (32, 4096), (128, 1024), (8, 128))
PARTS = (
    (0, 0, 16, 0, 3072, "zyx"),
    (0, 16, 16, 0, 3072, "zxy"),
    (1, 0, 16, 0, 1024, "zyx"),
    (1, 16, 16, 0, 1024, "zxy"),
    (2, 0, 32, 0, 1792, "zyx"),
    (2, 0, 32, 1792, 1792, "zxy"),
    (2, 0, 32, 3584, 512, "xyz"),
    (3, 0, 48, 0, 1024, "zyx"),
    (3, 48, 48, 0, 1024, "zxy"),
    (3, 96, 32, 0, 1024, "yxz"),
    (4, 0, 8, 0, 128, "zyx"),
)
GROUPS = ((10, 0, 1), (2, 3), (4, 5, 6), (7, 8, 9))


def hops(dim):
    return (1, 3, 2) if dim == "z" else (1,)


def moved(rel, dim, e):
    d, m, l = rel
    if dim == "z":
        return ((d + e) % NZ, m, l)
    return (d, 1 - m, l) if dim == "y" else (d, m, 1 - l)


def routes(stages):
    hold, arrivals, slot = [(0, 0, 0)], [], {}
    for s, dim in enumerate(stages):
        new = []
        for rel in hold:
            for e in hops(dim):
                slot[(rel, s, e)] = len(arrivals)
                arrivals.append((moved(rel, dim, e), s))
                new.append(arrivals[-1][0])
        hold = hold + new
    return arrivals, slot


class Gather:
    def __init__(self, ins, outs, sems, here):
        self.ins, self.outs, (self.ssem, self.rsem) = ins, outs, sems
        z, y, x, c = here
        self.core = c
        self.zfrom = [lax.rem(z + NZ - d, NZ) for d in range(NZ)]
        self.ys, self.xs = (y, 1 - y), (x, 1 - x)
        self.peer = {("z", e): device(lax.rem(z + e, NZ), y, x, c) for e in range(1, NZ)}
        self.peer["y", 1] = device(z, 1 - y, x, c)
        self.peer["x", 1] = device(z, y, 1 - x, c)
        self.other = device(z, y, x, 1 - c)
        self.plan = [routes(p[5]) for p in PARTS]
        self.sent = []

    def place(self, part, rel, core):
        w, r0, nr, c0, nc, stages = PARTS[part]
        o = owner(self.zfrom[rel[0]], self.ys[rel[1]], self.xs[rel[2]], core)
        n = SHARDS[w][0]
        return self.outs[w].at[pl.ds(pl.multiple_of(o * n + r0, math.gcd(n, r0 or n, 16)), nr), pl.ds(c0, nc)]

    def send(self, part, rel, k, peer, own):
        w, r0, nr, c0, nc, stages = PARTS[part]
        dst = self.place(part, rel, self.core)
        src = self.ins[w].at[pl.ds(r0, nr), pl.ds(c0, nc)] if own else dst
        cp = remote(src, dst, self.ssem.at[part, k], self.rsem.at[part, k], peer)
        cp.start()
        self.sent.append(cp)

    def wait(self, part, rel, core, k):
        ref = self.place(part, rel, core)
        remote(ref, ref, self.ssem.at[part, k], self.rsem.at[part, k], self.other).wait_recv()

    def forward(self, part, rel, s, i):
        stages, slot = PARTS[part][5], self.plan[part][1]
        for t in range(s + 1, 3):
            for e in hops(stages[t]):
                self.send(part, rel, slot[rel, t, e], self.peer[stages[t], e], s < 0)
        self.send(part, rel, 15 + i, self.other, s < 0)

    def start(self, group):
        for part in group:
            self.forward(part, (0, 0, 0), -1, 0)

    def arrive(self, group, s):
        ks = [[k for k, a in enumerate(self.plan[p][0]) if a[1] == s] for p in group]
        steps = []
        for j in range(max(map(len, ks))):
            steps.append([(p, k[j]) for p, k in zip(group, ks) if j < len(k)])

        def one(step):
            for part, k in step:
                rel = self.plan[part][0][k][0]
                self.wait(part, rel, self.core, k)
                self.forward(part, rel, s, 1 + k)

        return [functools.partial(one, step) for step in steps]

    def halves(self, group):
        for part in group:
            for i, rel in enumerate([(0, 0, 0)] + [a[0] for a in self.plan[part][0]]):
                self.wait(part, rel, 1 - self.core, 15 + i)


def dot(a, b, ca, cb):
    return lax.dot_general(
        a, b, (((ca,), (cb,)), ((), ())), preferred_element_type=jnp.float32
    )


def scale_of(values):
    return lax.rsqrt(jnp.mean(values * values, axis=-1, keepdims=True) + epsilon)


def rows_loop(step):
    @pl.loop(0, 8)
    def _(i):
        step(pl.ds(pl.multiple_of(i * 64, 64), 64))


LOG2E = math.log2(math.e)
SCALE2 = LOG2E / math.sqrt(HD)


def write_bias(lengths, bias):
    ends, total = [], jnp.int32(0)
    for j in range(lengths.shape[1]):
        total = total + lengths[0, j]
        ends.append(total)
    key = lax.broadcasted_iota(jnp.int32, (1, 512), 1)
    seg_key = sum((key >= e).astype(jnp.int32) for e in ends)

    @pl.loop(0, 8)
    def _(i):
        query = lax.broadcasted_iota(jnp.int32, (64, 1), 0) + i * 64
        seg_query = sum((query >= e).astype(jnp.int32) for e in ends)
        ok = (seg_query == seg_key) & (query >= key)
        bias[pl.ds(pl.multiple_of(i * 64, 64), 64), :] = jnp.where(ok, 0.0, -1e30)


def attend_pair(pair, qkv, bias, context, lse):
    lane = lax.broadcasted_iota(jnp.int32, (1, 128), 1)
    low = lane < HD
    col = pl.multiple_of(pair * 128, 128)
    q = qkv[:, pl.ds(col, 128)]
    k = qkv[:, pl.ds(1024 + col, 128)]
    v = qkv[:, pl.ds(2048 + col, 128)]
    parts, sums = [], lse[...]
    for h in range(2):
        qh = jnp.where(low if h == 0 else ~low, q, jnp.zeros_like(q))
        logits = dot(qh, k, 1, 1) * SCALE2 + bias[...]
        peak = jnp.max(logits, axis=1, keepdims=True)
        raised = jnp.exp2(logits - peak)
        total = jnp.sum(raised, axis=1, keepdims=True)
        parts.append(dot(raised.astype(jnp.bfloat16), v, 1, 0) * (1.0 / total))
        sums = jnp.where(lane == pair * 2 + h, peak + jnp.log2(total), sums)
    context[:, pl.ds(col, 128)] = jnp.where(low, parts[0], parts[1]).astype(jnp.bfloat16)
    lse[...] = sums


GELU_A = math.sqrt(2.0 / math.pi)


def forward_kernel(*refs):
    ins, gain_in, lengths, tokens, cotangent = refs[:4], *refs[4:8]
    outs = refs[8:12]
    o_gain, o_qkv, o_context, o_lse, o_middle, o_second, o_active, o_slope, o_grad = refs[12:21]
    w_qkv, w_out, w_up, normed, qkv, bias, context, lse, middle, second = refs[21:31]
    hid, act, slope, grad, gains, gain_row = refs[31:37]
    lsem, wsem, hsem, gsem, ssem, rsem = refs[37:]
    here = coords()
    me = owner(*here)
    g = Gather((*ins, gain_in), (*outs, gains), (ssem, rsem), here)
    greet([*g.peer.values(), g.other])
    g.start(GROUPS[0])
    for w in range(4):
        n = SHARDS[w][0]
        cp = pltpu.make_async_copy(
            ins[w], outs[w].at[pl.ds(pl.multiple_of(me * n, n), n)], lsem.at[w]
        )
        cp.start()
    own = [
        pltpu.make_async_copy(
            ins[w],
            outs[w].at[pl.ds(pl.multiple_of(me * SHARDS[w][0], SHARDS[w][0]), SHARDS[w][0])],
            lsem.at[w],
        )
        for w in range(4)
    ]
    gains[pl.ds(pl.multiple_of(me * 8, 8), 8), :] = gain_in[...]
    g.start(GROUPS[1])
    g.start(GROUPS[2])
    write_bias(lengths, bias)
    saves = []

    def save(src, dst, k):
        cp = pltpu.make_async_copy(src, dst, lsem.at[k])
        cp.start()
        saves.append(cp)

    def gain_rows():
        for b in range(8):
            total = gains[32 * b : 32 * b + 8, :]
            for j in range(1, 4):
                total = total + gains[32 * b + 8 * j : 32 * b + 8 * j + 8, :]
            gain_row[:, b * 128 : (b + 1) * 128] = total
        save(gain_row, o_gain, 4)

    def norm_one():
        def step(r):
            v = tokens[r, :].astype(jnp.float32)
            normed[r, :] = (v * scale_of(v) * gain_row[0:1, :]).astype(jnp.bfloat16)

        rows_loop(step)

    def load(w, dst, n):
        width = SHARDS[w][1] // n
        g.halves(GROUPS[w])
        own[w].wait()
        for i in range(n):
            s = pl.ds(i * width, width)
            pltpu.make_async_copy(outs[w].at[:, s], dst.at[:, s], wsem.at[w, i]).start()

    def loaded(w, dst, n, i):
        s = pl.ds(i * (SHARDS[w][1] // n), SHARDS[w][1] // n)
        pltpu.make_async_copy(outs[w].at[:, s], dst.at[:, s], wsem.at[w, i]).wait()

    def project(i):
        loaded(0, w_qkv, 6, i)
        s = slice(i * 512, (i + 1) * 512)
        qkv[:, s] = dot(normed[...], w_qkv[:, s], 1, 0).astype(jnp.bfloat16)

    def attend(i):
        @pl.loop(0, 2)
        def _(j):
            attend_pair(i * 2 + j, qkv, bias, context, lse)

    def attended():
        save(qkv, o_qkv, 5)
        save(context, o_context, 6)
        save(lse, o_lse, 7)

    def add_out(i):
        loaded(1, w_out, 2, i)
        s = slice(i * 512, (i + 1) * 512)
        middle[:, s] = tokens[:, s].astype(jnp.float32) + dot(context[...], w_out[:, s], 1, 0)

    def norm_two():
        save(middle, o_middle, 8)

        def step(r):
            v = middle[r, :]
            second[r, :] = (v * scale_of(v) * gain_row[1:2, :]).astype(jnp.bfloat16)

        rows_loop(step)
        save(second, o_second, 9)

    hid_copies, grad_copies = [], []

    def feed(i):
        loaded(2, w_up, 8, i)
        s = slice(i * 512, (i + 1) * 512)
        slot = i % 2
        if i >= 2:
            for cp in hid_copies[i - 2]:
                cp.wait()
        hid[...] = dot(second[...], w_up[:, s], 1, 0)

        def step(r):
            v = hid[r, :]
            sq = v * v
            t = jnp.tanh(GELU_A * (v + 0.044715 * v * sq))
            half = 0.5 * (1.0 + t)
            act[slot, r, :] = (v * half).astype(jnp.bfloat16)
            rise = half + 0.5 * v * (1.0 - t * t) * (GELU_A * (1.0 + 3 * 0.044715 * sq))
            slope[slot, r, :] = rise.astype(jnp.bfloat16)

        rows_loop(step)
        pair = [
            pltpu.make_async_copy(act.at[slot], o_active.at[:, s], hsem.at[slot]),
            pltpu.make_async_copy(slope.at[slot], o_slope.at[:, s], hsem.at[2 + slot]),
        ]
        for cp in pair:
            cp.start()
        hid_copies.append(pair)
        if i >= 2:
            grad_copies[i - 2].wait()
        grad[slot] = dot(act[slot], cotangent[...], 0, 0).astype(jnp.bfloat16)
        cp = pltpu.make_async_copy(grad.at[slot], o_grad.at[s, :], gsem.at[slot])
        cp.start()
        grad_copies.append(cp)

    events = []
    for t in range(1, 7):
        if t == 1:
            events += [functools.partial(g.start, GROUPS[3])]
        for s in (0, 1, 2):
            if 0 <= t - s - 1 < 4:
                events += g.arrive(GROUPS[t - s - 1], s)
                if s == 2:
                    events.append("whole%d" % (t - s - 1))
    F = functools.partial
    work = {
        0: [gain_rows, norm_one]
        + [F(project, i) for i in range(6)] + [F(attend, i) for i in range(4)] + [attended],
        1: [F(add_out, i) for i in range(2)] + [norm_two],
        2: [F(feed, i) for i in range(8)],
    }
    ready, since = [], 0
    n_load = {0: (w_qkv, 6), 1: (w_out, 2), 2: (w_up, 8)}
    lse[...] = jnp.zeros_like(lse)
    for e in events:
        if isinstance(e, str):
            w = int(e[5:])
            if w in n_load:
                ready.append(F(load, w, *n_load[w]))
                ready += work[w]
            continue
        e()
        since += 1
        if ready and since >= EVERY:
            ready.pop(0)()
            since = 0
    for step in ready:
        step()
    g.halves(GROUPS[3])
    own[3].wait()
    for cp in hid_copies[-2] + hid_copies[-1] + grad_copies[-2:] + saves:
        cp.wait()
    for cp in g.sent:
        cp.wait_send()


EVERY = 1


def forward(weights, gains, lengths, tokens, cotangent):
    hbm = pl.BlockSpec(memory_space=pl.ANY)
    vmem = pl.BlockSpec(memory_space=pltpu.VMEM)
    smem = pl.BlockSpec(memory_space=pltpu.SMEM)
    bf, f32 = jnp.bfloat16, jnp.float32
    saved = [
        ((8, 1024), f32),
        ((512, 3072), bf),
        ((512, 1024), bf),
        ((512, 128), f32),
        ((512, 1024), f32),
        ((512, 1024), bf),
        ((512, 4096), bf),
        ((512, 4096), bf),
        ((4096, 1024), bf),
    ]
    scratch = [
        ((1024, 3072), bf),
        ((1024, 1024), bf),
        ((1024, 4096), bf),
        ((512, 1024), bf),
        ((512, 3072), bf),
        ((512, 512), f32),
        ((512, 1024), bf),
        ((512, 128), f32),
        ((512, 1024), f32),
        ((512, 1024), bf),
        ((512, 512), f32),
        ((2, 512, 512), bf),
        ((2, 512, 512), bf),
        ((2, 512, 1024), bf),
        ((256, 128), f32),
        ((8, 1024), f32),
    ]
    dma = pltpu.SemaphoreType.DMA
    out = pl.pallas_call(
        forward_kernel,
        out_shape=[jax.ShapeDtypeStruct((w.shape[0] * 32, w.shape[1]), w.dtype) for w in weights]
        + [jax.ShapeDtypeStruct(*s) for s in saved],
        in_specs=[vmem] * 5 + [smem, vmem, vmem],
        out_specs=[hbm] * 13,
        scratch_shapes=[pltpu.VMEM(*s) for s in scratch]
        + [
            dma((10,)),
            dma((3, 8)),
            dma((4,)),
            dma((2,)),
            dma((len(PARTS), 31)),
            dma((len(PARTS), 31)),
        ],
        compiler_params=pltpu.CompilerParams(
            collective_id=0, has_side_effects=True, vmem_limit_bytes=60 << 20
        ),
    )(*weights, gains, lengths, tokens, cotangent)
    return out[:4], out[4:]


UNITS = ("dz", "d0", "u0", "u1", "o", "q", "k", "v")
SHAPE = {"dz": (32, 1024), "d0": (32, 1024), "u0": (16, 2048), "u1": (16, 2048)}
NEAR = (
    "d0.1", "dz.1", "c0", "c1", "c2", "c3", "u0.0", "c4", "c5", "d0.2", "c6", "c7", "u0.1", "u1.0",
    "ds0", "ds1", "ds2", "d0.3", "ds3", "nb",
)
LATE = (
    "u1.1", "go0", "go1", "o.0", "dc0", "dc1", "a0", "a1", "o.1", "u0.2", "a2", "a3", "a4", "a5",
    "a6", "u1.2", "a7", "rn", "gq0", "gq1", "q.0", "o.2", "gk0", "dz.2", "gk1", "k.0", "gv0", "gv1",
    "v.0", "ad0", "q.1", "u0.3", "ad1", "k.1", "ad2", "v.1", "ad3", "ad4", "u1.3", "ad5", "d0.4",
    "ad6", "o.3", "ad7", "oe", "dn0", "dn1", "dn2", "dz.3", "dn3", "nf", "gs", "q.2", "u0.4", "k.2",
    "dz.4", "u1.4", "v.2", "q.3", "o.4", "k.3", "v.3", "q.4", "k.4", "v.4",
)


def unit_shape(u):
    return SHAPE.get(u, (16, 1024))


def backward_kernel(*refs):
    f_qkv, f_out, f_up, f_down, h_qkv, h_context, h_lse, h_middle, h_second, h_act, h_slope, h_grad = (
        refs[:12]
    )
    h_gain, h_tokens, h_cot, lengths = refs[12:16]
    o_output, o_tokens, o_gqkv, o_gout, o_gup, o_gdown, o_gain = refs[16:23]
    refs = refs[23:]
    nu = len(UNITS)
    got1, got2, got3, res = (dict(zip(UNITS, refs[i * nu : (i + 1) * nu])) for i in range(4))
    refs = refs[4 * nu :]
    m_d, g_u0, g_u1, g_o, g_q, g_k, g_v, stage_a, stage_b, got0_d, got0_u = refs[:11]
    refs = refs[11:]
    cot, middle, dmid, rows_buf, wide_buf, part_buf, second, low, context, dcontext = refs[:10]
    gains, gain_sum, gain_send, got_gain = refs[10:14]
    ssem, rsem, lsem, osem, rsems, wsems, psems, gs, gr, credit, credit_u = refs[14:]
    here = coords()
    z, y, x, c = here
    me = owner(*here)
    ypeer, xpeer, speer = device(z, 1 - y, x, c), device(z, y, 1 - x, c), device(z, y, x, 1 - c)
    zof = [lax.rem(z + d, NZ) for d in range(NZ)]
    zpeers = [device(zof[d], y, x, c) for d in range(NZ)]
    peers = all_peers(*here)
    greet(peers)
    index = {u: i for i, u in enumerate(UNITS)}
    sent = {u: [] for u in UNITS}
    left = []
    every = slice(None)
    own = {"u0": g_u0, "u1": g_u1, "o": g_o, "q": g_q, "k": g_k, "v": g_v}
    staged = {
        "u0": (stage_a, 0, None),
        "u1": (stage_b, 0, None),
        "o": (stage_a, 0, "u0"),
        "q": (stage_a, 1024, "u0"),
        "k": (stage_b, 0, "u1"),
        "v": (stage_b, 1024, "u1"),
    }
    down_row = {"d0": 0, "dz": 64}

    def mine(u, k, yy, xx, lo, n):
        if u in down_row:
            return m_d.at[k, yy, xx, pl.ds(down_row[u] + lo, n)]
        return own[u].at[k, yy, xx, pl.ds(lo, n)]

    def first(u):
        if u in down_row:
            return got0_d.at[:, :, :, pl.ds(down_row[u], 64)]
        if u in ("u0", "u1"):
            return got0_u
        return got0_d.at[:, :, :, pl.ds("oqkv".index(u) * 32, 32)]

    def send(u, k, make, peer):
        def copy():
            src, dst = make()
            return remote(src, dst, ssem.at[index[u], k], rsem.at[index[u], k], peer)

        copy().start()
        sent[u].append(copy)

    def wait(u, k, ref):
        remote(ref, ref, ssem.at[index[u], k], rsem.at[index[u], k], speer).wait_recv()

    def add(dst, src):
        dst[...] = dst[...] + src[...]

    def own_down(u):
        src = h_grad.at[:, :, :, c, pl.ds(down_row[u], 64)]
        dst = m_d.at[:, :, :, pl.ds(down_row[u], 64)]
        return pltpu.make_async_copy(src, dst, lsem.at[7 if u == "d0" else 8])

    def stage0(u):
        if u in down_row:
            n = down_row[u]
            send(u, 0, lambda: (h_grad.at[:, :, :, 1 - c, pl.ds(n, 64)], first(u)), speer)
            own_down(u).start()
            return
        if u == "o":
            pl.semaphore_wait(credit, 2)
        if u == "u1":
            pl.semaphore_wait(credit_u, 1)
        buf, col, before = staged[u]
        send(u, 0, lambda: (buf.at[:, :, :, :, pl.ds(col, own[u].shape[4])], first(u)), speer)

    def put(u, t, lhs, rhs):
        buf, col, before = staged[u]
        if before and before not in left:
            sent[before].pop(0)().wait_send()
            left.append(before)
        far = slice(t.start + col, t.stop + col)
        for k in range(4):
            v = dot(lhs[:, k * 256 : (k + 1) * 256], rhs, 0, 0).astype(jnp.bfloat16)
            v = v.reshape(2, 2, 64, v.shape[1])
            for core in range(2):

                @pl.when(c == core)
                def _():
                    own[u][k, :, :, :, t] = v[:, :, core * 32 : core * 32 + 32]
                    buf[k, :, :, :, far] = v[:, :, 32 - core * 32 : 64 - core * 32]

    def stage1(u):
        h, n = unit_shape(u)
        got = first(u)
        if u in down_row:
            own_down(u).wait()
        wait(u, 0, got)
        if u == "dz":
            for d in (1, 2, 3, 0):
                for yy in range(2):
                    for xx in range(2):
                        add(mine(u, zof[d], yy, xx, 0, 64), got.at[zof[d], yy, xx])
                if d:
                    send(
                        u,
                        4 + d,
                        lambda d=d: (mine(u, zof[d], every, every, 0, 64), got1[u].at[d - 1]),
                        zpeers[d],
                    )
            pl.semaphore_signal(credit, inc=1, device_id=speer, device_id_type=MESH)
            return
        for far in (True, False):
            xx, yy = (1 - x, 1 - y) if far else (x, y)

            @pl.loop(0, NZ)
            def _(k):
                for j in range(2):
                    add(mine(u, k, j, xx, 0, h), got.at[k, j, xx, pl.ds(0, h)])
                    add(mine(u, k, yy, j, h, h), got.at[k, yy, j, pl.ds(h, h)])

            if far:
                send(u, 1, lambda: (mine(u, every, every, 1 - x, 0, h), got1[u].at[0]), xpeer)
                send(u, 2, lambda: (mine(u, every, 1 - y, every, h, h), got1[u].at[1]), ypeer)
        if u in ("d0", "u0"):
            done = credit if u == "d0" else credit_u
            pl.semaphore_signal(done, inc=1, device_id=speer, device_id_type=MESH)

    def stage2(u):
        h, n = unit_shape(u)
        if u == "dz":
            for d in range(1, NZ):
                wait(u, 4 + d, got1[u].at[d - 1])
            for xx in (1 - x, x):
                for yy in range(2):
                    at = mine(u, z, yy, xx, 0, 64)
                    total = at[...].astype(jnp.float32)
                    for d in range(1, NZ):
                        total = total + got1[u][d - 1, yy, xx].astype(jnp.float32)
                    at[...] = total.astype(jnp.bfloat16)
                if xx is not x:
                    send(u, 1, lambda: (mine(u, z, every, 1 - x, 0, 64), got2[u]), xpeer)
            return
        wait(u, 1, got1[u].at[0])
        wait(u, 2, got1[u].at[1])
        for far in (True, False):
            xx, yy = (1 - x, 1 - y) if far else (x, y)

            @pl.loop(0, NZ)
            def _(k):
                add(mine(u, k, yy, x, 0, h), got1[u].at[0, k, yy])
                add(mine(u, k, y, xx, h, h), got1[u].at[1, k, xx])

            if far:
                send(u, 3, lambda: (mine(u, every, 1 - y, x, 0, h), got2[u].at[0]), ypeer)
                send(u, 4, lambda: (mine(u, every, y, 1 - x, h, h), got2[u].at[1]), xpeer)

    def stage3(u):
        h, n = unit_shape(u)
        if u == "dz":
            wait(u, 1, got2[u])
            for yy in (1 - y, y):
                add(mine(u, z, yy, x, 0, 64), got2[u].at[yy])
                if yy is not y:
                    send(u, 3, lambda: (mine(u, z, 1 - y, x, 0, 64), got3[u]), ypeer)
            return
        wait(u, 3, got2[u].at[0])
        wait(u, 4, got2[u].at[1])

        @pl.loop(0, NZ)
        def _(k):
            add(mine(u, k, y, x, 0, h), got2[u].at[0, k])
            add(mine(u, k, y, x, h, h), got2[u].at[1, k])

        for d in range(1, NZ):

            def make(d=d):
                return mine(u, zof[d], y, x, 0, 2 * h), got3[u].at[d - 1]

            send(u, 4 + d, make, zpeers[d])

    finals = []

    def stage4(u):
        h, n = unit_shape(u)
        total = mine(u, z, y, x, 0, 2 * h)[...].astype(jnp.float32)
        if u == "dz":
            wait(u, 3, got3[u])
            total = total + got3[u][...].astype(jnp.float32)
        else:
            for d in range(1, NZ):
                wait(u, 4 + d, got3[u].at[d - 1])
            for d in range(1, NZ):
                total = total + got3[u][d - 1].astype(jnp.float32)
        res[u][...] = total
        result(u).start()
        finals.append(u)

    def result(u):
        dst = {
            "d0": o_gdown.at[pl.ds(0, 64)],
            "dz": o_gdown.at[pl.ds(64, 64)],
            "u0": o_gup.at[:, pl.ds(0, 2048)],
            "u1": o_gup.at[:, pl.ds(2048, 2048)],
            "o": o_gout,
            "q": o_gqkv.at[:, pl.ds(0, 1024)],
            "k": o_gqkv.at[:, pl.ds(1024, 1024)],
            "v": o_gqkv.at[:, pl.ds(2048, 1024)],
        }[u]
        return pltpu.make_async_copy(res[u], dst, osem.at[index[u]])

    stages = (stage0, stage1, stage2, stage3, stage4)
    stage0("d0")
    stage0("dz")

    def local(src, dst, k):
        cp = pltpu.make_async_copy(src, dst, lsem.at[k])
        cp.start()
        return cp

    row_steps = [(f_down, i) for i in range(8)] + [(f_out, i) for i in range(2)]
    row_steps += [(f_down, i) for i in range(8)]
    wide_steps = [(f_up, 4096, i) for i in range(4)] + [(f_qkv, 3072, i) for i in range(4)]
    part_steps = [(h_slope, i) for i in range(8)] + [(h_act, i) for i in range(8)]

    def row_copy(j):
        ref, i = row_steps[j]
        return pltpu.make_async_copy(ref.at[pl.ds(i * 512, 512)], rows_buf.at[j % 2], rsems.at[j % 2])

    def wide_copy(j):
        ref, n, i = wide_steps[j]
        dst = wide_buf.at[j % 2, :, pl.ds(0, n)]
        return pltpu.make_async_copy(ref.at[pl.ds(i * 256, 256)], dst, wsems.at[j % 2])

    def part_copy(j):
        ref, i = part_steps[j]
        return pltpu.make_async_copy(ref.at[:, pl.ds(i * 512, 512)], part_buf.at[j % 2], psems.at[j % 2])

    early = [local(h_cot, cot, 0), local(h_second, second, 2)]
    for copy in (row_copy, part_copy, wide_copy):
        copy(0).start()
        copy(1).start()
    early += [
        local(h_middle, middle, 1),
        local(h_gain, gains, 3),
        local(h_context, context, 4),
    ]

    def following(copy, steps, j):
        if j + 2 < len(steps):
            copy(j + 2).start()

    def run(order, work):
        for name in order:
            if "." in name:
                u, k = name.split(".")
                stages[int(k)](u)
            else:
                short = name.rstrip("0123456789")
                rest = name[len(short) :]
                work[short](*([int(rest)] if rest else []))

    def phase_one(dhid):
        def chunk(i):
            if i == 0:
                early[0].wait()
                early[1].wait()
            slot = i % 2
            s = slice(i * 512, (i + 1) * 512)
            row_copy(i).wait()
            part_copy(i).wait()
            grown = dot(cot[...], rows_buf[slot], 1, 1) * part_buf[slot].astype(jnp.float32)
            dhid[:, s] = grown.astype(jnp.bfloat16)
            following(row_copy, row_steps, i)
            following(part_copy, part_steps, i)
            t = slice((i % 4) * 512, (i % 4 + 1) * 512)
            put("u0" if i < 4 else "u1", t, second, dhid[:, s])

        def grad_second(i):
            wide_copy(i).wait()
            s = slice(i * 256, (i + 1) * 256)
            dmid[:, s] = dot(dhid[...], wide_buf[i % 2], 1, 1)
            following(wide_copy, wide_steps, i)

        def norm_back_two():
            for cp in early[2:]:
                cp.wait()
            gain_sum[...] = jnp.zeros_like(gain_sum)

            def step(r):
                v, dn = middle[r, :], dmid[r, :]
                sc = scale_of(v)
                gain_sum[1:2, :] += jnp.sum(dn * v * sc, axis=0, keepdims=True)
                scaled = dn * gains[1:2, :]
                inner = jnp.mean(scaled * v, axis=-1, keepdims=True)
                total = cot[r, :].astype(jnp.float32) + (sc * scaled - v * (sc * sc * sc) * inner)
                dmid[r, :] = total
                low[r, :] = total.astype(jnp.bfloat16)

            rows_loop(step)

        run(NEAR, {"c": chunk, "ds": grad_second, "nb": norm_back_two})

    f32, bf = jnp.float32, jnp.bfloat16
    pl.run_scoped(phase_one, pltpu.VMEM((512, 4096), bf))

    def phase_two(qkv, dqkv, bias, lse, dk_sum, dv_sum):
        load_qkv = local(h_qkv, qkv, 1)
        load_lse = local(h_lse, lse, 3)
        load_tokens = local(h_tokens, second, 2)
        late = {}

        def grad_out(i):
            s = slice(i * 512, (i + 1) * 512)
            put("o", s, context, low[:, s])

        def grad_context(i):
            j = 8 + i
            row_copy(j).wait()
            s = slice(i * 512, (i + 1) * 512)
            dcontext[:, s] = dot(low[...], rows_buf[j % 2], 1, 1).astype(bf)
            following(row_copy, row_steps, j)

        def attend_back(pair):
            if pair == 0:
                load_qkv.wait()
                load_lse.wait()
                write_bias(lengths, bias)
            lane = lax.broadcasted_iota(jnp.int32, (1, 128), 1)
            lower = lane < HD
            col = pair * 128
            scale = 1.0 / math.sqrt(HD)
            for r0 in (256, 0):
                limit = r0 + 256
                q = qkv[r0:limit, col : col + 128]
                do = dcontext[r0:limit, col : col + 128]
                k = qkv[0:limit, 1024 + col : 1152 + col]
                v = qkv[0:limit, 2048 + col : 2176 + col]
                parts, dk, dv = [], None, None
                for h in range(2):
                    keep_lane = lower if h == 0 else ~lower
                    qh = jnp.where(keep_lane, q, jnp.zeros_like(q))
                    dh = jnp.where(keep_lane, do, jnp.zeros_like(do))
                    sums = jnp.where(lane == pair * 2 + h, lse[r0:limit, :], 0.0)
                    sums = jnp.sum(sums, axis=1, keepdims=True)
                    prob = jnp.exp2(dot(qh, k, 1, 1) * SCALE2 + bias[r0:limit, 0:limit] - sums)
                    scaled = prob * dot(dh, v, 1, 1)
                    inner = jnp.sum(scaled, axis=1, keepdims=True)
                    dlogit = (scaled - prob * inner).astype(bf)
                    parts.append(dot(dlogit, k, 1, 0))
                    dk_h = dot(dlogit, qh, 0, 0)
                    dv_h = dot(prob.astype(bf), dh, 0, 0)
                    dk = dk_h if dk is None else dk + dk_h
                    dv = dv_h if dv is None else dv + dv_h
                dqkv[r0:limit, col : col + 128] = (
                    jnp.where(lower, parts[0], parts[1]) * scale
                ).astype(bf)
                if limit == 512:
                    dk_sum[...] = dk
                    dv_sum[...] = dv
                else:
                    dk_sum[0:limit] += dk
                    dv_sum[0:limit] += dv
            dqkv[:, 1024 + col : 1152 + col] = (dk_sum[...] * scale).astype(bf)
            dqkv[:, 2048 + col : 2176 + col] = dv_sum[...].astype(bf)

        def renorm():
            load_tokens.wait()

            def step(r):
                v = second[r, :].astype(f32)
                context[r, :] = (v * scale_of(v) * gains[0:1, :]).astype(bf)

            rows_loop(step)

        def grad_qkv(j, i):
            s = slice(i * 512, (i + 1) * 512)
            t = slice(j * 1024 + i * 512, j * 1024 + (i + 1) * 512)
            put("qkv"[j], s, context, dqkv[:, t])

        def add_down(i):
            j = 10 + i
            row_copy(j).wait()
            part_copy(8 + i).wait()
            middle[...] = middle[...] + dot(part_buf[i % 2], rows_buf[j % 2], 1, 0)
            following(row_copy, row_steps, j)
            following(part_copy, part_steps, 8 + i)

        def out_end():
            rows_loop(lambda r: dcontext.__setitem__((r, every), middle[r, :].astype(bf)))
            late["out"] = local(dcontext, o_output, 5)

        def grad_normed(i):
            j = 4 + i
            wide_copy(j).wait()
            s = slice(i * 256, (i + 1) * 256)
            middle[:, s] = dot(dqkv[...], wide_buf[j % 2, :, 0:3072], 1, 1)
            following(wide_copy, wide_steps, j)

        def norm_final():
            def step(r):
                v, dn = second[r, :].astype(f32), middle[r, :]
                sc = scale_of(v)
                gain_sum[0:1, :] += jnp.sum(dn * v * sc, axis=0, keepdims=True)
                scaled = dn * gains[0:1, :]
                inner = jnp.mean(scaled * v, axis=-1, keepdims=True)
                total = dmid[r, :] + (sc * scaled - v * (sc * sc * sc) * inner)
                low[r, :] = total.astype(bf)

            rows_loop(step)
            late["tokens"] = local(low, o_tokens, 0)

        gain_copies = []

        def gain_start():
            for b in range(8):
                gain_send[b] = gain_sum[:, b * 128 : (b + 1) * 128]
            for j, peer in enumerate(peers):
                block = (peer[0] * 4 + peer[1]) // 4
                cp = remote(gain_send.at[block], got_gain.at[me], gs.at[j], gr.at[j], peer)
                cp.start()
                gain_copies.append(cp)
            got_gain[me] = gain_send[me // 4]

        F = functools.partial
        run(
            LATE,
            {
                "go": grad_out,
                "dc": grad_context,
                "a": attend_back,
                "rn": renorm,
                "gq": F(grad_qkv, 0),
                "gk": F(grad_qkv, 1),
                "gv": F(grad_qkv, 2),
                "ad": add_down,
                "oe": out_end,
                "dn": grad_normed,
                "nf": norm_final,
                "gs": gain_start,
            },
        )
        for cp in gain_copies:
            cp.wait()
        total = got_gain[0]
        for j in range(1, 32):
            total = total + got_gain[j]
        o_gain[...] = total
        for cp in late.values():
            cp.wait()

    pl.run_scoped(
        phase_two,
        pltpu.VMEM((512, 3072), bf),
        pltpu.VMEM((512, 3072), bf),
        pltpu.VMEM((512, 512), f32),
        pltpu.VMEM((512, 128), f32),
        pltpu.VMEM((512, 128), f32),
        pltpu.VMEM((512, 128), f32),
    )
    for u in UNITS:
        for copy in sent[u]:
            copy().wait_send()
    for u in finals:
        result(u).wait()


def backward(whole, saved, tokens, cotangent, lengths):
    gains, qkv, context, lse, middle, second, active, slope, grad_down = saved
    grad_down = grad_down.reshape(4, 2, 2, 2, 128, 1024)
    hbm = pl.BlockSpec(memory_space=pl.ANY)
    vmem = pl.BlockSpec(memory_space=pltpu.VMEM)
    smem = pl.BlockSpec(memory_space=pltpu.SMEM)
    bf, f32, dma = jnp.bfloat16, jnp.float32, pltpu.SemaphoreType.DMA
    per = {u: unit_shape(u) for u in UNITS}
    got1 = [(2, 4, 2, h, n) if u != "dz" else (3, 2, 2, 64, n) for u, (h, n) in per.items()]
    got2 = [(2, 4, h, n) if u != "dz" else (2, 64, n) for u, (h, n) in per.items()]
    got3 = [(3, 2 * h, n) if u != "dz" else (64, n) for u, (h, n) in per.items()]
    scratch = (
        [(v, bf) for v in got1 + got2 + got3]
        + [((2 * h, n), f32) for h, n in per.values()]
        + [
            ((4, 2, 2, 128, 1024), bf),
            ((4, 2, 2, 32, 2048), bf),
            ((4, 2, 2, 32, 2048), bf),
            ((4, 2, 2, 32, 1024), bf),
            ((4, 2, 2, 32, 1024), bf),
            ((4, 2, 2, 32, 1024), bf),
            ((4, 2, 2, 32, 1024), bf),
            ((4, 2, 2, 32, 2048), bf),
            ((4, 2, 2, 32, 2048), bf),
            ((4, 2, 2, 128, 1024), bf),
            ((4, 2, 2, 32, 2048), bf),
            ((512, 1024), bf),
            ((512, 1024), f32),
            ((512, 1024), f32),
            ((2, 512, 1024), bf),
            ((2, 256, 4096), bf),
            ((2, 512, 512), bf),
            ((512, 1024), bf),
            ((512, 1024), bf),
            ((512, 1024), bf),
            ((512, 1024), bf),
            ((8, 1024), f32),
            ((8, 1024), f32),
            ((8, 8, 128), f32),
            ((32, 8, 128), f32),
        ]
    )
    outs = [
        ((512, 1024), bf),
        ((512, 1024), bf),
        ((32, 3072), f32),
        ((32, 1024), f32),
        ((32, 4096), f32),
        ((128, 1024), f32),
        ((8, 128), f32),
    ]
    nu = len(UNITS)
    return pl.pallas_call(
        backward_kernel,
        out_shape=[jax.ShapeDtypeStruct(*o) for o in outs],
        in_specs=[hbm] * 15 + [smem],
        out_specs=[hbm] * 6 + [vmem],
        scratch_shapes=[pltpu.VMEM(*v) for v in scratch]
        + [
            dma((nu, 8)),
            dma((nu, 8)),
            dma((9,)),
            dma((nu,)),
            dma((2,)),
            dma((2,)),
            dma((2,)),
            dma((31,)),
            dma((31,)),
            pltpu.SemaphoreType.REGULAR,
            pltpu.SemaphoreType.REGULAR,
        ],
        compiler_params=pltpu.CompilerParams(
            collective_id=1, has_side_effects=True, vmem_limit_bytes=63 << 20
        ),
    )(
        *whole, qkv, context, lse, middle, second, active, slope, grad_down, gains, tokens, cotangent, lengths
    )


def project_input(inputs, w_qkv, gain):
    normed, scale_one = normalize(inputs, gain)
    normed_low = normed.astype(jnp.bfloat16)
    mixed = jnp.dot(normed_low, w_qkv, preferred_element_type=jnp.float32).astype(jnp.bfloat16)
    split = mixed.reshape(inputs.shape[0], 3, H, HD)
    return (normed_low, scale_one, split[:, 0], split[:, 1], split[:, 2])


def feed_inputs(inputs, context, w_out, w_up, gain):
    middle = inputs + jnp.dot(context, w_out, preferred_element_type=jnp.float32)
    second, scale_two = normalize(middle, gain)
    second_low = second.astype(jnp.bfloat16)
    hidden = jnp.dot(second_low, w_up, preferred_element_type=jnp.float32)
    active = jax.nn.gelu(hidden, approximate=True).astype(jnp.bfloat16)
    return (middle, scale_two, second_low, hidden, active)


def layer(tokens, lengths, w_qkv, w_out, w_up, w_down, gain_attn, gain_mlp, cotangent, low_type):
    total_rows = tokens.shape[0]
    ends = jnp.cumsum(lengths[0])
    places = jnp.arange(total_rows, dtype=jnp.int32)
    segment = jnp.sum((places[:, None] >= ends[None, :]).astype(jnp.int32), axis=1)
    inputs = tokens.astype(jnp.float32)
    gain_attn, gain_mlp = gain_attn.astype(jnp.float32), gain_mlp.astype(jnp.float32)
    normed_low, scale_one, queries, keys_all, values_all = project_input(inputs, w_qkv, gain_attn)
    context_full, log_sums = attend_forward(queries, keys_all, values_all, segment)
    context = context_full.reshape(total_rows, H * HD).astype(jnp.bfloat16)
    middle, scale_two, second_low, hidden, active = feed_inputs(
        inputs, context, w_out, w_up, gain_mlp
    )
    output = (middle + jnp.dot(active, w_down, preferred_element_type=jnp.float32)).astype(
        jnp.bfloat16
    )
    grad_down = jnp.einsum("rf,rd->fd", active, cotangent, preferred_element_type=low_type)
    grad_active = jnp.einsum("rd,fd->rf", cotangent, w_down, preferred_element_type=jnp.float32)
    unused, gelu_pull = jax.vjp(lambda values: jax.nn.gelu(values, approximate=True), hidden)
    grad_hidden = gelu_pull(grad_active)[0].astype(jnp.bfloat16)
    grad_up = jnp.einsum("rd,rf->df", second_low, grad_hidden, preferred_element_type=low_type)
    grad_second = jnp.einsum("rf,df->rd", grad_hidden, w_up, preferred_element_type=jnp.float32)
    grad_mid_norm, grad_gain_m = norm_back(grad_second, middle, scale_two, gain_mlp)
    grad_middle = cotangent.astype(jnp.float32) + grad_mid_norm
    grad_mid_low = grad_middle.astype(jnp.bfloat16)
    grad_out = jnp.einsum("rc,rd->cd", context, grad_mid_low, preferred_element_type=low_type)
    grad_context = jnp.einsum("rd,cd->rc", grad_mid_low, w_out, preferred_element_type=jnp.float32)
    grad_context = grad_context.astype(jnp.bfloat16).reshape(total_rows, H, HD)
    grad_queries, grad_keys, grad_values = attend_backward(
        queries, keys_all, values_all, segment, log_sums, grad_context
    )
    grad_mixed = (
        jnp.stack([grad_queries, grad_keys, grad_values], axis=1)
        .reshape(total_rows, 3 * H * HD)
        .astype(jnp.bfloat16)
    )
    grad_qkv = jnp.einsum("rd,re->de", normed_low, grad_mixed, preferred_element_type=low_type)
    grad_normed = jnp.einsum("re,de->rd", grad_mixed, w_qkv, preferred_element_type=jnp.float32)
    grad_in_norm, grad_gain_a = norm_back(grad_normed, inputs, scale_one, gain_attn)
    grad_tokens = (grad_middle + grad_in_norm).astype(jnp.bfloat16)
    return (output, grad_tokens, grad_qkv, grad_out, grad_up, grad_down, grad_gain_a, grad_gain_m)


def shards_any(tokens, lengths, w_qkv, w_out, w_up, w_down, gain_attn, gain_mlp, cotangent):
    whole = gather_any(w_qkv, w_out, w_up, w_down, gain_attn, gain_mlp)
    out = layer(tokens, lengths, *whole, cotangent, jnp.float32)
    return out[:2] + sum_any(*out[2:])


def keep_kernel(*refs):
    n = (len(refs) - 2) // 3
    gets, puts = refs[-2:]
    into = [pltpu.make_async_copy(refs[i], refs[2 * n + i], gets.at[i]) for i in range(n)]
    back = [pltpu.make_async_copy(refs[2 * n + i], refs[n + i], puts.at[i]) for i in range(n)]
    for cp in into:
        cp.start()
    for i in range(n):
        into[i].wait()
        back[i].start()
    for cp in back:
        cp.wait()


def keep(arrays):
    hbm = pl.BlockSpec(memory_space=pl.ANY)
    return pl.pallas_call(
        keep_kernel,
        out_shape=[jax.ShapeDtypeStruct(a.shape, a.dtype) for a in arrays],
        in_specs=[hbm] * len(arrays),
        out_specs=[hbm] * len(arrays),
        scratch_shapes=[pltpu.VMEM(a.shape, a.dtype) for a in arrays]
        + [pltpu.SemaphoreType.DMA((len(arrays),))] * 2,
    )(*arrays)


def shards(tokens, lengths, w_qkv, w_out, w_up, w_down, gain_attn, gain_mlp, cotangent):
    me = lax.axis_index("dp") * 4 + lax.axis_index("fsdp")
    lanes = lax.rem(me, 4) * 32
    pair = jnp.stack([gain_attn, gain_mlp]).astype(jnp.float32)
    spot = lax.dynamic_update_slice(jnp.zeros((8, 128), jnp.float32), pair, (0, lanes))
    whole, saved = forward((w_qkv, w_out, w_up, w_down), spot, lengths, tokens, cotangent)
    output, grad_tokens, g_qkv, g_out, g_up, g_down, g_gain = backward(
        whole, saved, tokens, cotangent, lengths
    )
    own = lax.dynamic_slice(g_gain, (0, lanes), (2, 32))
    kept = keep((output, grad_tokens, g_qkv, g_out, g_up, g_down))
    return (*kept, own[0], own[1])


def solution(mesh):
    rows, flat = P(AXES, None), P(AXES)
    known = dict(mesh.shape) == {"dp": 8, "fsdp": 4}
    return jax.shard_map(
        shards if known else shards_any,
        mesh=mesh,
        in_specs=(rows, rows, rows, rows, rows, rows, flat, flat, rows),
        out_specs=(rows, rows, rows, rows, rows, rows, flat, flat),
        check_vma=False,
    )
```

```python
import functools
import math

import jax
import jax.numpy as jnp
from jax import lax
from jax.experimental import pallas as pl
from jax.experimental.pallas import tpu as pltpu
from jax.sharding import PartitionSpec as P

H = 16
HD = 64
MESH = pl.DeviceIdType.MESH
AXES = ("dp", "fsdp")


epsilon = 1e-05


def normalize(values, gain):
    scale_row = lax.rsqrt(jnp.mean(values * values, axis=-1, keepdims=True) + epsilon)
    return (values * scale_row * gain, scale_row)


def norm_back(grad_normed, values, scale_row, gain):
    scaled = grad_normed * gain
    grad_gain = jnp.sum(grad_normed * values * scale_row, axis=0)
    cubed = scale_row * scale_row * scale_row
    grad_values = scale_row * scaled - values * cubed * jnp.mean(
        scaled * values, axis=-1, keepdims=True
    )
    return (grad_values, grad_gain)


def block_logits(query_block, key_rows, segment):
    block_rows = query_block.shape[0]
    key_limit = key_rows.shape[0]
    raw = jnp.einsum("qhd,khd->hqk", query_block, key_rows, preferred_element_type=jnp.float32)
    query_place = jnp.arange(block_rows, dtype=jnp.int32)
    key_place = jnp.arange(key_limit, dtype=jnp.int32)
    allowed = (segment[:, None] == segment[None, :]) & (query_place[:, None] >= key_place[None, :])
    return jnp.where(allowed[None], raw * (1.0 / math.sqrt(HD)), -1e30)


def attend_forward(queries, keys_all, values_all, segment):
    logits = block_logits(queries, keys_all, segment)
    peak = jnp.max(logits, axis=-1, keepdims=True)
    raised = jnp.exp(logits - peak)
    totals = jnp.sum(raised, axis=-1, keepdims=True)
    attn_prob = (raised / totals).astype(jnp.bfloat16)
    contexts = jnp.einsum("hqk,khd->qhd", attn_prob, values_all, preferred_element_type=jnp.float32)
    log_sums = (peak + jnp.log(totals))[:, :, 0]
    return (contexts, log_sums)


def attend_backward(queries, keys_all, values_all, segment, log_sums, grad_context):
    logits = block_logits(queries, keys_all, segment)
    attn_prob = jnp.exp(logits - log_sums[:, :, None])
    rounded = attn_prob.astype(jnp.bfloat16)
    grad_prob = jnp.einsum(
        "qhd,khd->hqk", grad_context, values_all, preferred_element_type=jnp.float32
    )
    inner = jnp.sum(attn_prob * grad_prob, axis=-1, keepdims=True)
    grad_logit = (1.0 / math.sqrt(HD) * attn_prob * (grad_prob - inner)).astype(jnp.bfloat16)
    grad_queries = jnp.einsum(
        "hqk,khd->qhd", grad_logit, keys_all, preferred_element_type=jnp.float32
    )
    grad_keys = jnp.einsum("hqk,qhd->khd", grad_logit, queries, preferred_element_type=jnp.float32)
    grad_values = jnp.einsum(
        "hqk,qhd->khd", rounded, grad_context, preferred_element_type=jnp.float32
    )
    return (grad_queries, grad_keys, grad_values)


def gather_any(*weights):
    return tuple(lax.all_gather(w, AXES, axis=0, tiled=True) for w in weights)


def sum_any(*grads):
    return tuple(lax.psum_scatter(g, AXES, scatter_dimension=0, tiled=True) for g in grads)


NZ = 4


def coords():
    a, b = lax.axis_index("dp"), lax.axis_index("fsdp")
    return a // 2, a % 2, b // 2, b % 2


def device(z, y, x, c):
    return (z * 2 + y, x * 2 + c)


def owner(z, y, x, c):
    return ((z * 2 + y) * 2 + x) * 2 + c


def all_peers(z, y, x, c):
    peers = []
    for d in range(NZ):
        for m in range(2):
            for l in range(2):
                for s in range(2):
                    if d + m + l + s:
                        peers.append(
                            device(
                                lax.rem(z + d, NZ),
                                1 - y if m else y,
                                1 - x if l else x,
                                1 - c if s else c,
                            )
                        )
    return peers


def greet(peers):
    sem = pltpu.get_barrier_semaphore()
    for peer in peers:
        pl.semaphore_signal(sem, inc=1, device_id=peer, device_id_type=MESH)
    pl.semaphore_wait(sem, len(peers))


def remote(src, dst, send_sem, recv_sem, peer):
    return pltpu.make_async_remote_copy(
        src_ref=src, dst_ref=dst, send_sem=send_sem, recv_sem=recv_sem,
        device_id=peer, device_id_type=MESH,
    )


FORWARD = 512
SHARDS = ((32, 3072), (32, 1024), (32, 4096), (128, 1024), (8, 128))
PARTS = (
    (0, 0, 32, 0, 1280, "21yx"),
    (0, 0, 32, 1280, 1280, "21xy"),
    (0, 0, 32, 2560, 512, "xy21"),
    (1, 0, 16, 0, 1024, "21yx"),
    (1, 16, 16, 0, 1024, "21xy"),
    (2, 0, 32, 0, 896, "21yx"),
    (2, 0, 32, 896, 768, "21xy"),
    (2, 0, 32, 1664, 384, "xy21"),
    (2, 0, 32, 2048, 768, "21yx"),
    (2, 0, 32, 2816, 896, "21xy"),
    (2, 0, 32, 3712, 384, "yx21"),
    (3, 0, 48, 0, 1024, "21yx"),
    (3, 48, 48, 0, 1024, "21xy"),
    (3, 96, 32, 0, 1024, "yx21"),
    (4, 0, 8, 0, 128, "21yx"),
)
GROUPS = ((14, 0, 1, 2), (3, 4), (5, 6, 7), (8, 9, 10), (11, 12, 13))
STEPS = 4


def z_twins(z):
    return (z, z + 1 - 2 * lax.rem(z, 2), lax.rem(z + 2, NZ), NZ - 1 - z)


def moved(rel, dim):
    e, m, l = rel
    return {"1": (e ^ 1, m, l), "2": (e ^ 2, m, l), "y": (e, 1 - m, l), "x": (e, m, 1 - l)}[dim]


def routes(stages):
    hold, arrivals, slot = [(0, 0, 0)], [], {}
    for s, dim in enumerate(stages):
        new = []
        for rel in hold:
            slot[rel, s] = len(arrivals)
            arrivals.append((moved(rel, dim), s))
            new.append(arrivals[-1][0])
        hold = hold + new
    return arrivals, slot


class Gather:
    def __init__(self, ins, outs, sems, here):
        self.ins, self.outs, (self.ssem, self.rsem) = ins, outs, sems
        z, y, x, c = here
        self.core = c
        self.zfrom = z_twins(z)
        self.ys, self.xs = (y, 1 - y), (x, 1 - x)
        self.peer = {"1": device(self.zfrom[1], y, x, c), "2": device(self.zfrom[2], y, x, c)}
        self.peer["y"] = device(z, 1 - y, x, c)
        self.peer["x"] = device(z, y, 1 - x, c)
        self.other = device(z, y, x, 1 - c)
        self.plan = [routes(p[5]) for p in PARTS]
        self.sent = []

    def place(self, part, rel, core):
        w, r0, nr, c0, nc, stages = PARTS[part]
        o = owner(self.zfrom[rel[0]], self.ys[rel[1]], self.xs[rel[2]], core)
        n = SHARDS[w][0]
        return self.outs[w].at[pl.ds(pl.multiple_of(o * n + r0, math.gcd(n, r0 or n, 16)), nr), pl.ds(c0, nc)]

    def send(self, part, rel, k, peer, own):
        w, r0, nr, c0, nc, stages = PARTS[part]
        dst = self.place(part, rel, self.core)
        src = self.ins[w].at[pl.ds(r0, nr), pl.ds(c0, nc)] if own else dst
        cp = remote(src, dst, self.ssem.at[part, k], self.rsem.at[part, k], peer)
        cp.start()
        self.sent.append(cp)

    def wait(self, part, rel, core, k):
        ref = self.place(part, rel, core)
        remote(ref, ref, self.ssem.at[part, k], self.rsem.at[part, k], self.other).wait_recv()

    def forward(self, part, rel, s, i):
        stages, slot = PARTS[part][5], self.plan[part][1]
        for t in range(s + 1, STEPS):
            self.send(part, rel, slot[rel, t], self.peer[stages[t]], s < 0)
        self.send(part, rel, 15 + i, self.other, s < 0)

    def start(self, group):
        for part in group:
            self.forward(part, (0, 0, 0), -1, 0)

    def arrive(self, group, s):
        ks = [[k for k, a in enumerate(self.plan[p][0]) if a[1] == s] for p in group]
        steps = []
        for j in range(max(map(len, ks))):
            steps.append([(p, k[j]) for p, k in zip(group, ks) if j < len(k)])

        def one(step):
            for part, k in step:
                rel = self.plan[part][0][k][0]
                self.wait(part, rel, self.core, k)
                self.forward(part, rel, s, 1 + k)

        return [functools.partial(one, step) for step in steps]

    def halves(self, group):
        for part in group:
            for i, rel in enumerate([(0, 0, 0)] + [a[0] for a in self.plan[part][0]]):
                self.wait(part, rel, 1 - self.core, 15 + i)


def dot(a, b, ca, cb):
    return lax.dot_general(
        a, b, (((ca,), (cb,)), ((), ())), preferred_element_type=jnp.float32
    )


def scale_of(values):
    return lax.rsqrt(jnp.mean(values * values, axis=-1, keepdims=True) + epsilon)


def rows_loop(step):
    @pl.loop(0, 8)
    def _(i):
        step(pl.ds(pl.multiple_of(i * 64, 64), 64))


LOG2E = math.log2(math.e)
SCALE2 = LOG2E / math.sqrt(HD)


def write_bias(lengths, bias):
    ends, total = [], jnp.int32(0)
    for j in range(lengths.shape[1]):
        total = total + lengths[0, j]
        ends.append(total)
    key = lax.broadcasted_iota(jnp.int32, (1, 512), 1)
    seg_key = sum((key >= e).astype(jnp.int32) for e in ends)

    @pl.loop(0, 8)
    def _(i):
        query = lax.broadcasted_iota(jnp.int32, (64, 1), 0) + i * 64
        seg_query = sum((query >= e).astype(jnp.int32) for e in ends)
        ok = (seg_query == seg_key) & (query >= key)
        bias[pl.ds(pl.multiple_of(i * 64, 64), 64), :] = jnp.where(ok, 0.0, -1e30)


def attend_pair(pair, qkv, bias, context, lse):
    lane = lax.broadcasted_iota(jnp.int32, (1, 128), 1)
    low = lane < HD
    col = pl.multiple_of(pair * 128, 128)
    q = qkv[:, pl.ds(col, 128)]
    k = qkv[:, pl.ds(1024 + col, 128)]
    v = qkv[:, pl.ds(2048 + col, 128)]
    parts, sums = [], lse[...]
    for h in range(2):
        qh = jnp.where(low if h == 0 else ~low, q, jnp.zeros_like(q))
        logits = dot(qh, k, 1, 1) * SCALE2 + bias[...]
        peak = jnp.max(logits, axis=1, keepdims=True)
        raised = jnp.exp2(logits - peak)
        total = jnp.sum(raised, axis=1, keepdims=True)
        parts.append(dot(raised.astype(jnp.bfloat16), v, 1, 0) * (1.0 / total))
        sums = jnp.where(lane == pair * 2 + h, peak + jnp.log2(total), sums)
    context[:, pl.ds(col, 128)] = jnp.where(low, parts[0], parts[1]).astype(jnp.bfloat16)
    lse[...] = sums


GELU_A = math.sqrt(2.0 / math.pi)


def forward_kernel(*refs):
    ins, gain_in, lengths, tokens, cotangent = refs[:4], *refs[4:8]
    outs = refs[8:12]
    o_gain, o_qkv, o_context, o_lse, o_middle, o_second, o_active, o_slope, o_grad = refs[12:21]
    w_qkv, w_out, w_up, normed, qkv, bias, context, lse, middle, second = refs[21:31]
    hid, act, slope, grad, gains, gain_row = refs[31:37]
    lsem, wsem, hsem, gsem, ssem, rsem = refs[37:]
    here = coords()
    me = owner(*here)
    g = Gather((*ins, gain_in), (*outs, gains), (ssem, rsem), here)
    greet([*g.peer.values(), g.other])
    g.start(GROUPS[0])
    for w in range(4):
        n = SHARDS[w][0]
        cp = pltpu.make_async_copy(
            ins[w], outs[w].at[pl.ds(pl.multiple_of(me * n, n), n)], lsem.at[w]
        )
        cp.start()
    own = [
        pltpu.make_async_copy(
            ins[w],
            outs[w].at[pl.ds(pl.multiple_of(me * SHARDS[w][0], SHARDS[w][0]), SHARDS[w][0])],
            lsem.at[w],
        )
        for w in range(4)
    ]
    gains[pl.ds(pl.multiple_of(me * 8, 8), 8), :] = gain_in[...]
    write_bias(lengths, bias)
    saves = []

    def save(src, dst, k):
        cp = pltpu.make_async_copy(src, dst, lsem.at[k])
        cp.start()
        saves.append(cp)

    def gain_rows():
        for b in range(8):
            total = gains[32 * b : 32 * b + 8, :]
            for j in range(1, 4):
                total = total + gains[32 * b + 8 * j : 32 * b + 8 * j + 8, :]
            gain_row[:, b * 128 : (b + 1) * 128] = total
        save(gain_row, o_gain, 4)

    def norm_one():
        def step(r):
            v = tokens[r, :].astype(jnp.float32)
            normed[r, :] = (v * scale_of(v) * gain_row[0:1, :]).astype(jnp.bfloat16)

        rows_loop(step)

    def load(group, w, dst, n, blocks):
        width = SHARDS[w][1] // n
        g.halves(GROUPS[group])
        if 0 in blocks:
            own[w].wait()
        for i in blocks:
            s = pl.ds(i * width, width)
            pltpu.make_async_copy(outs[w].at[:, s], dst.at[:, s], wsem.at[w, i]).start()

    def loaded(w, dst, n, i):
        s = pl.ds(i * (SHARDS[w][1] // n), SHARDS[w][1] // n)
        pltpu.make_async_copy(outs[w].at[:, s], dst.at[:, s], wsem.at[w, i]).wait()

    def project(i):
        loaded(0, w_qkv, 6, i)
        s = slice(i * 512, (i + 1) * 512)
        qkv[:, s] = dot(normed[...], w_qkv[:, s], 1, 0).astype(jnp.bfloat16)

    def attend(i):
        attend_pair(i, qkv, bias, context, lse)

    def attended():
        save(qkv, o_qkv, 5)
        save(context, o_context, 6)
        save(lse, o_lse, 7)

    def add_out(i):
        loaded(1, w_out, 2, i)
        s = slice(i * 512, (i + 1) * 512)
        middle[:, s] = tokens[:, s].astype(jnp.float32) + dot(context[...], w_out[:, s], 1, 0)

    def norm_two():
        save(middle, o_middle, 8)

        def step(r):
            v = middle[r, :]
            second[r, :] = (v * scale_of(v) * gain_row[1:2, :]).astype(jnp.bfloat16)

        rows_loop(step)
        save(second, o_second, 9)

    hid_copies, grad_copies = [], []

    def feed(i):
        loaded(2, w_up, 8, i)
        s = slice(i * 512, (i + 1) * 512)
        slot = i % 2
        if i >= 2:
            for cp in hid_copies[i - 2]:
                cp.wait()
        hid[...] = dot(second[...], w_up[:, s], 1, 0)

        def step(r):
            v = hid[r, :]
            sq = v * v
            t = jnp.tanh(GELU_A * (v + 0.044715 * v * sq))
            half = 0.5 * (1.0 + t)
            act[slot, r, :] = (v * half).astype(jnp.bfloat16)
            rise = half + 0.5 * v * (1.0 - t * t) * (GELU_A * (1.0 + 3 * 0.044715 * sq))
            slope[slot, r, :] = rise.astype(jnp.bfloat16)

        rows_loop(step)
        pair = [
            pltpu.make_async_copy(act.at[slot], o_active.at[:, s], hsem.at[slot]),
            pltpu.make_async_copy(slope.at[slot], o_slope.at[:, s], hsem.at[2 + slot]),
        ]
        for cp in pair:
            cp.start()
        hid_copies.append(pair)

    def feed_grad(i):
        slot = i % 2
        s = slice(i * 512, (i + 1) * 512)
        if i >= 2:
            grad_copies[i - 2].wait()
        grad[slot] = dot(act[slot], cotangent[...], 0, 0).astype(jnp.bfloat16)
        cp = pltpu.make_async_copy(grad.at[slot], o_grad.at[s, :], gsem.at[slot])
        cp.start()
        grad_copies.append(cp)

    events = []
    for t in range(1, STEPS + len(GROUPS)):
        if t < len(GROUPS):
            events += [functools.partial(g.start, GROUPS[t])]
        for s in reversed(range(STEPS)):
            if 0 <= t - s - 1 < len(GROUPS):
                events += g.arrive(GROUPS[t - s - 1], s)
                if s == STEPS - 1:
                    events.append("whole%d" % (t - s - 1))
    F = functools.partial
    work = {
        0: [gain_rows, norm_one]
        + [F(project, i) for i in range(6)] + [F(attend, i) for i in range(8)] + [attended],
        1: [F(add_out, i) for i in range(2)] + [norm_two],
        2: [F(f, i) for i in range(4) for f in (feed, feed_grad)],
        3: [F(f, i) for i in range(4, 8) for f in (feed, feed_grad)],
    }
    ready, since = [], 0
    n_load = {
        0: (0, w_qkv, 6, range(6)),
        1: (1, w_out, 2, range(2)),
        2: (2, w_up, 8, range(4)),
        3: (2, w_up, 8, range(4, 8)),
    }
    lse[...] = jnp.zeros_like(lse)
    for e in events:
        if isinstance(e, str):
            w = int(e[5:])
            if w in n_load:
                ready.append(F(load, w, *n_load[w]))
                ready += work[w]
            continue
        e()
        since += 1
        if ready and since >= EVERY:
            ready.pop(0)()
            since = 0
    for step in ready:
        step()
    g.halves(GROUPS[-1])
    own[3].wait()
    for cp in hid_copies[-2] + hid_copies[-1] + grad_copies[-2:] + saves:
        cp.wait()
    for cp in g.sent:
        cp.wait_send()


EVERY = 1


def forward(weights, gains, lengths, tokens, cotangent):
    hbm = pl.BlockSpec(memory_space=pl.ANY)
    vmem = pl.BlockSpec(memory_space=pltpu.VMEM)
    smem = pl.BlockSpec(memory_space=pltpu.SMEM)
    bf, f32 = jnp.bfloat16, jnp.float32
    saved = [
        ((8, 1024), f32),
        ((512, 3072), bf),
        ((512, 1024), bf),
        ((512, 128), f32),
        ((512, 1024), f32),
        ((512, 1024), bf),
        ((512, 4096), bf),
        ((512, 4096), bf),
        ((4096, 1024), bf),
    ]
    scratch = [
        ((1024, 3072), bf),
        ((1024, 1024), bf),
        ((1024, 4096), bf),
        ((512, 1024), bf),
        ((512, 3072), bf),
        ((512, 512), f32),
        ((512, 1024), bf),
        ((512, 128), f32),
        ((512, 1024), f32),
        ((512, 1024), bf),
        ((512, 512), f32),
        ((2, 512, 512), bf),
        ((2, 512, 512), bf),
        ((2, 512, 1024), bf),
        ((256, 128), f32),
        ((8, 1024), f32),
    ]
    dma = pltpu.SemaphoreType.DMA
    out = pl.pallas_call(
        forward_kernel,
        out_shape=[jax.ShapeDtypeStruct((w.shape[0] * 32, w.shape[1]), w.dtype) for w in weights]
        + [jax.ShapeDtypeStruct(*s) for s in saved],
        in_specs=[vmem] * 5 + [smem, vmem, vmem],
        out_specs=[hbm] * 13,
        scratch_shapes=[pltpu.VMEM(*s) for s in scratch]
        + [
            dma((10,)),
            dma((3, 8)),
            dma((4,)),
            dma((2,)),
            dma((len(PARTS), 31)),
            dma((len(PARTS), 31)),
        ],
        compiler_params=pltpu.CompilerParams(
            collective_id=0, has_side_effects=True, vmem_limit_bytes=60 << 20
        ),
    )(*weights, gains, lengths, tokens, cotangent)
    return out[:4], out[4:]


UNITS = ("dz", "d0", "u0", "u1", "o", "q", "k", "v")
SHAPE = {"dz": (32, 1024), "d0": (32, 1024), "u0": (16, 2048), "u1": (16, 2048)}
NEAR = (
    "d0.1", "dz.1", "c0", "c1", "c2", "c3", "u0.0", "c4", "d0.2", "c5", "c6", "u0.1", "c7", "u1.0",
    "ds0", "d0.3", "ds1", "ds2", "ds3", "nb",
)
LATE = (
    "u1.1", "go0", "dz.2", "go1", "o.0", "dc0", "dc1", "a0", "u0.2", "o.1", "d0.4", "a1", "a2",
    "a3", "a4", "a5", "u1.2", "a6", "a7", "u0.3", "rn", "gq0", "gq1", "q.0", "gk0", "gk1", "k.0",
    "gv0", "o.2", "dz.3", "gv1", "v.0", "q.1", "ad0", "k.1", "u0.4", "ad1", "u1.3", "d0.5", "ad2",
    "ad3", "o.3", "ad4", "ad5", "ad6", "ad7", "u0.5", "oe", "dz.4", "u1.4", "dn0", "dn1", "dn2",
    "o.4", "dn3", "nf", "q.2", "v.1", "dz.5", "gs", "u1.5", "k.2", "o.5", "q.3", "q.4", "v.2",
    "k.3", "q.5", "v.3", "k.4", "v.4", "k.5", "v.5",
)


def unit_shape(u):
    return SHAPE.get(u, (16, 1024))


def backward_kernel(*refs):
    f_qkv, f_out, f_up, f_down, h_qkv, h_context, h_lse, h_middle, h_second, h_act, h_slope, h_grad = (
        refs[:12]
    )
    h_gain, h_tokens, h_cot, lengths = refs[12:16]
    o_output, o_tokens, o_gqkv, o_gout, o_gup, o_gdown, o_gain = refs[16:23]
    refs = refs[23:]
    nu = len(UNITS)
    got1, got2, got3, res = (dict(zip(UNITS, refs[i * nu : (i + 1) * nu])) for i in range(4))
    refs = refs[4 * nu :]
    m_d, g_u0, g_u1, g_o, g_q, g_k, g_v, stage_a, stage_b, got0_d, got0_u = refs[:11]
    refs = refs[11:]
    cot, middle, dmid, rows_buf, wide_buf, part_buf, second, low, context, dcontext = refs[:10]
    gains, gain_sum, gain_send, got_gain = refs[10:14]
    ssem, rsem, lsem, osem, rsems, wsems, psems, gs, gr, credit, credit_u = refs[14:]
    here = coords()
    z, y, x, c = here
    me = owner(*here)
    ypeer, xpeer, speer = device(z, 1 - y, x, c), device(z, y, 1 - x, c), device(z, y, x, 1 - c)
    twin = z_twins(z)
    pair_peer, twin_peer = device(twin[1], y, x, c), device(twin[2], y, x, c)
    peers = all_peers(*here)
    greet(peers)
    index = {u: i for i, u in enumerate(UNITS)}
    sent = {u: [] for u in UNITS}
    left = []
    every = slice(None)
    own = {"u0": g_u0, "u1": g_u1, "o": g_o, "q": g_q, "k": g_k, "v": g_v}
    staged = {
        "u0": (stage_a, 0, None),
        "u1": (stage_b, 0, None),
        "o": (stage_a, 0, "u0"),
        "q": (stage_a, 1024, "u0"),
        "k": (stage_b, 0, "u1"),
        "v": (stage_b, 1024, "u1"),
    }
    down_row = {"d0": 0, "dz": 64}

    def mine(u, k, yy, xx, lo, n):
        if u in down_row:
            return m_d.at[k, yy, xx, pl.ds(down_row[u] + lo, n)]
        return own[u].at[k, yy, xx, pl.ds(lo, n)]

    def first(u):
        if u in down_row:
            return got0_d.at[:, :, :, pl.ds(down_row[u], 64)]
        if u in ("u0", "u1"):
            return got0_u
        return got0_d.at[:, :, :, pl.ds("oqkv".index(u) * 32, 32)]

    def send(u, k, make, peer):
        def copy():
            src, dst = make()
            return remote(src, dst, ssem.at[index[u], k], rsem.at[index[u], k], peer)

        copy().start()
        sent[u].append(copy)

    def wait(u, k, ref):
        remote(ref, ref, ssem.at[index[u], k], rsem.at[index[u], k], speer).wait_recv()

    def add(dst, src):
        dst[...] = dst[...] + src[...]

    def own_down(u):
        src = h_grad.at[:, :, :, c, pl.ds(down_row[u], 64)]
        dst = m_d.at[:, :, :, pl.ds(down_row[u], 64)]
        return pltpu.make_async_copy(src, dst, lsem.at[7 if u == "d0" else 8])

    def stage0(u):
        if u in down_row:
            n = down_row[u]
            send(u, 0, lambda: (h_grad.at[:, :, :, 1 - c, pl.ds(n, 64)], first(u)), speer)
            own_down(u).start()
            return
        if u == "o":
            pl.semaphore_wait(credit, 2)
        if u == "u1":
            pl.semaphore_wait(credit_u, 1)
        buf, col, before = staged[u]
        send(u, 0, lambda: (buf.at[:, :, :, :, pl.ds(col, own[u].shape[4])], first(u)), speer)

    def put(u, t, lhs, rhs):
        buf, col, before = staged[u]
        if before and before not in left:
            sent[before].pop(0)().wait_send()
            left.append(before)
        far = slice(t.start + col, t.stop + col)
        for k in range(4):
            v = dot(lhs[:, k * 256 : (k + 1) * 256], rhs, 0, 0).astype(jnp.bfloat16)
            v = v.reshape(2, 2, 64, v.shape[1])
            for core in range(2):

                @pl.when(c == core)
                def _():
                    own[u][k, :, :, :, t] = v[:, :, core * 32 : core * 32 + 32]
                    buf[k, :, :, :, far] = v[:, :, 32 - core * 32 : 64 - core * 32]

    def stage1(u):
        h, n = unit_shape(u)
        got = first(u)
        if u in down_row:
            own_down(u).wait()
        wait(u, 0, got)
        if u == "dz":
            for j in (1, 3, 2, 0):
                for yy in range(2):
                    for xx in range(2):
                        add(mine(u, twin[j], yy, xx, 0, 64), got.at[twin[j], yy, xx])
                if j % 2:
                    send(
                        u,
                        5 + j // 2,
                        lambda j=j: (mine(u, twin[j], every, every, 0, 64), got1[u].at[j // 2]),
                        pair_peer,
                    )
            pl.semaphore_signal(credit, inc=1, device_id=speer, device_id_type=MESH)
            return
        for far in (True, False):
            xx, yy = (1 - x, 1 - y) if far else (x, y)

            @pl.loop(0, NZ)
            def _(k):
                for j in range(2):
                    add(mine(u, k, j, xx, 0, h), got.at[k, j, xx, pl.ds(0, h)])
                    add(mine(u, k, yy, j, h, h), got.at[k, yy, j, pl.ds(h, h)])

            if far:
                send(u, 1, lambda: (mine(u, every, every, 1 - x, 0, h), got1[u].at[0]), xpeer)
                send(u, 2, lambda: (mine(u, every, 1 - y, every, h, h), got1[u].at[1]), ypeer)
        if u in ("d0", "u0"):
            done = credit if u == "d0" else credit_u
            pl.semaphore_signal(done, inc=1, device_id=speer, device_id_type=MESH)

    def stage2(u):
        h, n = unit_shape(u)
        if u == "dz":
            wait(u, 6, got1[u].at[1])
            for yy in range(2):
                for xx in range(2):
                    add(mine(u, twin[2], yy, xx, 0, 64), got1[u].at[1, yy, xx])
            send(u, 7, lambda: (mine(u, twin[2], every, every, 0, 64), got1[u].at[2]), twin_peer)
            return
        wait(u, 1, got1[u].at[0])
        wait(u, 2, got1[u].at[1])
        for far in (True, False):
            xx, yy = (1 - x, 1 - y) if far else (x, y)

            @pl.loop(0, NZ)
            def _(k):
                add(mine(u, k, yy, x, 0, h), got1[u].at[0, k, yy])
                add(mine(u, k, y, xx, h, h), got1[u].at[1, k, xx])

            if far:
                send(u, 3, lambda: (mine(u, every, 1 - y, x, 0, h), got2[u].at[0]), ypeer)
                send(u, 4, lambda: (mine(u, every, y, 1 - x, h, h), got2[u].at[1]), xpeer)

    def stage3(u):
        h, n = unit_shape(u)
        if u == "dz":
            wait(u, 5, got1[u].at[0])
            wait(u, 7, got1[u].at[2])
            for xx in (1 - x, x):
                for yy in range(2):
                    at = mine(u, z, yy, xx, 0, 64)
                    total = at[...].astype(jnp.float32)
                    for j in (0, 2):
                        total = total + got1[u][j, yy, xx].astype(jnp.float32)
                    at[...] = total.astype(jnp.bfloat16)
                if xx is not x:
                    send(u, 1, lambda: (mine(u, z, every, 1 - x, 0, 64), got2[u]), xpeer)
            return
        wait(u, 3, got2[u].at[0])
        wait(u, 4, got2[u].at[1])

        @pl.loop(0, NZ)
        def _(k):
            add(mine(u, k, y, x, 0, h), got2[u].at[0, k])
            add(mine(u, k, y, x, h, h), got2[u].at[1, k])

        for j in (3, 1):

            def make(j=j):
                return mine(u, twin[j], y, x, 0, 2 * h), got3[u].at[j // 2]

            send(u, 5 + j // 2, make, pair_peer)

    def stage4(u):
        h, n = unit_shape(u)
        if u == "dz":
            wait(u, 1, got2[u])
            for yy in (1 - y, y):
                add(mine(u, z, yy, x, 0, 64), got2[u].at[yy])
                if yy is not y:
                    send(u, 3, lambda: (mine(u, z, 1 - y, x, 0, 64), got3[u]), ypeer)
            return
        wait(u, 6, got3[u].at[1])
        add(mine(u, twin[2], y, x, 0, 2 * h), got3[u].at[1])
        send(u, 7, lambda: (mine(u, twin[2], y, x, 0, 2 * h), got3[u].at[2]), twin_peer)

    finals = []

    def stage5(u):
        h, n = unit_shape(u)
        total = mine(u, z, y, x, 0, 2 * h)[...].astype(jnp.float32)
        if u == "dz":
            wait(u, 3, got3[u])
            total = total + got3[u][...].astype(jnp.float32)
        else:
            wait(u, 5, got3[u].at[0])
            wait(u, 7, got3[u].at[2])
            total = total + got3[u][0].astype(jnp.float32) + got3[u][2].astype(jnp.float32)
        res[u][...] = total
        result(u).start()
        finals.append(u)

    def result(u):
        dst = {
            "d0": o_gdown.at[pl.ds(0, 64)],
            "dz": o_gdown.at[pl.ds(64, 64)],
            "u0": o_gup.at[:, pl.ds(0, 2048)],
            "u1": o_gup.at[:, pl.ds(2048, 2048)],
            "o": o_gout,
            "q": o_gqkv.at[:, pl.ds(0, 1024)],
            "k": o_gqkv.at[:, pl.ds(1024, 1024)],
            "v": o_gqkv.at[:, pl.ds(2048, 1024)],
        }[u]
        return pltpu.make_async_copy(res[u], dst, osem.at[index[u]])

    stages = (stage0, stage1, stage2, stage3, stage4, stage5)
    stage0("d0")
    stage0("dz")

    def local(src, dst, k):
        cp = pltpu.make_async_copy(src, dst, lsem.at[k])
        cp.start()
        return cp

    row_steps = [(f_down, i) for i in range(8)] + [(f_out, i) for i in range(2)]
    row_steps += [(f_down, i) for i in range(8)]
    wide_steps = [(f_up, 4096, i) for i in range(4)] + [(f_qkv, 3072, i) for i in range(4)]
    part_steps = [(h_slope, i) for i in range(8)] + [(h_act, i) for i in range(8)]

    def row_copy(j):
        ref, i = row_steps[j]
        return pltpu.make_async_copy(ref.at[pl.ds(i * 512, 512)], rows_buf.at[j % 2], rsems.at[j % 2])

    def wide_copy(j):
        ref, n, i = wide_steps[j]
        dst = wide_buf.at[j % 2, :, pl.ds(0, n)]
        return pltpu.make_async_copy(ref.at[pl.ds(i * 256, 256)], dst, wsems.at[j % 2])

    def part_copy(j):
        ref, i = part_steps[j]
        return pltpu.make_async_copy(ref.at[:, pl.ds(i * 512, 512)], part_buf.at[j % 2], psems.at[j % 2])

    early = [local(h_cot, cot, 0), local(h_second, second, 2)]
    for copy in (row_copy, part_copy, wide_copy):
        copy(0).start()
        copy(1).start()
    early += [
        local(h_middle, middle, 1),
        local(h_gain, gains, 3),
        local(h_context, context, 4),
    ]

    def following(copy, steps, j):
        if j + 2 < len(steps):
            copy(j + 2).start()

    def run(order, work):
        for name in order:
            if "." in name:
                u, k = name.split(".")
                stages[int(k)](u)
            else:
                short = name.rstrip("0123456789")
                rest = name[len(short) :]
                work[short](*([int(rest)] if rest else []))

    def phase_one(dhid):
        def chunk(i):
            if i == 0:
                early[0].wait()
                early[1].wait()
            slot = i % 2
            s = slice(i * 512, (i + 1) * 512)
            row_copy(i).wait()
            part_copy(i).wait()
            grown = dot(cot[...], rows_buf[slot], 1, 1) * part_buf[slot].astype(jnp.float32)
            dhid[:, s] = grown.astype(jnp.bfloat16)
            following(row_copy, row_steps, i)
            following(part_copy, part_steps, i)
            t = slice((i % 4) * 512, (i % 4 + 1) * 512)
            put("u0" if i < 4 else "u1", t, second, dhid[:, s])

        def grad_second(i):
            wide_copy(i).wait()
            s = slice(i * 256, (i + 1) * 256)
            dmid[:, s] = dot(dhid[...], wide_buf[i % 2], 1, 1)
            following(wide_copy, wide_steps, i)

        def norm_back_two():
            for cp in early[2:]:
                cp.wait()
            gain_sum[...] = jnp.zeros_like(gain_sum)

            def step(r):
                v, dn = middle[r, :], dmid[r, :]
                sc = scale_of(v)
                gain_sum[1:2, :] += jnp.sum(dn * v * sc, axis=0, keepdims=True)
                scaled = dn * gains[1:2, :]
                inner = jnp.mean(scaled * v, axis=-1, keepdims=True)
                total = cot[r, :].astype(jnp.float32) + (sc * scaled - v * (sc * sc * sc) * inner)
                dmid[r, :] = total
                low[r, :] = total.astype(jnp.bfloat16)

            rows_loop(step)

        run(NEAR, {"c": chunk, "ds": grad_second, "nb": norm_back_two})

    f32, bf = jnp.float32, jnp.bfloat16
    pl.run_scoped(phase_one, pltpu.VMEM((512, 4096), bf))

    def phase_two(qkv, dqkv, bias, lse, dk_sum, dv_sum):
        load_qkv = local(h_qkv, qkv, 1)
        load_lse = local(h_lse, lse, 3)
        load_tokens = local(h_tokens, second, 2)
        late = {}

        def grad_out(i):
            s = slice(i * 512, (i + 1) * 512)
            put("o", s, context, low[:, s])

        def grad_context(i):
            j = 8 + i
            row_copy(j).wait()
            s = slice(i * 512, (i + 1) * 512)
            dcontext[:, s] = dot(low[...], rows_buf[j % 2], 1, 1).astype(bf)
            following(row_copy, row_steps, j)

        def attend_back(pair):
            if pair == 0:
                load_qkv.wait()
                load_lse.wait()
                write_bias(lengths, bias)
            lane = lax.broadcasted_iota(jnp.int32, (1, 128), 1)
            lower = lane < HD
            col = pair * 128
            scale = 1.0 / math.sqrt(HD)
            for r0 in (256, 0):
                limit = r0 + 256
                q = qkv[r0:limit, col : col + 128]
                do = dcontext[r0:limit, col : col + 128]
                k = qkv[0:limit, 1024 + col : 1152 + col]
                v = qkv[0:limit, 2048 + col : 2176 + col]
                parts, dk, dv = [], None, None
                for h in range(2):
                    keep_lane = lower if h == 0 else ~lower
                    qh = jnp.where(keep_lane, q, jnp.zeros_like(q))
                    dh = jnp.where(keep_lane, do, jnp.zeros_like(do))
                    sums = jnp.where(lane == pair * 2 + h, lse[r0:limit, :], 0.0)
                    sums = jnp.sum(sums, axis=1, keepdims=True)
                    prob = jnp.exp2(dot(qh, k, 1, 1) * SCALE2 + bias[r0:limit, 0:limit] - sums)
                    scaled = prob * dot(dh, v, 1, 1)
                    inner = jnp.sum(scaled, axis=1, keepdims=True)
                    dlogit = (scaled - prob * inner).astype(bf)
                    parts.append(dot(dlogit, k, 1, 0))
                    dk_h = dot(dlogit, qh, 0, 0)
                    dv_h = dot(prob.astype(bf), dh, 0, 0)
                    dk = dk_h if dk is None else dk + dk_h
                    dv = dv_h if dv is None else dv + dv_h
                dqkv[r0:limit, col : col + 128] = (
                    jnp.where(lower, parts[0], parts[1]) * scale
                ).astype(bf)
                if limit == 512:
                    dk_sum[...] = dk
                    dv_sum[...] = dv
                else:
                    dk_sum[0:limit] += dk
                    dv_sum[0:limit] += dv
            dqkv[:, 1024 + col : 1152 + col] = (dk_sum[...] * scale).astype(bf)
            dqkv[:, 2048 + col : 2176 + col] = dv_sum[...].astype(bf)

        def renorm():
            load_tokens.wait()

            def step(r):
                v = second[r, :].astype(f32)
                context[r, :] = (v * scale_of(v) * gains[0:1, :]).astype(bf)

            rows_loop(step)

        def grad_qkv(j, i):
            s = slice(i * 512, (i + 1) * 512)
            t = slice(j * 1024 + i * 512, j * 1024 + (i + 1) * 512)
            put("qkv"[j], s, context, dqkv[:, t])

        def add_down(i):
            j = 10 + i
            row_copy(j).wait()
            part_copy(8 + i).wait()
            middle[...] = middle[...] + dot(part_buf[i % 2], rows_buf[j % 2], 1, 0)
            following(row_copy, row_steps, j)
            following(part_copy, part_steps, 8 + i)

        def out_end():
            rows_loop(lambda r: dcontext.__setitem__((r, every), middle[r, :].astype(bf)))
            late["out"] = local(dcontext, o_output, 5)

        def grad_normed(i):
            j = 4 + i
            wide_copy(j).wait()
            s = slice(i * 256, (i + 1) * 256)
            middle[:, s] = dot(dqkv[...], wide_buf[j % 2, :, 0:3072], 1, 1)
            following(wide_copy, wide_steps, j)

        def norm_final():
            def step(r):
                v, dn = second[r, :].astype(f32), middle[r, :]
                sc = scale_of(v)
                gain_sum[0:1, :] += jnp.sum(dn * v * sc, axis=0, keepdims=True)
                scaled = dn * gains[0:1, :]
                inner = jnp.mean(scaled * v, axis=-1, keepdims=True)
                total = dmid[r, :] + (sc * scaled - v * (sc * sc * sc) * inner)
                low[r, :] = total.astype(bf)

            rows_loop(step)
            late["tokens"] = local(low, o_tokens, 0)

        gain_copies = []

        def gain_start():
            for b in range(8):
                gain_send[b] = gain_sum[:, b * 128 : (b + 1) * 128]
            for j, peer in enumerate(peers):
                block = (peer[0] * 4 + peer[1]) // 4
                cp = remote(gain_send.at[block], got_gain.at[me], gs.at[j], gr.at[j], peer)
                cp.start()
                gain_copies.append(cp)
            got_gain[me] = gain_send[me // 4]

        F = functools.partial
        run(
            LATE,
            {
                "go": grad_out,
                "dc": grad_context,
                "a": attend_back,
                "rn": renorm,
                "gq": F(grad_qkv, 0),
                "gk": F(grad_qkv, 1),
                "gv": F(grad_qkv, 2),
                "ad": add_down,
                "oe": out_end,
                "dn": grad_normed,
                "nf": norm_final,
                "gs": gain_start,
            },
        )
        for cp in gain_copies:
            cp.wait()
        total = got_gain[0]
        for j in range(1, 32):
            total = total + got_gain[j]
        o_gain[...] = total
        for cp in late.values():
            cp.wait()

    pl.run_scoped(
        phase_two,
        pltpu.VMEM((512, 3072), bf),
        pltpu.VMEM((512, 3072), bf),
        pltpu.VMEM((512, 512), f32),
        pltpu.VMEM((512, 128), f32),
        pltpu.VMEM((512, 128), f32),
        pltpu.VMEM((512, 128), f32),
    )
    for u in UNITS:
        for copy in sent[u]:
            copy().wait_send()
    for u in finals:
        result(u).wait()


def backward(whole, saved, tokens, cotangent, lengths):
    gains, qkv, context, lse, middle, second, active, slope, grad_down = saved
    grad_down = grad_down.reshape(4, 2, 2, 2, 128, 1024)
    hbm = pl.BlockSpec(memory_space=pl.ANY)
    vmem = pl.BlockSpec(memory_space=pltpu.VMEM)
    smem = pl.BlockSpec(memory_space=pltpu.SMEM)
    bf, f32, dma = jnp.bfloat16, jnp.float32, pltpu.SemaphoreType.DMA
    per = {u: unit_shape(u) for u in UNITS}
    got1 = [(2, 4, 2, h, n) if u != "dz" else (3, 2, 2, 64, n) for u, (h, n) in per.items()]
    got2 = [(2, 4, h, n) if u != "dz" else (2, 64, n) for u, (h, n) in per.items()]
    got3 = [(3, 2 * h, n) if u != "dz" else (64, n) for u, (h, n) in per.items()]
    scratch = (
        [(v, bf) for v in got1 + got2 + got3]
        + [((2 * h, n), f32) for h, n in per.values()]
        + [
            ((4, 2, 2, 128, 1024), bf),
            ((4, 2, 2, 32, 2048), bf),
            ((4, 2, 2, 32, 2048), bf),
            ((4, 2, 2, 32, 1024), bf),
            ((4, 2, 2, 32, 1024), bf),
            ((4, 2, 2, 32, 1024), bf),
            ((4, 2, 2, 32, 1024), bf),
            ((4, 2, 2, 32, 2048), bf),
            ((4, 2, 2, 32, 2048), bf),
            ((4, 2, 2, 128, 1024), bf),
            ((4, 2, 2, 32, 2048), bf),
            ((512, 1024), bf),
            ((512, 1024), f32),
            ((512, 1024), f32),
            ((2, 512, 1024), bf),
            ((2, 256, 4096), bf),
            ((2, 512, 512), bf),
            ((512, 1024), bf),
            ((512, 1024), bf),
            ((512, 1024), bf),
            ((512, 1024), bf),
            ((8, 1024), f32),
            ((8, 1024), f32),
            ((8, 8, 128), f32),
            ((32, 8, 128), f32),
        ]
    )
    outs = [
        ((512, 1024), bf),
        ((512, 1024), bf),
        ((32, 3072), f32),
        ((32, 1024), f32),
        ((32, 4096), f32),
        ((128, 1024), f32),
        ((8, 128), f32),
    ]
    nu = len(UNITS)
    return pl.pallas_call(
        backward_kernel,
        out_shape=[jax.ShapeDtypeStruct(*o) for o in outs],
        in_specs=[hbm] * 15 + [smem],
        out_specs=[hbm] * 6 + [vmem],
        scratch_shapes=[pltpu.VMEM(*v) for v in scratch]
        + [
            dma((nu, 8)),
            dma((nu, 8)),
            dma((9,)),
            dma((nu,)),
            dma((2,)),
            dma((2,)),
            dma((2,)),
            dma((31,)),
            dma((31,)),
            pltpu.SemaphoreType.REGULAR,
            pltpu.SemaphoreType.REGULAR,
        ],
        compiler_params=pltpu.CompilerParams(
            collective_id=1, has_side_effects=True, vmem_limit_bytes=63 << 20
        ),
    )(
        *whole, qkv, context, lse, middle, second, active, slope, grad_down, gains, tokens, cotangent, lengths
    )


def project_input(inputs, w_qkv, gain):
    normed, scale_one = normalize(inputs, gain)
    normed_low = normed.astype(jnp.bfloat16)
    mixed = jnp.dot(normed_low, w_qkv, preferred_element_type=jnp.float32).astype(jnp.bfloat16)
    split = mixed.reshape(inputs.shape[0], 3, H, HD)
    return (normed_low, scale_one, split[:, 0], split[:, 1], split[:, 2])


def feed_inputs(inputs, context, w_out, w_up, gain):
    middle = inputs + jnp.dot(context, w_out, preferred_element_type=jnp.float32)
    second, scale_two = normalize(middle, gain)
    second_low = second.astype(jnp.bfloat16)
    hidden = jnp.dot(second_low, w_up, preferred_element_type=jnp.float32)
    active = jax.nn.gelu(hidden, approximate=True).astype(jnp.bfloat16)
    return (middle, scale_two, second_low, hidden, active)


def layer(tokens, lengths, w_qkv, w_out, w_up, w_down, gain_attn, gain_mlp, cotangent, low_type):
    total_rows = tokens.shape[0]
    ends = jnp.cumsum(lengths[0])
    places = jnp.arange(total_rows, dtype=jnp.int32)
    segment = jnp.sum((places[:, None] >= ends[None, :]).astype(jnp.int32), axis=1)
    inputs = tokens.astype(jnp.float32)
    gain_attn, gain_mlp = gain_attn.astype(jnp.float32), gain_mlp.astype(jnp.float32)
    normed_low, scale_one, queries, keys_all, values_all = project_input(inputs, w_qkv, gain_attn)
    context_full, log_sums = attend_forward(queries, keys_all, values_all, segment)
    context = context_full.reshape(total_rows, H * HD).astype(jnp.bfloat16)
    middle, scale_two, second_low, hidden, active = feed_inputs(
        inputs, context, w_out, w_up, gain_mlp
    )
    output = (middle + jnp.dot(active, w_down, preferred_element_type=jnp.float32)).astype(
        jnp.bfloat16
    )
    grad_down = jnp.einsum("rf,rd->fd", active, cotangent, preferred_element_type=low_type)
    grad_active = jnp.einsum("rd,fd->rf", cotangent, w_down, preferred_element_type=jnp.float32)
    unused, gelu_pull = jax.vjp(lambda values: jax.nn.gelu(values, approximate=True), hidden)
    grad_hidden = gelu_pull(grad_active)[0].astype(jnp.bfloat16)
    grad_up = jnp.einsum("rd,rf->df", second_low, grad_hidden, preferred_element_type=low_type)
    grad_second = jnp.einsum("rf,df->rd", grad_hidden, w_up, preferred_element_type=jnp.float32)
    grad_mid_norm, grad_gain_m = norm_back(grad_second, middle, scale_two, gain_mlp)
    grad_middle = cotangent.astype(jnp.float32) + grad_mid_norm
    grad_mid_low = grad_middle.astype(jnp.bfloat16)
    grad_out = jnp.einsum("rc,rd->cd", context, grad_mid_low, preferred_element_type=low_type)
    grad_context = jnp.einsum("rd,cd->rc", grad_mid_low, w_out, preferred_element_type=jnp.float32)
    grad_context = grad_context.astype(jnp.bfloat16).reshape(total_rows, H, HD)
    grad_queries, grad_keys, grad_values = attend_backward(
        queries, keys_all, values_all, segment, log_sums, grad_context
    )
    grad_mixed = (
        jnp.stack([grad_queries, grad_keys, grad_values], axis=1)
        .reshape(total_rows, 3 * H * HD)
        .astype(jnp.bfloat16)
    )
    grad_qkv = jnp.einsum("rd,re->de", normed_low, grad_mixed, preferred_element_type=low_type)
    grad_normed = jnp.einsum("re,de->rd", grad_mixed, w_qkv, preferred_element_type=jnp.float32)
    grad_in_norm, grad_gain_a = norm_back(grad_normed, inputs, scale_one, gain_attn)
    grad_tokens = (grad_middle + grad_in_norm).astype(jnp.bfloat16)
    return (output, grad_tokens, grad_qkv, grad_out, grad_up, grad_down, grad_gain_a, grad_gain_m)


def shards_any(tokens, lengths, w_qkv, w_out, w_up, w_down, gain_attn, gain_mlp, cotangent):
    whole = gather_any(w_qkv, w_out, w_up, w_down, gain_attn, gain_mlp)
    out = layer(tokens, lengths, *whole, cotangent, jnp.float32)
    return out[:2] + sum_any(*out[2:])


def keep_kernel(*refs):
    n = (len(refs) - 2) // 3
    gets, puts = refs[-2:]
    into = [pltpu.make_async_copy(refs[i], refs[2 * n + i], gets.at[i]) for i in range(n)]
    back = [pltpu.make_async_copy(refs[2 * n + i], refs[n + i], puts.at[i]) for i in range(n)]
    for cp in into:
        cp.start()
    for i in range(n):
        into[i].wait()
        back[i].start()
    for cp in back:
        cp.wait()


def keep(arrays):
    hbm = pl.BlockSpec(memory_space=pl.ANY)
    return pl.pallas_call(
        keep_kernel,
        out_shape=[jax.ShapeDtypeStruct(a.shape, a.dtype) for a in arrays],
        in_specs=[hbm] * len(arrays),
        out_specs=[hbm] * len(arrays),
        scratch_shapes=[pltpu.VMEM(a.shape, a.dtype) for a in arrays]
        + [pltpu.SemaphoreType.DMA((len(arrays),))] * 2,
    )(*arrays)


def shards(tokens, lengths, w_qkv, w_out, w_up, w_down, gain_attn, gain_mlp, cotangent):
    me = lax.axis_index("dp") * 4 + lax.axis_index("fsdp")
    lanes = lax.rem(me, 4) * 32
    pair = jnp.stack([gain_attn, gain_mlp]).astype(jnp.float32)
    spot = lax.dynamic_update_slice(jnp.zeros((8, 128), jnp.float32), pair, (0, lanes))
    whole, saved = forward((w_qkv, w_out, w_up, w_down), spot, lengths, tokens, cotangent)
    output, grad_tokens, g_qkv, g_out, g_up, g_down, g_gain = backward(
        whole, saved, tokens, cotangent, lengths
    )
    own = lax.dynamic_slice(g_gain, (0, lanes), (2, 32))
    kept = keep((output, grad_tokens, g_qkv, g_out, g_up, g_down))
    return (*kept, own[0], own[1])


def solution(mesh):
    rows, flat = P(AXES, None), P(AXES)
    known = dict(mesh.shape) == {"dp": 8, "fsdp": 4}
    return jax.shard_map(
        shards if known else shards_any,
        mesh=mesh,
        in_specs=(rows, rows, rows, rows, rows, rows, flat, flat, rows),
        out_specs=(rows, rows, rows, rows, rows, rows, flat, flat),
        check_vma=False,
    )
```

```python
import functools
import math

import jax
import jax.numpy as jnp
from jax import lax
from jax.experimental import pallas as pl
from jax.experimental.pallas import tpu as pltpu
from jax.sharding import PartitionSpec as P

H = 16
HD = 64
MESH = pl.DeviceIdType.MESH
AXES = ("dp", "fsdp")


epsilon = 1e-05


def normalize(values, gain):
    scale_row = lax.rsqrt(jnp.mean(values * values, axis=-1, keepdims=True) + epsilon)
    return (values * scale_row * gain, scale_row)


def norm_back(grad_normed, values, scale_row, gain):
    scaled = grad_normed * gain
    grad_gain = jnp.sum(grad_normed * values * scale_row, axis=0)
    cubed = scale_row * scale_row * scale_row
    grad_values = scale_row * scaled - values * cubed * jnp.mean(
        scaled * values, axis=-1, keepdims=True
    )
    return (grad_values, grad_gain)


def block_logits(query_block, key_rows, segment):
    block_rows = query_block.shape[0]
    key_limit = key_rows.shape[0]
    raw = jnp.einsum("qhd,khd->hqk", query_block, key_rows, preferred_element_type=jnp.float32)
    query_place = jnp.arange(block_rows, dtype=jnp.int32)
    key_place = jnp.arange(key_limit, dtype=jnp.int32)
    allowed = (segment[:, None] == segment[None, :]) & (query_place[:, None] >= key_place[None, :])
    return jnp.where(allowed[None], raw * (1.0 / math.sqrt(HD)), -1e30)


def attend_forward(queries, keys_all, values_all, segment):
    logits = block_logits(queries, keys_all, segment)
    peak = jnp.max(logits, axis=-1, keepdims=True)
    raised = jnp.exp(logits - peak)
    totals = jnp.sum(raised, axis=-1, keepdims=True)
    attn_prob = (raised / totals).astype(jnp.bfloat16)
    contexts = jnp.einsum("hqk,khd->qhd", attn_prob, values_all, preferred_element_type=jnp.float32)
    log_sums = (peak + jnp.log(totals))[:, :, 0]
    return (contexts, log_sums)


def attend_backward(queries, keys_all, values_all, segment, log_sums, grad_context):
    logits = block_logits(queries, keys_all, segment)
    attn_prob = jnp.exp(logits - log_sums[:, :, None])
    rounded = attn_prob.astype(jnp.bfloat16)
    grad_prob = jnp.einsum(
        "qhd,khd->hqk", grad_context, values_all, preferred_element_type=jnp.float32
    )
    inner = jnp.sum(attn_prob * grad_prob, axis=-1, keepdims=True)
    grad_logit = (1.0 / math.sqrt(HD) * attn_prob * (grad_prob - inner)).astype(jnp.bfloat16)
    grad_queries = jnp.einsum(
        "hqk,khd->qhd", grad_logit, keys_all, preferred_element_type=jnp.float32
    )
    grad_keys = jnp.einsum("hqk,qhd->khd", grad_logit, queries, preferred_element_type=jnp.float32)
    grad_values = jnp.einsum(
        "hqk,qhd->khd", rounded, grad_context, preferred_element_type=jnp.float32
    )
    return (grad_queries, grad_keys, grad_values)


def gather_any(*weights):
    return tuple(lax.all_gather(w, AXES, axis=0, tiled=True) for w in weights)


def sum_any(*grads):
    return tuple(lax.psum_scatter(g, AXES, scatter_dimension=0, tiled=True) for g in grads)


NZ = 4


def coords():
    a, b = lax.axis_index("dp"), lax.axis_index("fsdp")
    return a // 2, a % 2, b // 2, b % 2


def device(z, y, x, c):
    return (z * 2 + y, x * 2 + c)


def owner(z, y, x, c):
    return ((z * 2 + y) * 2 + x) * 2 + c


def all_peers(z, y, x, c):
    peers = []
    for d in range(NZ):
        for m in range(2):
            for l in range(2):
                for s in range(2):
                    if d + m + l + s:
                        peers.append(
                            device(
                                lax.rem(z + d, NZ),
                                1 - y if m else y,
                                1 - x if l else x,
                                1 - c if s else c,
                            )
                        )
    return peers


def greet(peers):
    sem = pltpu.get_barrier_semaphore()
    for peer in peers:
        pl.semaphore_signal(sem, inc=1, device_id=peer, device_id_type=MESH)
    pl.semaphore_wait(sem, len(peers))


def remote(src, dst, send_sem, recv_sem, peer):
    return pltpu.make_async_remote_copy(
        src_ref=src, dst_ref=dst, send_sem=send_sem, recv_sem=recv_sem,
        device_id=peer, device_id_type=MESH,
    )


FORWARD = 512
SHARDS = ((32, 3072), (32, 1024), (32, 4096), (128, 1024), (8, 128))
PARTS = (
    (0, 0, 32, 0, 1280, "21yx"),
    (0, 0, 32, 1280, 1280, "21xy"),
    (0, 0, 32, 2560, 512, "xy21"),
    (1, 0, 16, 0, 1024, "21yx"),
    (1, 16, 16, 0, 1024, "21xy"),
    (2, 0, 32, 0, 896, "21yx"),
    (2, 0, 32, 896, 768, "21xy"),
    (2, 0, 32, 1664, 384, "xy21"),
    (2, 0, 32, 2048, 768, "21yx"),
    (2, 0, 32, 2816, 896, "21xy"),
    (2, 0, 32, 3712, 384, "yx21"),
    (3, 0, 48, 0, 1024, "21yx"),
    (3, 48, 48, 0, 1024, "21xy"),
    (3, 96, 32, 0, 1024, "yx21"),
    (4, 0, 8, 0, 128, "21yx"),
)
GROUPS = ((14, 0, 1, 2), (3, 4), (5, 6, 7), (8, 9, 10), (11, 12, 13))
STEPS = 4


def z_twins(z):
    return (z, z + 1 - 2 * lax.rem(z, 2), lax.rem(z + 2, NZ), NZ - 1 - z)


def moved(rel, dim):
    e, m, l = rel
    return {"1": (e ^ 1, m, l), "2": (e ^ 2, m, l), "y": (e, 1 - m, l), "x": (e, m, 1 - l)}[dim]


def routes(stages):
    hold, arrivals, slot = [(0, 0, 0)], [], {}
    for s, dim in enumerate(stages):
        new = []
        for rel in hold:
            slot[rel, s] = len(arrivals)
            arrivals.append((moved(rel, dim), s))
            new.append(arrivals[-1][0])
        hold = hold + new
    return arrivals, slot


class Gather:
    def __init__(self, ins, outs, sems, here):
        self.ins, self.outs, (self.ssem, self.rsem) = ins, outs, sems
        z, y, x, c = here
        self.core = c
        self.zfrom = z_twins(z)
        self.ys, self.xs = (y, 1 - y), (x, 1 - x)
        self.peer = {"1": device(self.zfrom[1], y, x, c), "2": device(self.zfrom[2], y, x, c)}
        self.peer["y"] = device(z, 1 - y, x, c)
        self.peer["x"] = device(z, y, 1 - x, c)
        self.other = device(z, y, x, 1 - c)
        self.plan = [routes(p[5]) for p in PARTS]
        self.sent = []

    def place(self, part, rel, core):
        w, r0, nr, c0, nc, stages = PARTS[part]
        o = owner(self.zfrom[rel[0]], self.ys[rel[1]], self.xs[rel[2]], core)
        n = SHARDS[w][0]
        return self.outs[w].at[pl.ds(pl.multiple_of(o * n + r0, math.gcd(n, r0 or n, 16)), nr), pl.ds(c0, nc)]

    def send(self, part, rel, k, peer, own):
        w, r0, nr, c0, nc, stages = PARTS[part]
        dst = self.place(part, rel, self.core)
        src = self.ins[w].at[pl.ds(r0, nr), pl.ds(c0, nc)] if own else dst
        cp = remote(src, dst, self.ssem.at[part, k], self.rsem.at[part, k], peer)
        cp.start()
        self.sent.append(cp)

    def wait(self, part, rel, core, k):
        ref = self.place(part, rel, core)
        remote(ref, ref, self.ssem.at[part, k], self.rsem.at[part, k], self.other).wait_recv()

    def forward(self, part, rel, s, i):
        stages, slot = PARTS[part][5], self.plan[part][1]
        for t in range(s + 1, STEPS):
            self.send(part, rel, slot[rel, t], self.peer[stages[t]], s < 0)
        self.send(part, rel, 15 + i, self.other, s < 0)

    def start(self, group):
        for part in group:
            self.forward(part, (0, 0, 0), -1, 0)

    def arrive(self, group, s):
        ks = [[k for k, a in enumerate(self.plan[p][0]) if a[1] == s] for p in group]
        steps = []
        for j in range(max(map(len, ks))):
            steps.append([(p, k[j]) for p, k in zip(group, ks) if j < len(k)])

        def one(step):
            for part, k in step:
                rel = self.plan[part][0][k][0]
                self.wait(part, rel, self.core, k)
                self.forward(part, rel, s, 1 + k)

        return [functools.partial(one, step) for step in steps]

    def halves(self, group):
        for part in group:
            for i, rel in enumerate([(0, 0, 0)] + [a[0] for a in self.plan[part][0]]):
                self.wait(part, rel, 1 - self.core, 15 + i)


def dot(a, b, ca, cb):
    return lax.dot_general(
        a, b, (((ca,), (cb,)), ((), ())), preferred_element_type=jnp.float32
    )


def scale_of(values):
    return lax.rsqrt(jnp.mean(values * values, axis=-1, keepdims=True) + epsilon)


def rows_loop(step):
    @pl.loop(0, 8)
    def _(i):
        step(pl.ds(pl.multiple_of(i * 64, 64), 64))


LOG2E = math.log2(math.e)
SCALE2 = LOG2E / math.sqrt(HD)


def write_bias(lengths, bias):
    ends, total = [], jnp.int32(0)
    for j in range(lengths.shape[1]):
        total = total + lengths[0, j]
        ends.append(total)
    key = lax.broadcasted_iota(jnp.int32, (1, 512), 1)
    seg_key = sum((key >= e).astype(jnp.int32) for e in ends)

    @pl.loop(0, 8)
    def _(i):
        query = lax.broadcasted_iota(jnp.int32, (64, 1), 0) + i * 64
        seg_query = sum((query >= e).astype(jnp.int32) for e in ends)
        ok = (seg_query == seg_key) & (query >= key)
        bias[pl.ds(pl.multiple_of(i * 64, 64), 64), :] = jnp.where(ok, 0.0, -1e30)


def attend_pair(pair, qkv, bias, context, lse):
    lane = lax.broadcasted_iota(jnp.int32, (1, 128), 1)
    low = lane < HD
    col = pl.multiple_of(pair * 128, 128)
    q = qkv[:, pl.ds(col, 128)]
    k = qkv[:, pl.ds(1024 + col, 128)]
    v = qkv[:, pl.ds(2048 + col, 128)]
    parts, sums = [], lse[...]
    for h in range(2):
        qh = jnp.where(low if h == 0 else ~low, q, jnp.zeros_like(q))
        logits = dot(qh, k, 1, 1) * SCALE2 + bias[...]
        peak = jnp.max(logits, axis=1, keepdims=True)
        raised = jnp.exp2(logits - peak)
        total = jnp.sum(raised, axis=1, keepdims=True)
        parts.append(dot(raised.astype(jnp.bfloat16), v, 1, 0) * (1.0 / total))
        sums = jnp.where(lane == pair * 2 + h, peak + jnp.log2(total), sums)
    context[:, pl.ds(col, 128)] = jnp.where(low, parts[0], parts[1]).astype(jnp.bfloat16)
    lse[...] = sums


GELU_A = math.sqrt(2.0 / math.pi)


def forward_kernel(*refs):
    ins, gain_in, lengths, tokens, cotangent = refs[:4], *refs[4:8]
    outs = refs[8:12]
    o_gain, o_qkv, o_context, o_lse, o_middle, o_second, o_active, o_slope, o_grad = refs[12:21]
    w_qkv, w_out, w_up, normed, qkv, bias, context, lse, middle, second = refs[21:31]
    hid, act, slope, grad, grad_in, gains, gain_row = refs[31:38]
    lsem, wsem, hsem, gsem, gssem, grsem, ssem, rsem = refs[38:]
    here = coords()
    me = owner(*here)
    g = Gather((*ins, gain_in), (*outs, gains), (ssem, rsem), here)
    greet([*g.peer.values(), g.other])
    g.start(GROUPS[0])
    for w in range(4):
        n = SHARDS[w][0]
        cp = pltpu.make_async_copy(
            ins[w], outs[w].at[pl.ds(pl.multiple_of(me * n, n), n)], lsem.at[w]
        )
        cp.start()
    own = [
        pltpu.make_async_copy(
            ins[w],
            outs[w].at[pl.ds(pl.multiple_of(me * SHARDS[w][0], SHARDS[w][0]), SHARDS[w][0])],
            lsem.at[w],
        )
        for w in range(4)
    ]
    gains[pl.ds(pl.multiple_of(me * 8, 8), 8), :] = gain_in[...]
    write_bias(lengths, bias)
    saves = []

    def save(src, dst, k):
        cp = pltpu.make_async_copy(src, dst, lsem.at[k])
        cp.start()
        saves.append(cp)

    def gain_rows():
        for b in range(8):
            total = gains[32 * b : 32 * b + 8, :]
            for j in range(1, 4):
                total = total + gains[32 * b + 8 * j : 32 * b + 8 * j + 8, :]
            gain_row[:, b * 128 : (b + 1) * 128] = total
        save(gain_row, o_gain, 4)

    def norm_one():
        def step(r):
            v = tokens[r, :].astype(jnp.float32)
            normed[r, :] = (v * scale_of(v) * gain_row[0:1, :]).astype(jnp.bfloat16)

        rows_loop(step)

    def load(group, w, dst, n, blocks):
        width = SHARDS[w][1] // n
        g.halves(GROUPS[group])
        if 0 in blocks:
            own[w].wait()
        for i in blocks:
            s = pl.ds(i * width, width)
            pltpu.make_async_copy(outs[w].at[:, s], dst.at[:, s], wsem.at[w, i]).start()

    def loaded(w, dst, n, i):
        s = pl.ds(i * (SHARDS[w][1] // n), SHARDS[w][1] // n)
        pltpu.make_async_copy(outs[w].at[:, s], dst.at[:, s], wsem.at[w, i]).wait()

    def project(i):
        loaded(0, w_qkv, 6, i)
        s = slice(i * 512, (i + 1) * 512)
        qkv[:, s] = dot(normed[...], w_qkv[:, s], 1, 0).astype(jnp.bfloat16)

    def attend(i):
        attend_pair(i, qkv, bias, context, lse)

    def attended():
        save(qkv, o_qkv, 5)
        save(context, o_context, 6)
        save(lse, o_lse, 7)

    def add_out(i):
        loaded(1, w_out, 2, i)
        s = slice(i * 512, (i + 1) * 512)
        middle[:, s] = tokens[:, s].astype(jnp.float32) + dot(context[...], w_out[:, s], 1, 0)

    def norm_two():
        save(middle, o_middle, 8)

        def step(r):
            v = middle[r, :]
            second[r, :] = (v * scale_of(v) * gain_row[1:2, :]).astype(jnp.bfloat16)

        rows_loop(step)
        save(second, o_second, 9)

    hid_copies = []
    core = here[3]

    def feed(i):
        loaded(2, w_up, 8, i)
        s = slice(i * 512, (i + 1) * 512)
        slot = i % 2
        if i >= 2:
            for cp in hid_copies[i - 2]:
                cp.wait()
        hid[...] = dot(second[...], w_up[:, s], 1, 0)

        def step(r):
            v = hid[r, :]
            sq = v * v
            t = jnp.tanh(GELU_A * (v + 0.044715 * v * sq))
            half = 0.5 * (1.0 + t)
            act[slot, r, :] = (v * half).astype(jnp.bfloat16)
            rise = half + 0.5 * v * (1.0 - t * t) * (GELU_A * (1.0 + 3 * 0.044715 * sq))
            slope[slot, r, :] = rise.astype(jnp.bfloat16)

        rows_loop(step)
        pair = [
            pltpu.make_async_copy(act.at[slot], o_active.at[:, s], hsem.at[slot]),
            pltpu.make_async_copy(slope.at[slot], o_slope.at[:, s], hsem.at[2 + slot]),
        ]
        for cp in pair:
            cp.start()
        hid_copies.append(pair)

    def feed_grad(i):
        slot = i % 2
        s = slice(i * 512, (i + 1) * 512)
        grad[i] = (
            dot(act[slot], cotangent[...], 0, 0).astype(jnp.bfloat16).reshape(2, 2, 128, 1024)
        )
        share(i).start()

    def share(i):
        return remote(grad.at[i, :, 1 - core], grad_in.at[i], gssem.at[i], grsem.at[i], g.other)

    def grad_out(i):
        return pltpu.make_async_copy(grad.at[i, :, core], o_grad.at[pl.ds(2 * i, 2)], gsem.at[i])

    def sum_grad(i):
        share(i).wait_recv()
        for chip in range(2):
            at = grad.at[i, chip, core]
            at[...] = at[...] + grad_in[i, chip]
        grad_out(i).start()

    events = []
    for t in range(1, STEPS + len(GROUPS)):
        if t < len(GROUPS):
            events += [functools.partial(g.start, GROUPS[t])]
        for s in reversed(range(STEPS)):
            if 0 <= t - s - 1 < len(GROUPS):
                events += g.arrive(GROUPS[t - s - 1], s)
                if s == STEPS - 1:
                    events.append("whole%d" % (t - s - 1))
    F = functools.partial
    work = {
        0: [gain_rows, norm_one]
        + [F(project, i) for i in range(6)] + [F(attend, i) for i in range(8)] + [attended],
        1: [F(add_out, i) for i in range(2)] + [norm_two],
        2: [F(f, i) for i in range(4) for f in (feed, feed_grad)] + [F(sum_grad, 0)],
        3: [
            F(f, j)
            for i in range(4, 8)
            for f, j in ((feed, i), (feed_grad, i), (sum_grad, i - 3))
        ]
        + [F(sum_grad, i) for i in (5, 6, 7)],
    }
    ready, since = [], 0
    n_load = {
        0: (0, w_qkv, 6, range(6)),
        1: (1, w_out, 2, range(2)),
        2: (2, w_up, 8, range(4)),
        3: (2, w_up, 8, range(4, 8)),
    }
    lse[...] = jnp.zeros_like(lse)
    for e in events:
        if isinstance(e, str):
            w = int(e[5:])
            if w in n_load:
                ready.append(F(load, w, *n_load[w]))
                ready += work[w]
            continue
        e()
        since += 1
        if ready and since >= EVERY:
            ready.pop(0)()
            since = 0
    for step in ready:
        step()
    g.halves(GROUPS[-1])
    own[3].wait()
    for cp in hid_copies[-2] + hid_copies[-1] + saves:
        cp.wait()
    for i in range(8):
        share(i).wait_send()
        grad_out(i).wait()
    for cp in g.sent:
        cp.wait_send()


EVERY = 1


def forward(weights, gains, lengths, tokens, cotangent):
    hbm = pl.BlockSpec(memory_space=pl.ANY)
    vmem = pl.BlockSpec(memory_space=pltpu.VMEM)
    smem = pl.BlockSpec(memory_space=pltpu.SMEM)
    bf, f32 = jnp.bfloat16, jnp.float32
    saved = [
        ((8, 1024), f32),
        ((512, 3072), bf),
        ((512, 1024), bf),
        ((512, 128), f32),
        ((512, 1024), f32),
        ((512, 1024), bf),
        ((512, 4096), bf),
        ((512, 4096), bf),
        ((16, 128, 1024), bf),
    ]
    scratch = [
        ((1024, 3072), bf),
        ((1024, 1024), bf),
        ((1024, 4096), bf),
        ((512, 1024), bf),
        ((512, 3072), bf),
        ((512, 512), f32),
        ((512, 1024), bf),
        ((512, 128), f32),
        ((512, 1024), f32),
        ((512, 1024), bf),
        ((512, 512), f32),
        ((2, 512, 512), bf),
        ((2, 512, 512), bf),
        ((8, 2, 2, 128, 1024), bf),
        ((8, 2, 128, 1024), bf),
        ((256, 128), f32),
        ((8, 1024), f32),
    ]
    dma = pltpu.SemaphoreType.DMA
    out = pl.pallas_call(
        forward_kernel,
        out_shape=[jax.ShapeDtypeStruct((w.shape[0] * 32, w.shape[1]), w.dtype) for w in weights]
        + [jax.ShapeDtypeStruct(*s) for s in saved],
        in_specs=[vmem] * 5 + [smem, vmem, vmem],
        out_specs=[hbm] * 13,
        scratch_shapes=[pltpu.VMEM(*s) for s in scratch]
        + [
            dma((10,)),
            dma((3, 8)),
            dma((4,)),
            dma((8,)),
            dma((8,)),
            dma((8,)),
            dma((len(PARTS), 31)),
            dma((len(PARTS), 31)),
        ],
        compiler_params=pltpu.CompilerParams(
            collective_id=0, has_side_effects=True, vmem_limit_bytes=60 << 20
        ),
    )(*weights, gains, lengths, tokens, cotangent)
    return out[:4], out[4:]


UNITS = ("dz", "d0", "u0", "u1", "o", "q", "k", "v")
SHAPE = {"dz": (32, 1024), "d0": (32, 1024), "u0": (16, 2048), "u1": (16, 2048)}
NEAR = (
    "d0.1", "dz.1", "c0", "c1", "c2", "c3", "u0.0", "c4", "c5", "d0.2", "c6", "u0.1", "c7", "u1.0",
    "ds0", "ds1", "d0.3", "ds2", "dz.2", "ds3", "u1.1", "nb",
)
LATE = (
    "go0", "go1", "o.0", "d0.4", "dc0", "dc1", "a0", "o.1", "u0.2", "a1", "a2", "a3", "a4", "u1.2",
    "a5", "a6", "o.2", "dz.3", "a7", "rn", "gq0", "gq1", "q.0", "u0.3", "d0.5", "gk0", "gk1", "k.0",
    "gv0", "gv1", "v.0", "ad0", "q.1", "u1.3", "ad1", "k.1", "o.3", "u0.4", "ad2", "ad3", "ad4",
    "dz.4", "ad5", "u1.4", "ad6", "o.4", "ad7", "q.2", "v.1", "oe", "dn0", "u0.5", "dn1", "dz.5",
    "dn2", "dn3", "k.2", "u1.5", "nf", "g.0", "q.3", "o.5", "g.1", "v.2", "q.4", "k.3", "g.2",
    "v.3", "g.3", "q.5", "k.4", "v.4", "g.4", "k.5", "v.5", "g.5",
)


def unit_shape(u):
    return SHAPE.get(u, (16, 1024))


def backward_kernel(*refs):
    f_qkv, f_out, f_up, f_down, h_qkv, h_context, h_lse, h_middle, h_second, h_act, h_slope, h_grad = (
        refs[:12]
    )
    h_gain, h_tokens, h_cot, lengths = refs[12:16]
    o_output, o_tokens, o_gqkv, o_gout, o_gup, o_gdown, o_gain = refs[16:23]
    refs = refs[23:]
    nu = len(UNITS)
    got1, got2, got3, res = (dict(zip(UNITS, refs[i * nu : (i + 1) * nu])) for i in range(4))
    refs = refs[4 * nu :]
    m_d, g_u0, g_u1, g_o, g_q, g_k, g_v, stage_a, stage_b, got0_d, got0_u = refs[:11]
    refs = refs[11:]
    cot, middle, dmid, rows_buf, wide_buf, part_buf, second, low, context, dcontext = refs[:10]
    gains, gain_sum, got_gain = refs[10:13]
    ssem, rsem, lsem, osem, rsems, wsems, psems, gs, gr, credit_u = refs[13:]
    here = coords()
    z, y, x, c = here
    me = owner(*here)
    ypeer, xpeer, speer = device(z, 1 - y, x, c), device(z, y, 1 - x, c), device(z, y, x, 1 - c)
    twin = z_twins(z)
    pair_peer, twin_peer = device(twin[1], y, x, c), device(twin[2], y, x, c)
    greet([xpeer, ypeer, speer, pair_peer, twin_peer])
    index = {u: i for i, u in enumerate(UNITS)}
    sent = {u: [] for u in UNITS}
    left = []
    every = slice(None)
    own = {"u0": g_u0, "u1": g_u1, "o": g_o, "q": g_q, "k": g_k, "v": g_v}
    staged = {
        "u0": (stage_a, 0, None),
        "u1": (stage_b, 0, None),
        "o": (stage_a, 0, "u0"),
        "q": (stage_a, 1024, "u0"),
        "k": (stage_b, 0, "u1"),
        "v": (stage_b, 1024, "u1"),
    }
    down_row = {"d0": 0, "dz": 64}

    def mine(u, k, yy, xx, lo, n):
        if u in down_row:
            return m_d.at[k, yy, xx, pl.ds(down_row[u] + lo, n)]
        return own[u].at[k, yy, xx, pl.ds(lo, n)]

    def first(u):
        if u in ("u0", "u1"):
            return got0_u
        return got0_d.at[:, :, :, pl.ds("oqkv".index(u) * 32, 32)]

    def send(u, k, make, peer):
        def copy():
            src, dst = make()
            return remote(src, dst, ssem.at[index[u], k], rsem.at[index[u], k], peer)

        copy().start()
        sent[u].append(copy)

    def wait(u, k, ref):
        remote(ref, ref, ssem.at[index[u], k], rsem.at[index[u], k], speer).wait_recv()

    def add(dst, src):
        dst[...] = dst[...] + src[...]

    def own_down(u):
        src = h_grad.at[:, :, :, pl.ds(down_row[u], 64)]
        dst = m_d.at[:, :, :, pl.ds(down_row[u], 64)]
        return pltpu.make_async_copy(src, dst, lsem.at[7 if u == "d0" else 8])

    def stage0(u):
        if u in down_row:
            own_down(u).start()
            return
        if u == "u1":
            pl.semaphore_wait(credit_u, 1)
        buf, col, before = staged[u]
        send(u, 0, lambda: (buf.at[:, :, :, :, pl.ds(col, own[u].shape[4])], first(u)), speer)

    def put(u, t, lhs, rhs):
        buf, col, before = staged[u]
        if before and before not in left:
            sent[before].pop(0)().wait_send()
            left.append(before)
        far = slice(t.start + col, t.stop + col)
        for k in range(4):
            v = dot(lhs[:, k * 256 : (k + 1) * 256], rhs, 0, 0).astype(jnp.bfloat16)
            v = v.reshape(2, 2, 64, v.shape[1])
            for core in range(2):

                @pl.when(c == core)
                def _():
                    own[u][k, :, :, :, t] = v[:, :, core * 32 : core * 32 + 32]
                    buf[k, :, :, :, far] = v[:, :, 32 - core * 32 : 64 - core * 32]

    def stage1(u):
        h, n = unit_shape(u)
        if u in down_row:
            own_down(u).wait()
        if u == "dz":
            for j in (1, 3):
                send(
                    u,
                    5 + j // 2,
                    lambda j=j: (mine(u, twin[j], every, every, 0, 64), got1[u].at[j // 2]),
                    pair_peer,
                )
            return

        def send_far():
            send(u, 1, lambda: (mine(u, every, every, 1 - x, 0, h), got1[u].at[0]), xpeer)
            send(u, 2, lambda: (mine(u, every, 1 - y, every, h, h), got1[u].at[1]), ypeer)

        if u == "d0":
            send_far()
            return
        got = first(u)
        wait(u, 0, got)
        for far in (True, False):
            xx, yy = (1 - x, 1 - y) if far else (x, y)

            @pl.loop(0, NZ)
            def _(k):
                for j in range(2):
                    add(mine(u, k, j, xx, 0, h), got.at[k, j, xx, pl.ds(0, h)])
                    add(mine(u, k, yy, j, h, h), got.at[k, yy, j, pl.ds(h, h)])

            if far:
                send_far()
        if u == "u0":
            pl.semaphore_signal(credit_u, inc=1, device_id=speer, device_id_type=MESH)

    def stage2(u):
        h, n = unit_shape(u)
        if u == "dz":
            wait(u, 6, got1[u].at[1])
            for yy in range(2):
                for xx in range(2):
                    add(mine(u, twin[2], yy, xx, 0, 64), got1[u].at[1, yy, xx])
            send(u, 7, lambda: (mine(u, twin[2], every, every, 0, 64), got1[u].at[2]), twin_peer)
            return
        wait(u, 1, got1[u].at[0])
        wait(u, 2, got1[u].at[1])
        for far in (True, False):
            xx, yy = (1 - x, 1 - y) if far else (x, y)

            @pl.loop(0, NZ)
            def _(k):
                add(mine(u, k, yy, x, 0, h), got1[u].at[0, k, yy])
                add(mine(u, k, y, xx, h, h), got1[u].at[1, k, xx])

            if far:
                send(u, 3, lambda: (mine(u, every, 1 - y, x, 0, h), got2[u].at[0]), ypeer)
                send(u, 4, lambda: (mine(u, every, y, 1 - x, h, h), got2[u].at[1]), xpeer)

    def stage3(u):
        h, n = unit_shape(u)
        if u == "dz":
            wait(u, 5, got1[u].at[0])
            wait(u, 7, got1[u].at[2])
            for xx in (1 - x, x):
                for yy in range(2):
                    at = mine(u, z, yy, xx, 0, 64)
                    total = at[...].astype(jnp.float32)
                    for j in (0, 2):
                        total = total + got1[u][j, yy, xx].astype(jnp.float32)
                    at[...] = total.astype(jnp.bfloat16)
                if xx is not x:
                    send(u, 1, lambda: (mine(u, z, every, 1 - x, 0, 64), got2[u]), xpeer)
            return
        wait(u, 3, got2[u].at[0])
        wait(u, 4, got2[u].at[1])

        @pl.loop(0, NZ)
        def _(k):
            add(mine(u, k, y, x, 0, h), got2[u].at[0, k])
            add(mine(u, k, y, x, h, h), got2[u].at[1, k])

        for j in (3, 1):

            def make(j=j):
                return mine(u, twin[j], y, x, 0, 2 * h), got3[u].at[j // 2]

            send(u, 5 + j // 2, make, pair_peer)

    def stage4(u):
        h, n = unit_shape(u)
        if u == "dz":
            wait(u, 1, got2[u])
            for yy in (1 - y, y):
                add(mine(u, z, yy, x, 0, 64), got2[u].at[yy])
                if yy is not y:
                    send(u, 3, lambda: (mine(u, z, 1 - y, x, 0, 64), got3[u]), ypeer)
            return
        wait(u, 6, got3[u].at[1])
        add(mine(u, twin[2], y, x, 0, 2 * h), got3[u].at[1])
        send(u, 7, lambda: (mine(u, twin[2], y, x, 0, 2 * h), got3[u].at[2]), twin_peer)

    finals = []

    def stage5(u):
        h, n = unit_shape(u)
        total = mine(u, z, y, x, 0, 2 * h)[...].astype(jnp.float32)
        if u == "dz":
            wait(u, 3, got3[u])
            total = total + got3[u][...].astype(jnp.float32)
        else:
            wait(u, 5, got3[u].at[0])
            wait(u, 7, got3[u].at[2])
            total = total + got3[u][0].astype(jnp.float32) + got3[u][2].astype(jnp.float32)
        res[u][...] = total
        result(u).start()
        finals.append(u)

    def result(u):
        dst = {
            "d0": o_gdown.at[pl.ds(0, 64)],
            "dz": o_gdown.at[pl.ds(64, 64)],
            "u0": o_gup.at[:, pl.ds(0, 2048)],
            "u1": o_gup.at[:, pl.ds(2048, 2048)],
            "o": o_gout,
            "q": o_gqkv.at[:, pl.ds(0, 1024)],
            "k": o_gqkv.at[:, pl.ds(1024, 1024)],
            "v": o_gqkv.at[:, pl.ds(2048, 1024)],
        }[u]
        return pltpu.make_async_copy(res[u], dst, osem.at[index[u]])

    stages = (stage0, stage1, stage2, stage3, stage4, stage5)
    stage0("d0")
    stage0("dz")

    def local(src, dst, k):
        cp = pltpu.make_async_copy(src, dst, lsem.at[k])
        cp.start()
        return cp

    row_steps = [(f_down, i) for i in range(8)] + [(f_out, i) for i in range(2)]
    row_steps += [(f_down, i) for i in range(8)]
    wide_steps = [(f_up, 4096, i) for i in range(4)] + [(f_qkv, 3072, i) for i in range(4)]
    part_steps = [(h_slope, i) for i in range(8)] + [(h_act, i) for i in range(8)]

    def row_copy(j):
        ref, i = row_steps[j]
        return pltpu.make_async_copy(ref.at[pl.ds(i * 512, 512)], rows_buf.at[j % 2], rsems.at[j % 2])

    def wide_copy(j):
        ref, n, i = wide_steps[j]
        dst = wide_buf.at[j % 2, :, pl.ds(0, n)]
        return pltpu.make_async_copy(ref.at[pl.ds(i * 256, 256)], dst, wsems.at[j % 2])

    def part_copy(j):
        ref, i = part_steps[j]
        return pltpu.make_async_copy(ref.at[:, pl.ds(i * 512, 512)], part_buf.at[j % 2], psems.at[j % 2])

    early = [local(h_cot, cot, 0), local(h_second, second, 2)]
    for copy in (row_copy, part_copy, wide_copy):
        copy(0).start()
        copy(1).start()
    early += [
        local(h_middle, middle, 1),
        local(h_gain, gains, 3),
        local(h_context, context, 4),
    ]

    def following(copy, steps, j):
        if j + 2 < len(steps):
            copy(j + 2).start()

    def run(order, work):
        for name in order:
            if "." in name:
                u, k = name.split(".")
                (work["gain"] if u == "g" else functools.partial(stages[int(k)], u))(
                    *([int(k)] if u == "g" else [])
                )
            else:
                short = name.rstrip("0123456789")
                rest = name[len(short) :]
                work[short](*([int(rest)] if rest else []))

    def phase_one(dhid):
        def chunk(i):
            if i == 0:
                early[0].wait()
                early[1].wait()
            slot = i % 2
            s = slice(i * 512, (i + 1) * 512)
            row_copy(i).wait()
            part_copy(i).wait()
            grown = dot(cot[...], rows_buf[slot], 1, 1) * part_buf[slot].astype(jnp.float32)
            dhid[:, s] = grown.astype(jnp.bfloat16)
            following(row_copy, row_steps, i)
            following(part_copy, part_steps, i)
            t = slice((i % 4) * 512, (i % 4 + 1) * 512)
            put("u0" if i < 4 else "u1", t, second, dhid[:, s])

        def grad_second(i):
            wide_copy(i).wait()
            s = slice(i * 256, (i + 1) * 256)
            dmid[:, s] = dot(dhid[...], wide_buf[i % 2], 1, 1)
            following(wide_copy, wide_steps, i)

        def norm_back_two():
            for cp in early[2:]:
                cp.wait()
            gain_sum[...] = jnp.zeros_like(gain_sum)

            def step(r):
                v, dn = middle[r, :], dmid[r, :]
                sc = scale_of(v)
                gain_sum[1:2, :] += jnp.sum(dn * v * sc, axis=0, keepdims=True)
                scaled = dn * gains[1:2, :]
                inner = jnp.mean(scaled * v, axis=-1, keepdims=True)
                total = cot[r, :].astype(jnp.float32) + (sc * scaled - v * (sc * sc * sc) * inner)
                dmid[r, :] = total
                low[r, :] = total.astype(jnp.bfloat16)

            rows_loop(step)

        run(NEAR, {"c": chunk, "ds": grad_second, "nb": norm_back_two})

    f32, bf = jnp.float32, jnp.bfloat16
    pl.run_scoped(phase_one, pltpu.VMEM((512, 4096), bf))

    def phase_two(qkv, dqkv, bias, lse, dk_sum, dv_sum):
        load_qkv = local(h_qkv, qkv, 1)
        load_lse = local(h_lse, lse, 3)
        load_tokens = local(h_tokens, second, 2)
        late = {}

        def grad_out(i):
            s = slice(i * 512, (i + 1) * 512)
            put("o", s, context, low[:, s])

        def grad_context(i):
            j = 8 + i
            row_copy(j).wait()
            s = slice(i * 512, (i + 1) * 512)
            dcontext[:, s] = dot(low[...], rows_buf[j % 2], 1, 1).astype(bf)
            following(row_copy, row_steps, j)

        def attend_back(pair):
            if pair == 0:
                load_qkv.wait()
                load_lse.wait()
                write_bias(lengths, bias)
            lane = lax.broadcasted_iota(jnp.int32, (1, 128), 1)
            lower = lane < HD
            col = pair * 128
            scale = 1.0 / math.sqrt(HD)
            for r0 in (256, 0):
                limit = r0 + 256
                q = qkv[r0:limit, col : col + 128]
                do = dcontext[r0:limit, col : col + 128]
                k = qkv[0:limit, 1024 + col : 1152 + col]
                v = qkv[0:limit, 2048 + col : 2176 + col]
                parts, dk, dv = [], None, None
                for h in range(2):
                    keep_lane = lower if h == 0 else ~lower
                    qh = jnp.where(keep_lane, q, jnp.zeros_like(q))
                    dh = jnp.where(keep_lane, do, jnp.zeros_like(do))
                    sums = jnp.where(lane == pair * 2 + h, lse[r0:limit, :], 0.0)
                    sums = jnp.sum(sums, axis=1, keepdims=True)
                    prob = jnp.exp2(dot(qh, k, 1, 1) * SCALE2 + bias[r0:limit, 0:limit] - sums)
                    scaled = prob * dot(dh, v, 1, 1)
                    inner = jnp.sum(scaled, axis=1, keepdims=True)
                    dlogit = (scaled - prob * inner).astype(bf)
                    parts.append(dot(dlogit, k, 1, 0))
                    dk_h = dot(dlogit, qh, 0, 0)
                    dv_h = dot(prob.astype(bf), dh, 0, 0)
                    dk = dk_h if dk is None else dk + dk_h
                    dv = dv_h if dv is None else dv + dv_h
                dqkv[r0:limit, col : col + 128] = (
                    jnp.where(lower, parts[0], parts[1]) * scale
                ).astype(bf)
                if limit == 512:
                    dk_sum[...] = dk
                    dv_sum[...] = dv
                else:
                    dk_sum[0:limit] += dk
                    dv_sum[0:limit] += dv
            dqkv[:, 1024 + col : 1152 + col] = (dk_sum[...] * scale).astype(bf)
            dqkv[:, 2048 + col : 2176 + col] = dv_sum[...].astype(bf)

        def renorm():
            load_tokens.wait()

            def step(r):
                v = second[r, :].astype(f32)
                context[r, :] = (v * scale_of(v) * gains[0:1, :]).astype(bf)

            rows_loop(step)

        def grad_qkv(j, i):
            s = slice(i * 512, (i + 1) * 512)
            t = slice(j * 1024 + i * 512, j * 1024 + (i + 1) * 512)
            put("qkv"[j], s, context, dqkv[:, t])

        def add_down(i):
            j = 10 + i
            row_copy(j).wait()
            part_copy(8 + i).wait()
            middle[...] = middle[...] + dot(part_buf[i % 2], rows_buf[j % 2], 1, 0)
            following(row_copy, row_steps, j)
            following(part_copy, part_steps, 8 + i)

        def out_end():
            rows_loop(lambda r: dcontext.__setitem__((r, every), middle[r, :].astype(bf)))
            late["out"] = local(dcontext, o_output, 5)

        def grad_normed(i):
            j = 4 + i
            wide_copy(j).wait()
            s = slice(i * 256, (i + 1) * 256)
            middle[:, s] = dot(dqkv[...], wide_buf[j % 2, :, 0:3072], 1, 1)
            following(wide_copy, wide_steps, j)

        def norm_final():
            def step(r):
                v, dn = second[r, :].astype(f32), middle[r, :]
                sc = scale_of(v)
                gain_sum[0:1, :] += jnp.sum(dn * v * sc, axis=0, keepdims=True)
                scaled = dn * gains[0:1, :]
                inner = jnp.mean(scaled * v, axis=-1, keepdims=True)
                total = dmid[r, :] + (sc * scaled - v * (sc * sc * sc) * inner)
                low[r, :] = total.astype(bf)

            rows_loop(step)
            late["tokens"] = local(low, o_tokens, 0)

        partners = (speer, xpeer, ypeer, pair_peer, twin_peer)

        def gain_step(k):
            if k:
                exchange(k - 1).wait()
                gain_sum[...] = gain_sum[...] + got_gain[k - 1]
            if k < 5:
                exchange(k).start()
            else:
                block = pl.multiple_of(me // 4 * 128, 128)
                o_gain[...] = gain_sum[:, pl.ds(block, 128)]

        def exchange(k):
            return remote(gain_sum, got_gain.at[k], gs.at[k], gr.at[k], partners[k])

        F = functools.partial
        run(
            LATE,
            {
                "go": grad_out,
                "dc": grad_context,
                "a": attend_back,
                "rn": renorm,
                "gq": F(grad_qkv, 0),
                "gk": F(grad_qkv, 1),
                "gv": F(grad_qkv, 2),
                "ad": add_down,
                "oe": out_end,
                "dn": grad_normed,
                "nf": norm_final,
                "gain": gain_step,
            },
        )
        for cp in late.values():
            cp.wait()

    pl.run_scoped(
        phase_two,
        pltpu.VMEM((512, 3072), bf),
        pltpu.VMEM((512, 3072), bf),
        pltpu.VMEM((512, 512), f32),
        pltpu.VMEM((512, 128), f32),
        pltpu.VMEM((512, 128), f32),
        pltpu.VMEM((512, 128), f32),
    )
    for u in UNITS:
        for copy in sent[u]:
            copy().wait_send()
    for u in finals:
        result(u).wait()


def backward(whole, saved, tokens, cotangent, lengths):
    gains, qkv, context, lse, middle, second, active, slope, grad_down = saved
    grad_down = grad_down.reshape(4, 2, 2, 128, 1024)
    hbm = pl.BlockSpec(memory_space=pl.ANY)
    vmem = pl.BlockSpec(memory_space=pltpu.VMEM)
    smem = pl.BlockSpec(memory_space=pltpu.SMEM)
    bf, f32, dma = jnp.bfloat16, jnp.float32, pltpu.SemaphoreType.DMA
    per = {u: unit_shape(u) for u in UNITS}
    got1 = [(2, 4, 2, h, n) if u != "dz" else (3, 2, 2, 64, n) for u, (h, n) in per.items()]
    got2 = [(2, 4, h, n) if u != "dz" else (2, 64, n) for u, (h, n) in per.items()]
    got3 = [(3, 2 * h, n) if u != "dz" else (64, n) for u, (h, n) in per.items()]
    scratch = (
        [(v, bf) for v in got1 + got2 + got3]
        + [((2 * h, n), f32) for h, n in per.values()]
        + [
            ((4, 2, 2, 128, 1024), bf),
            ((4, 2, 2, 32, 2048), bf),
            ((4, 2, 2, 32, 2048), bf),
            ((4, 2, 2, 32, 1024), bf),
            ((4, 2, 2, 32, 1024), bf),
            ((4, 2, 2, 32, 1024), bf),
            ((4, 2, 2, 32, 1024), bf),
            ((4, 2, 2, 32, 2048), bf),
            ((4, 2, 2, 32, 2048), bf),
            ((4, 2, 2, 128, 1024), bf),
            ((4, 2, 2, 32, 2048), bf),
            ((512, 1024), bf),
            ((512, 1024), f32),
            ((512, 1024), f32),
            ((2, 512, 1024), bf),
            ((2, 256, 4096), bf),
            ((2, 512, 512), bf),
            ((512, 1024), bf),
            ((512, 1024), bf),
            ((512, 1024), bf),
            ((512, 1024), bf),
            ((8, 1024), f32),
            ((8, 1024), f32),
            ((5, 8, 1024), f32),
        ]
    )
    outs = [
        ((512, 1024), bf),
        ((512, 1024), bf),
        ((32, 3072), f32),
        ((32, 1024), f32),
        ((32, 4096), f32),
        ((128, 1024), f32),
        ((8, 128), f32),
    ]
    nu = len(UNITS)
    return pl.pallas_call(
        backward_kernel,
        out_shape=[jax.ShapeDtypeStruct(*o) for o in outs],
        in_specs=[hbm] * 15 + [smem],
        out_specs=[hbm] * 6 + [vmem],
        scratch_shapes=[pltpu.VMEM(*v) for v in scratch]
        + [
            dma((nu, 8)),
            dma((nu, 8)),
            dma((9,)),
            dma((nu,)),
            dma((2,)),
            dma((2,)),
            dma((2,)),
            dma((5,)),
            dma((5,)),
            pltpu.SemaphoreType.REGULAR,
        ],
        compiler_params=pltpu.CompilerParams(
            collective_id=1, has_side_effects=True, vmem_limit_bytes=63 << 20
        ),
    )(
        *whole, qkv, context, lse, middle, second, active, slope, grad_down, gains, tokens, cotangent, lengths
    )


def project_input(inputs, w_qkv, gain):
    normed, scale_one = normalize(inputs, gain)
    normed_low = normed.astype(jnp.bfloat16)
    mixed = jnp.dot(normed_low, w_qkv, preferred_element_type=jnp.float32).astype(jnp.bfloat16)
    split = mixed.reshape(inputs.shape[0], 3, H, HD)
    return (normed_low, scale_one, split[:, 0], split[:, 1], split[:, 2])


def feed_inputs(inputs, context, w_out, w_up, gain):
    middle = inputs + jnp.dot(context, w_out, preferred_element_type=jnp.float32)
    second, scale_two = normalize(middle, gain)
    second_low = second.astype(jnp.bfloat16)
    hidden = jnp.dot(second_low, w_up, preferred_element_type=jnp.float32)
    active = jax.nn.gelu(hidden, approximate=True).astype(jnp.bfloat16)
    return (middle, scale_two, second_low, hidden, active)


def layer(tokens, lengths, w_qkv, w_out, w_up, w_down, gain_attn, gain_mlp, cotangent, low_type):
    total_rows = tokens.shape[0]
    ends = jnp.cumsum(lengths[0])
    places = jnp.arange(total_rows, dtype=jnp.int32)
    segment = jnp.sum((places[:, None] >= ends[None, :]).astype(jnp.int32), axis=1)
    inputs = tokens.astype(jnp.float32)
    gain_attn, gain_mlp = gain_attn.astype(jnp.float32), gain_mlp.astype(jnp.float32)
    normed_low, scale_one, queries, keys_all, values_all = project_input(inputs, w_qkv, gain_attn)
    context_full, log_sums = attend_forward(queries, keys_all, values_all, segment)
    context = context_full.reshape(total_rows, H * HD).astype(jnp.bfloat16)
    middle, scale_two, second_low, hidden, active = feed_inputs(
        inputs, context, w_out, w_up, gain_mlp
    )
    output = (middle + jnp.dot(active, w_down, preferred_element_type=jnp.float32)).astype(
        jnp.bfloat16
    )
    grad_down = jnp.einsum("rf,rd->fd", active, cotangent, preferred_element_type=low_type)
    grad_active = jnp.einsum("rd,fd->rf", cotangent, w_down, preferred_element_type=jnp.float32)
    unused, gelu_pull = jax.vjp(lambda values: jax.nn.gelu(values, approximate=True), hidden)
    grad_hidden = gelu_pull(grad_active)[0].astype(jnp.bfloat16)
    grad_up = jnp.einsum("rd,rf->df", second_low, grad_hidden, preferred_element_type=low_type)
    grad_second = jnp.einsum("rf,df->rd", grad_hidden, w_up, preferred_element_type=jnp.float32)
    grad_mid_norm, grad_gain_m = norm_back(grad_second, middle, scale_two, gain_mlp)
    grad_middle = cotangent.astype(jnp.float32) + grad_mid_norm
    grad_mid_low = grad_middle.astype(jnp.bfloat16)
    grad_out = jnp.einsum("rc,rd->cd", context, grad_mid_low, preferred_element_type=low_type)
    grad_context = jnp.einsum("rd,cd->rc", grad_mid_low, w_out, preferred_element_type=jnp.float32)
    grad_context = grad_context.astype(jnp.bfloat16).reshape(total_rows, H, HD)
    grad_queries, grad_keys, grad_values = attend_backward(
        queries, keys_all, values_all, segment, log_sums, grad_context
    )
    grad_mixed = (
        jnp.stack([grad_queries, grad_keys, grad_values], axis=1)
        .reshape(total_rows, 3 * H * HD)
        .astype(jnp.bfloat16)
    )
    grad_qkv = jnp.einsum("rd,re->de", normed_low, grad_mixed, preferred_element_type=low_type)
    grad_normed = jnp.einsum("re,de->rd", grad_mixed, w_qkv, preferred_element_type=jnp.float32)
    grad_in_norm, grad_gain_a = norm_back(grad_normed, inputs, scale_one, gain_attn)
    grad_tokens = (grad_middle + grad_in_norm).astype(jnp.bfloat16)
    return (output, grad_tokens, grad_qkv, grad_out, grad_up, grad_down, grad_gain_a, grad_gain_m)


def shards_any(tokens, lengths, w_qkv, w_out, w_up, w_down, gain_attn, gain_mlp, cotangent):
    whole = gather_any(w_qkv, w_out, w_up, w_down, gain_attn, gain_mlp)
    out = layer(tokens, lengths, *whole, cotangent, jnp.float32)
    return out[:2] + sum_any(*out[2:])


def keep_kernel(*refs):
    n = (len(refs) - 2) // 3
    gets, puts = refs[-2:]
    into = [pltpu.make_async_copy(refs[i], refs[2 * n + i], gets.at[i]) for i in range(n)]
    back = [pltpu.make_async_copy(refs[2 * n + i], refs[n + i], puts.at[i]) for i in range(n)]
    for cp in into:
        cp.start()
    for i in range(n):
        into[i].wait()
        back[i].start()
    for cp in back:
        cp.wait()


def keep(arrays):
    hbm = pl.BlockSpec(memory_space=pl.ANY)
    return pl.pallas_call(
        keep_kernel,
        out_shape=[jax.ShapeDtypeStruct(a.shape, a.dtype) for a in arrays],
        in_specs=[hbm] * len(arrays),
        out_specs=[hbm] * len(arrays),
        scratch_shapes=[pltpu.VMEM(a.shape, a.dtype) for a in arrays]
        + [pltpu.SemaphoreType.DMA((len(arrays),))] * 2,
    )(*arrays)


def shards(tokens, lengths, w_qkv, w_out, w_up, w_down, gain_attn, gain_mlp, cotangent):
    me = lax.axis_index("dp") * 4 + lax.axis_index("fsdp")
    lanes = lax.rem(me, 4) * 32
    pair = jnp.stack([gain_attn, gain_mlp]).astype(jnp.float32)
    spot = lax.dynamic_update_slice(jnp.zeros((8, 128), jnp.float32), pair, (0, lanes))
    whole, saved = forward((w_qkv, w_out, w_up, w_down), spot, lengths, tokens, cotangent)
    output, grad_tokens, g_qkv, g_out, g_up, g_down, g_gain = backward(
        whole, saved, tokens, cotangent, lengths
    )
    own = lax.dynamic_slice(g_gain, (0, lanes), (2, 32))
    kept = keep((output, grad_tokens, g_qkv, g_out, g_up, g_down))
    return (*kept, own[0], own[1])


def solution(mesh):
    rows, flat = P(AXES, None), P(AXES)
    known = dict(mesh.shape) == {"dp": 8, "fsdp": 4}
    return jax.shard_map(
        shards if known else shards_any,
        mesh=mesh,
        in_specs=(rows, rows, rows, rows, rows, rows, flat, flat, rows),
        out_specs=(rows, rows, rows, rows, rows, rows, flat, flat),
        check_vma=False,
    )
```

```python
import functools
import math

import jax
import jax.numpy as jnp
from jax import lax
from jax.experimental import pallas as pl
from jax.experimental.pallas import tpu as pltpu
from jax.sharding import PartitionSpec as P

H = 16
HD = 64
MESH = pl.DeviceIdType.MESH
AXES = ("dp", "fsdp")


epsilon = 1e-05


def normalize(values, gain):
    scale_row = lax.rsqrt(jnp.mean(values * values, axis=-1, keepdims=True) + epsilon)
    return (values * scale_row * gain, scale_row)


def norm_back(grad_normed, values, scale_row, gain):
    scaled = grad_normed * gain
    grad_gain = jnp.sum(grad_normed * values * scale_row, axis=0)
    cubed = scale_row * scale_row * scale_row
    grad_values = scale_row * scaled - values * cubed * jnp.mean(
        scaled * values, axis=-1, keepdims=True
    )
    return (grad_values, grad_gain)


def block_logits(query_block, key_rows, segment):
    block_rows = query_block.shape[0]
    key_limit = key_rows.shape[0]
    raw = jnp.einsum("qhd,khd->hqk", query_block, key_rows, preferred_element_type=jnp.float32)
    query_place = jnp.arange(block_rows, dtype=jnp.int32)
    key_place = jnp.arange(key_limit, dtype=jnp.int32)
    allowed = (segment[:, None] == segment[None, :]) & (query_place[:, None] >= key_place[None, :])
    return jnp.where(allowed[None], raw * (1.0 / math.sqrt(HD)), -1e30)


def attend_forward(queries, keys_all, values_all, segment):
    logits = block_logits(queries, keys_all, segment)
    peak = jnp.max(logits, axis=-1, keepdims=True)
    raised = jnp.exp(logits - peak)
    totals = jnp.sum(raised, axis=-1, keepdims=True)
    attn_prob = (raised / totals).astype(jnp.bfloat16)
    contexts = jnp.einsum("hqk,khd->qhd", attn_prob, values_all, preferred_element_type=jnp.float32)
    log_sums = (peak + jnp.log(totals))[:, :, 0]
    return (contexts, log_sums)


def attend_backward(queries, keys_all, values_all, segment, log_sums, grad_context):
    logits = block_logits(queries, keys_all, segment)
    attn_prob = jnp.exp(logits - log_sums[:, :, None])
    rounded = attn_prob.astype(jnp.bfloat16)
    grad_prob = jnp.einsum(
        "qhd,khd->hqk", grad_context, values_all, preferred_element_type=jnp.float32
    )
    inner = jnp.sum(attn_prob * grad_prob, axis=-1, keepdims=True)
    grad_logit = (1.0 / math.sqrt(HD) * attn_prob * (grad_prob - inner)).astype(jnp.bfloat16)
    grad_queries = jnp.einsum(
        "hqk,khd->qhd", grad_logit, keys_all, preferred_element_type=jnp.float32
    )
    grad_keys = jnp.einsum("hqk,qhd->khd", grad_logit, queries, preferred_element_type=jnp.float32)
    grad_values = jnp.einsum(
        "hqk,qhd->khd", rounded, grad_context, preferred_element_type=jnp.float32
    )
    return (grad_queries, grad_keys, grad_values)


def gather_any(*weights):
    return tuple(lax.all_gather(w, AXES, axis=0, tiled=True) for w in weights)


def sum_any(*grads):
    return tuple(lax.psum_scatter(g, AXES, scatter_dimension=0, tiled=True) for g in grads)


NZ = 4


def coords():
    a, b = lax.axis_index("dp"), lax.axis_index("fsdp")
    return a // 2, a % 2, b // 2, b % 2


def device(z, y, x, c):
    return (z * 2 + y, x * 2 + c)


def owner(z, y, x, c):
    return ((z * 2 + y) * 2 + x) * 2 + c


def all_peers(z, y, x, c):
    peers = []
    for d in range(NZ):
        for m in range(2):
            for l in range(2):
                for s in range(2):
                    if d + m + l + s:
                        peers.append(
                            device(
                                lax.rem(z + d, NZ),
                                1 - y if m else y,
                                1 - x if l else x,
                                1 - c if s else c,
                            )
                        )
    return peers


def greet(peers):
    sem = pltpu.get_barrier_semaphore()
    for peer in peers:
        pl.semaphore_signal(sem, inc=1, device_id=peer, device_id_type=MESH)
    pl.semaphore_wait(sem, len(peers))


def remote(src, dst, send_sem, recv_sem, peer):
    return pltpu.make_async_remote_copy(
        src_ref=src, dst_ref=dst, send_sem=send_sem, recv_sem=recv_sem,
        device_id=peer, device_id_type=MESH,
    )


FORWARD = 512
SHARDS = ((32, 3072), (32, 1024), (32, 4096), (128, 1024), (8, 128))
PARTS = (
    (0, 0, 32, 0, 1280, "21yx"),
    (0, 0, 32, 1280, 1280, "21xy"),
    (0, 0, 32, 2560, 512, "xy21"),
    (1, 0, 16, 0, 1024, "21yx"),
    (1, 16, 16, 0, 1024, "21xy"),
    (2, 0, 32, 0, 896, "21yx"),
    (2, 0, 32, 896, 768, "21xy"),
    (2, 0, 32, 1664, 384, "xy21"),
    (2, 0, 32, 2048, 768, "21yx"),
    (2, 0, 32, 2816, 896, "21xy"),
    (2, 0, 32, 3712, 384, "yx21"),
    (3, 0, 48, 0, 1024, "21yx"),
    (3, 48, 48, 0, 1024, "21xy"),
    (3, 96, 32, 0, 1024, "yx21"),
    (4, 0, 8, 0, 128, "21yx"),
)
GROUPS = ((14, 0, 1, 2), (3, 4), (5, 6, 7), (8, 9, 10), (11, 12, 13))
STEPS = 4


def z_twins(z):
    return (z, z + 1 - 2 * lax.rem(z, 2), lax.rem(z + 2, NZ), NZ - 1 - z)


def moved(rel, dim):
    e, m, l = rel
    return {"1": (e ^ 1, m, l), "2": (e ^ 2, m, l), "y": (e, 1 - m, l), "x": (e, m, 1 - l)}[dim]


def routes(stages):
    hold, arrivals, slot = [(0, 0, 0)], [], {}
    for s, dim in enumerate(stages):
        new = []
        for rel in hold:
            slot[rel, s] = len(arrivals)
            arrivals.append((moved(rel, dim), s))
            new.append(arrivals[-1][0])
        hold = hold + new
    return arrivals, slot


class Gather:
    def __init__(self, ins, outs, sems, here):
        self.ins, self.outs, (self.ssem, self.rsem) = ins, outs, sems
        z, y, x, c = here
        self.core = c
        self.zfrom = z_twins(z)
        self.ys, self.xs = (y, 1 - y), (x, 1 - x)
        self.peer = {"1": device(self.zfrom[1], y, x, c), "2": device(self.zfrom[2], y, x, c)}
        self.peer["y"] = device(z, 1 - y, x, c)
        self.peer["x"] = device(z, y, 1 - x, c)
        self.other = device(z, y, x, 1 - c)
        self.plan = [routes(p[5]) for p in PARTS]
        self.sent = []

    def place(self, part, rel, core):
        w, r0, nr, c0, nc, stages = PARTS[part]
        o = owner(self.zfrom[rel[0]], self.ys[rel[1]], self.xs[rel[2]], core)
        n = SHARDS[w][0]
        return self.outs[w].at[pl.ds(pl.multiple_of(o * n + r0, math.gcd(n, r0 or n, 16)), nr), pl.ds(c0, nc)]

    def send(self, part, rel, k, peer, own):
        w, r0, nr, c0, nc, stages = PARTS[part]
        dst = self.place(part, rel, self.core)
        src = self.ins[w].at[pl.ds(r0, nr), pl.ds(c0, nc)] if own else dst
        cp = remote(src, dst, self.ssem.at[part, k], self.rsem.at[part, k], peer)
        cp.start()
        self.sent.append(cp)

    def wait(self, part, rel, core, k):
        ref = self.place(part, rel, core)
        remote(ref, ref, self.ssem.at[part, k], self.rsem.at[part, k], self.other).wait_recv()

    def forward(self, part, rel, s, i):
        stages, slot = PARTS[part][5], self.plan[part][1]
        for t in range(s + 1, STEPS):
            self.send(part, rel, slot[rel, t], self.peer[stages[t]], s < 0)
        self.send(part, rel, 15 + i, self.other, s < 0)

    def start(self, group):
        for part in group:
            self.forward(part, (0, 0, 0), -1, 0)

    def arrive(self, group, s):
        ks = [[k for k, a in enumerate(self.plan[p][0]) if a[1] == s] for p in group]
        steps = []
        for j in range(max(map(len, ks))):
            steps.append([(p, k[j]) for p, k in zip(group, ks) if j < len(k)])

        def one(step):
            for part, k in step:
                rel = self.plan[part][0][k][0]
                self.wait(part, rel, self.core, k)
                self.forward(part, rel, s, 1 + k)

        return [functools.partial(one, step) for step in steps]

    def halves(self, group):
        for part in group:
            for i, rel in enumerate([(0, 0, 0)] + [a[0] for a in self.plan[part][0]]):
                self.wait(part, rel, 1 - self.core, 15 + i)


def dot(a, b, ca, cb):
    return lax.dot_general(
        a, b, (((ca,), (cb,)), ((), ())), preferred_element_type=jnp.float32
    )


def scale_of(values):
    return lax.rsqrt(jnp.mean(values * values, axis=-1, keepdims=True) + epsilon)


def rows_loop(step):
    @pl.loop(0, 8)
    def _(i):
        step(pl.ds(pl.multiple_of(i * 64, 64), 64))


LOG2E = math.log2(math.e)
SCALE2 = LOG2E / math.sqrt(HD)


def write_bias(lengths, bias):
    ends, total = [], jnp.int32(0)
    for j in range(lengths.shape[1]):
        total = total + lengths[0, j]
        ends.append(total)
    key = lax.broadcasted_iota(jnp.int32, (1, 512), 1)
    seg_key = sum((key >= e).astype(jnp.int32) for e in ends)

    @pl.loop(0, 8)
    def _(i):
        query = lax.broadcasted_iota(jnp.int32, (64, 1), 0) + i * 64
        seg_query = sum((query >= e).astype(jnp.int32) for e in ends)
        ok = (seg_query == seg_key) & (query >= key)
        bias[pl.ds(pl.multiple_of(i * 64, 64), 64), :] = jnp.where(ok, 0.0, -1e30)


def attend_pair(pair, qkv, bias, context, lse):
    lane = lax.broadcasted_iota(jnp.int32, (1, 128), 1)
    low = lane < HD
    col = pl.multiple_of(pair * 128, 128)
    q = qkv[:, pl.ds(col, 128)]
    k = qkv[:, pl.ds(1024 + col, 128)]
    v = qkv[:, pl.ds(2048 + col, 128)]
    parts, sums = [], lse[...]
    for h in range(2):
        qh = jnp.where(low if h == 0 else ~low, q, jnp.zeros_like(q))
        logits = dot(qh, k, 1, 1) * SCALE2 + bias[...]
        peak = jnp.max(logits, axis=1, keepdims=True)
        raised = jnp.exp2(logits - peak)
        total = jnp.sum(raised, axis=1, keepdims=True)
        parts.append(dot(raised.astype(jnp.bfloat16), v, 1, 0) * (1.0 / total))
        sums = jnp.where(lane == pair * 2 + h, peak + jnp.log2(total), sums)
    context[:, pl.ds(col, 128)] = jnp.where(low, parts[0], parts[1]).astype(jnp.bfloat16)
    lse[...] = sums


GELU_A = math.sqrt(2.0 / math.pi)


def forward_kernel(*refs):
    ins, gain_in, lengths, tokens, cotangent = refs[:4], *refs[4:8]
    outs = refs[8:12]
    o_gain, o_qkv, o_context, o_lse, o_middle, o_second, o_active, o_slope, o_grad = refs[12:21]
    w_qkv, w_out, w_up, normed, qkv, bias, context, lse, middle, second = refs[21:31]
    hid, act, slope, grad, grad_in, gains, gain_row = refs[31:38]
    lsem, wsem, hsem, gsem, gssem, grsem, ssem, rsem = refs[38:]
    here = coords()
    me = owner(*here)
    g = Gather((*ins, gain_in), (*outs, gains), (ssem, rsem), here)
    greet([*g.peer.values(), g.other])
    g.start(GROUPS[0])
    for w in range(4):
        n = SHARDS[w][0]
        cp = pltpu.make_async_copy(
            ins[w], outs[w].at[pl.ds(pl.multiple_of(me * n, n), n)], lsem.at[w]
        )
        cp.start()
    own = [
        pltpu.make_async_copy(
            ins[w],
            outs[w].at[pl.ds(pl.multiple_of(me * SHARDS[w][0], SHARDS[w][0]), SHARDS[w][0])],
            lsem.at[w],
        )
        for w in range(4)
    ]
    gains[pl.ds(pl.multiple_of(me * 8, 8), 8), :] = gain_in[...]
    write_bias(lengths, bias)
    saves = []

    def save(src, dst, k):
        cp = pltpu.make_async_copy(src, dst, lsem.at[k])
        cp.start()
        saves.append(cp)

    def gain_rows():
        for b in range(8):
            total = gains[32 * b : 32 * b + 8, :]
            for j in range(1, 4):
                total = total + gains[32 * b + 8 * j : 32 * b + 8 * j + 8, :]
            gain_row[:, b * 128 : (b + 1) * 128] = total
        save(gain_row, o_gain, 4)

    def norm_one():
        def step(r):
            v = tokens[r, :].astype(jnp.float32)
            normed[r, :] = (v * scale_of(v) * gain_row[0:1, :]).astype(jnp.bfloat16)

        rows_loop(step)

    def load(group, w, dst, n, blocks):
        width = SHARDS[w][1] // n
        g.halves(GROUPS[group])
        if 0 in blocks:
            own[w].wait()
        for i in blocks:
            s = pl.ds(i * width, width)
            pltpu.make_async_copy(outs[w].at[:, s], dst.at[:, s], wsem.at[w, i]).start()

    def loaded(w, dst, n, i):
        s = pl.ds(i * (SHARDS[w][1] // n), SHARDS[w][1] // n)
        pltpu.make_async_copy(outs[w].at[:, s], dst.at[:, s], wsem.at[w, i]).wait()

    def project(i):
        loaded(0, w_qkv, 6, i)
        s = slice(i * 512, (i + 1) * 512)
        qkv[:, s] = dot(normed[...], w_qkv[:, s], 1, 0).astype(jnp.bfloat16)

    def attend(i):
        attend_pair(i, qkv, bias, context, lse)

    def attended():
        save(qkv, o_qkv, 5)
        save(context, o_context, 6)
        save(lse, o_lse, 7)

    def add_out(i):
        loaded(1, w_out, 2, i)
        s = slice(i * 512, (i + 1) * 512)
        middle[:, s] = tokens[:, s].astype(jnp.float32) + dot(context[...], w_out[:, s], 1, 0)

    def norm_two():
        save(middle, o_middle, 8)

        def step(r):
            v = middle[r, :]
            second[r, :] = (v * scale_of(v) * gain_row[1:2, :]).astype(jnp.bfloat16)

        rows_loop(step)
        save(second, o_second, 9)

    hid_copies = []
    core = here[3]

    def feed(i):
        loaded(2, w_up, 8, i)
        s = slice(i * 512, (i + 1) * 512)
        slot = i % 2
        if i >= 2:
            for cp in hid_copies[i - 2]:
                cp.wait()
        hid[...] = dot(second[...], w_up[:, s], 1, 0)

        def step(r):
            v = hid[r, :]
            sq = v * v
            t = jnp.tanh(GELU_A * (v + 0.044715 * v * sq))
            half = 0.5 * (1.0 + t)
            act[slot, r, :] = (v * half).astype(jnp.bfloat16)
            rise = half + 0.5 * v * (1.0 - t * t) * (GELU_A * (1.0 + 3 * 0.044715 * sq))
            slope[slot, r, :] = rise.astype(jnp.bfloat16)

        rows_loop(step)
        pair = [
            pltpu.make_async_copy(act.at[slot], o_active.at[:, s], hsem.at[slot]),
            pltpu.make_async_copy(slope.at[slot], o_slope.at[:, s], hsem.at[2 + slot]),
        ]
        for cp in pair:
            cp.start()
        hid_copies.append(pair)

    def feed_grad(i):
        slot = i % 2
        s = slice(i * 512, (i + 1) * 512)
        grad[i] = (
            dot(act[slot], cotangent[...], 0, 0).astype(jnp.bfloat16).reshape(2, 2, 128, 1024)
        )
        share(i).start()

    def share(i):
        return remote(grad.at[i, :, 1 - core], grad_in.at[i], gssem.at[i], grsem.at[i], g.other)

    def grad_out(i):
        return pltpu.make_async_copy(grad.at[i, :, core], o_grad.at[pl.ds(2 * i, 2)], gsem.at[i])

    def sum_grad(i):
        share(i).wait_recv()
        for chip in range(2):
            at = grad.at[i, chip, core]
            at[...] = at[...] + grad_in[i, chip]
        grad_out(i).start()

    events = []
    for t in range(1, STEPS + len(GROUPS)):
        if t < len(GROUPS):
            events += [functools.partial(g.start, GROUPS[t])]
        for s in reversed(range(STEPS)):
            if 0 <= t - s - 1 < len(GROUPS):
                events += g.arrive(GROUPS[t - s - 1], s)
                if s == STEPS - 1:
                    events.append("whole%d" % (t - s - 1))
    F = functools.partial
    work = {
        0: [gain_rows, norm_one]
        + [F(project, i) for i in range(6)] + [F(attend, i) for i in range(8)] + [attended],
        1: [F(add_out, i) for i in range(2)] + [norm_two],
        2: [F(f, i) for i in range(4) for f in (feed, feed_grad)] + [F(sum_grad, 0)],
        3: [
            F(f, j)
            for i in range(4, 8)
            for f, j in ((feed, i), (feed_grad, i), (sum_grad, i - 3))
        ]
        + [F(sum_grad, i) for i in (5, 6, 7)],
    }
    ready, since = [], 0
    n_load = {
        0: (0, w_qkv, 6, range(6)),
        1: (1, w_out, 2, range(2)),
        2: (2, w_up, 8, range(4)),
        3: (2, w_up, 8, range(4, 8)),
    }
    lse[...] = jnp.zeros_like(lse)
    for e in events:
        if isinstance(e, str):
            w = int(e[5:])
            if w in n_load:
                ready.append(F(load, w, *n_load[w]))
                ready += work[w]
            continue
        e()
        since += 1
        if ready and since >= EVERY:
            ready.pop(0)()
            since = 0
    for step in ready:
        step()
    g.halves(GROUPS[-1])
    own[3].wait()
    for cp in hid_copies[-2] + hid_copies[-1] + saves:
        cp.wait()
    for i in range(8):
        share(i).wait_send()
        grad_out(i).wait()
    for cp in g.sent:
        cp.wait_send()


EVERY = 1


def forward(weights, gains, lengths, tokens, cotangent):
    hbm = pl.BlockSpec(memory_space=pl.ANY)
    vmem = pl.BlockSpec(memory_space=pltpu.VMEM)
    smem = pl.BlockSpec(memory_space=pltpu.SMEM)
    bf, f32 = jnp.bfloat16, jnp.float32
    saved = [
        ((8, 1024), f32),
        ((512, 3072), bf),
        ((512, 1024), bf),
        ((512, 128), f32),
        ((512, 1024), f32),
        ((512, 1024), bf),
        ((512, 4096), bf),
        ((512, 4096), bf),
        ((16, 128, 1024), bf),
    ]
    scratch = [
        ((1024, 3072), bf),
        ((1024, 1024), bf),
        ((1024, 4096), bf),
        ((512, 1024), bf),
        ((512, 3072), bf),
        ((512, 512), f32),
        ((512, 1024), bf),
        ((512, 128), f32),
        ((512, 1024), f32),
        ((512, 1024), bf),
        ((512, 512), f32),
        ((2, 512, 512), bf),
        ((2, 512, 512), bf),
        ((8, 2, 2, 128, 1024), bf),
        ((8, 2, 128, 1024), bf),
        ((256, 128), f32),
        ((8, 1024), f32),
    ]
    dma = pltpu.SemaphoreType.DMA
    out = pl.pallas_call(
        forward_kernel,
        out_shape=[jax.ShapeDtypeStruct((w.shape[0] * 32, w.shape[1]), w.dtype) for w in weights]
        + [jax.ShapeDtypeStruct(*s) for s in saved],
        in_specs=[vmem] * 5 + [smem, vmem, vmem],
        out_specs=[hbm] * 13,
        scratch_shapes=[pltpu.VMEM(*s) for s in scratch]
        + [
            dma((10,)),
            dma((3, 8)),
            dma((4,)),
            dma((8,)),
            dma((8,)),
            dma((8,)),
            dma((len(PARTS), 31)),
            dma((len(PARTS), 31)),
        ],
        compiler_params=pltpu.CompilerParams(
            collective_id=0, has_side_effects=True, vmem_limit_bytes=60 << 20
        ),
    )(*weights, gains, lengths, tokens, cotangent)
    return out[:4], out[4:]


UNITS = ("dz", "d0", "u0", "u1", "o", "q", "k", "v")
SHAPE = {"dz": (32, 1024), "d0": (32, 1024), "u0": (16, 2048), "u1": (16, 2048)}
NEAR = (
    "d0.1", "dz.1", "c0", "c1", "c2", "c3", "u0.0", "c4", "c5", "d0.2", "c6", "u0.1", "c7", "u1.0",
    "ds0", "ds1", "d0.3", "ds2", "ds3", "u1.1", "dz.2", "nb",
)
LATE = (
    "go0", "go1", "o.0", "d0.4", "dc0", "dc1", "a0", "u0.2", "o.1", "a1", "a2", "a3", "a4", "u1.2",
    "a5", "a6", "a7", "u0.3", "rn", "dz.3", "gq0", "gq1", "q.0", "gk0", "gk1", "k.0", "o.2", "gv0",
    "gv1", "v.0", "d0.5", "ad0", "q.1", "u0.4", "k.1", "u1.3", "ad1", "ad2", "ad3", "ad4", "dz.4",
    "ad5", "ad6", "o.3", "u0.5", "ad7", "u1.4", "oe", "dn0", "dn1", "dn2", "q.2", "v.1", "o.4",
    "dn3", "dz.5", "nf", "g.0", "k.2", "u1.5", "q.3", "o.5", "g.1", "q.4", "v.2", "k.3", "g.2",
    "q.5", "v.3", "g.3", "k.4", "v.4", "g.4", "k.5", "v.5", "g.5",
)


def unit_shape(u):
    return SHAPE.get(u, (16, 1024))


def backward_kernel(*refs):
    f_qkv, f_out, f_up, f_down, h_qkv, h_context, h_lse, h_middle, h_second, h_act, h_slope, h_grad = (
        refs[:12]
    )
    h_gain, h_tokens, h_cot, lengths = refs[12:16]
    o_output, o_tokens, o_gqkv, o_gout, o_gup, o_gdown, o_gain = refs[16:23]
    refs = refs[23:]
    nu = len(UNITS)
    got1, got2, got3, res = (dict(zip(UNITS, refs[i * nu : (i + 1) * nu])) for i in range(4))
    refs = refs[4 * nu :]
    m_d, g_u0, g_u1, g_o, g_q, g_k, g_v, stage_a, stage_b, got0_d, got0_u = refs[:11]
    refs = refs[11:]
    cot, middle, dmid, rows_buf, wide_buf, part_buf, second, low, context, dcontext = refs[:10]
    gains, gain_sum, got_gain = refs[10:13]
    ssem, rsem, lsem, osem, rsems, wsems, psems, gs, gr, credit_u = refs[13:]
    here = coords()
    z, y, x, c = here
    me = owner(*here)
    ypeer, xpeer, speer = device(z, 1 - y, x, c), device(z, y, 1 - x, c), device(z, y, x, 1 - c)
    twin = z_twins(z)
    pair_peer, twin_peer = device(twin[1], y, x, c), device(twin[2], y, x, c)
    greet([xpeer, ypeer, speer, pair_peer, twin_peer])
    index = {u: i for i, u in enumerate(UNITS)}
    sent = {u: [] for u in UNITS}
    left = []
    every = slice(None)
    own = {"u0": g_u0, "u1": g_u1, "o": g_o, "q": g_q, "k": g_k, "v": g_v}
    staged = {
        "u0": (stage_a, 0, None),
        "u1": (stage_b, 0, None),
        "o": (stage_a, 0, "u0"),
        "q": (stage_a, 1024, "u0"),
        "k": (stage_b, 0, "u1"),
        "v": (stage_b, 1024, "u1"),
    }
    down_row = {"d0": 0, "dz": 64}

    def mine(u, k, yy, xx, lo, n):
        if u in down_row:
            return m_d.at[k, yy, xx, pl.ds(down_row[u] + lo, n)]
        return own[u].at[k, yy, xx, pl.ds(lo, n)]

    def first(u):
        if u in ("u0", "u1"):
            return got0_u
        return got0_d.at[:, :, :, pl.ds("oqkv".index(u) * 32, 32)]

    def send(u, k, make, peer):
        def copy():
            src, dst = make()
            return remote(src, dst, ssem.at[index[u], k], rsem.at[index[u], k], peer)

        copy().start()
        sent[u].append(copy)

    def wait(u, k, ref):
        remote(ref, ref, ssem.at[index[u], k], rsem.at[index[u], k], speer).wait_recv()

    def add(dst, src):
        dst[...] = dst[...] + src[...]

    def own_down(u):
        src = h_grad.at[:, :, :, pl.ds(down_row[u], 64)]
        dst = m_d.at[:, :, :, pl.ds(down_row[u], 64)]
        return pltpu.make_async_copy(src, dst, lsem.at[7 if u == "d0" else 8])

    def stage0(u):
        if u in down_row:
            own_down(u).start()
            return
        if u == "u1":
            pl.semaphore_wait(credit_u, 1)
        buf, col, before = staged[u]
        send(u, 0, lambda: (buf.at[:, :, :, :, pl.ds(col, own[u].shape[4])], first(u)), speer)

    def put(u, t, lhs, rhs):
        buf, col, before = staged[u]
        if before and before not in left:
            sent[before].pop(0)().wait_send()
            left.append(before)
        far = slice(t.start + col, t.stop + col)
        for k in range(4):
            v = dot(lhs[:, k * 256 : (k + 1) * 256], rhs, 0, 0).astype(jnp.bfloat16)
            v = v.reshape(2, 2, 64, v.shape[1])
            for core in range(2):

                @pl.when(c == core)
                def _():
                    own[u][k, :, :, :, t] = v[:, :, core * 32 : core * 32 + 32]
                    buf[k, :, :, :, far] = v[:, :, 32 - core * 32 : 64 - core * 32]

    def stage1(u):
        h, n = unit_shape(u)
        if u in down_row:
            own_down(u).wait()
        if u == "dz":
            for j in (1, 3):
                send(
                    u,
                    5 + j // 2,
                    lambda j=j: (mine(u, twin[j], every, every, 0, 64), got1[u].at[j // 2]),
                    pair_peer,
                )
            return

        def send_far():
            send(u, 1, lambda: (mine(u, every, every, 1 - x, 0, h), got1[u].at[0]), xpeer)
            send(u, 2, lambda: (mine(u, every, 1 - y, every, h, h), got1[u].at[1]), ypeer)

        if u == "d0":
            send_far()
            return
        got = first(u)
        wait(u, 0, got)
        for far in (True, False):
            xx, yy = (1 - x, 1 - y) if far else (x, y)

            @pl.loop(0, NZ)
            def _(k):
                for j in range(2):
                    add(mine(u, k, j, xx, 0, h), got.at[k, j, xx, pl.ds(0, h)])
                    add(mine(u, k, yy, j, h, h), got.at[k, yy, j, pl.ds(h, h)])

            if far:
                send_far()
        if u == "u0":
            pl.semaphore_signal(credit_u, inc=1, device_id=speer, device_id_type=MESH)

    def stage2(u):
        h, n = unit_shape(u)
        if u == "dz":
            wait(u, 6, got1[u].at[1])
            for yy in range(2):
                for xx in range(2):
                    add(mine(u, twin[2], yy, xx, 0, 64), got1[u].at[1, yy, xx])
            send(u, 7, lambda: (mine(u, twin[2], every, every, 0, 64), got1[u].at[2]), twin_peer)
            return
        wait(u, 1, got1[u].at[0])
        wait(u, 2, got1[u].at[1])
        for far in (True, False):
            xx, yy = (1 - x, 1 - y) if far else (x, y)

            @pl.loop(0, NZ)
            def _(k):
                add(mine(u, k, yy, x, 0, h), got1[u].at[0, k, yy])
                add(mine(u, k, y, xx, h, h), got1[u].at[1, k, xx])

            if far:
                send(u, 3, lambda: (mine(u, every, 1 - y, x, 0, h), got2[u].at[0]), ypeer)
                send(u, 4, lambda: (mine(u, every, y, 1 - x, h, h), got2[u].at[1]), xpeer)

    def stage3(u):
        h, n = unit_shape(u)
        if u == "dz":
            wait(u, 5, got1[u].at[0])
            wait(u, 7, got1[u].at[2])
            for xx in (1 - x, x):
                for yy in range(2):
                    at = mine(u, z, yy, xx, 0, 64)
                    total = at[...].astype(jnp.float32)
                    for j in (0, 2):
                        total = total + got1[u][j, yy, xx].astype(jnp.float32)
                    at[...] = total.astype(jnp.bfloat16)
                if xx is not x:
                    send(u, 1, lambda: (mine(u, z, every, 1 - x, 0, 64), got2[u]), xpeer)
            return
        wait(u, 3, got2[u].at[0])
        wait(u, 4, got2[u].at[1])

        @pl.loop(0, NZ)
        def _(k):
            add(mine(u, k, y, x, 0, h), got2[u].at[0, k])
            add(mine(u, k, y, x, h, h), got2[u].at[1, k])

        for j in (3, 1):

            def make(j=j):
                return mine(u, twin[j], y, x, 0, 2 * h), got3[u].at[j // 2]

            send(u, 5 + j // 2, make, pair_peer)

    def stage4(u):
        h, n = unit_shape(u)
        if u == "dz":
            wait(u, 1, got2[u])
            for yy in (1 - y, y):
                add(mine(u, z, yy, x, 0, 64), got2[u].at[yy])
                if yy is not y:
                    send(u, 3, lambda: (mine(u, z, 1 - y, x, 0, 64), got3[u]), ypeer)
            return
        wait(u, 6, got3[u].at[1])
        add(mine(u, twin[2], y, x, 0, 2 * h), got3[u].at[1])
        send(u, 7, lambda: (mine(u, twin[2], y, x, 0, 2 * h), got3[u].at[2]), twin_peer)

    finals = []

    def stage5(u):
        h, n = unit_shape(u)
        total = mine(u, z, y, x, 0, 2 * h)[...].astype(jnp.float32)
        if u == "dz":
            wait(u, 3, got3[u])
            total = total + got3[u][...].astype(jnp.float32)
        else:
            wait(u, 5, got3[u].at[0])
            wait(u, 7, got3[u].at[2])
            total = total + got3[u][0].astype(jnp.float32) + got3[u][2].astype(jnp.float32)
        res[u][...] = total
        result(u).start()
        finals.append(u)

    def result(u):
        dst = {
            "d0": o_gdown.at[pl.ds(0, 64)],
            "dz": o_gdown.at[pl.ds(64, 64)],
            "u0": o_gup.at[:, pl.ds(0, 2048)],
            "u1": o_gup.at[:, pl.ds(2048, 2048)],
            "o": o_gout,
            "q": o_gqkv.at[:, pl.ds(0, 1024)],
            "k": o_gqkv.at[:, pl.ds(1024, 1024)],
            "v": o_gqkv.at[:, pl.ds(2048, 1024)],
        }[u]
        return pltpu.make_async_copy(res[u], dst, osem.at[index[u]])

    stages = (stage0, stage1, stage2, stage3, stage4, stage5)
    stage0("d0")
    stage0("dz")

    def local(src, dst, k):
        cp = pltpu.make_async_copy(src, dst, lsem.at[k])
        cp.start()
        return cp

    row_steps = [(f_down, i) for i in range(8)] + [(f_out, i) for i in range(2)]
    row_steps += [(f_down, i) for i in range(8)]
    wide_steps = [(f_up, 4096, i) for i in range(4)] + [(f_qkv, 3072, i) for i in range(4)]
    part_steps = [(h_slope, i) for i in range(8)] + [(h_act, i) for i in range(8)]

    def row_copy(j):
        ref, i = row_steps[j]
        return pltpu.make_async_copy(ref.at[pl.ds(i * 512, 512)], rows_buf.at[j % 2], rsems.at[j % 2])

    def wide_copy(j):
        ref, n, i = wide_steps[j]
        dst = wide_buf.at[j % 2, :, pl.ds(0, n)]
        return pltpu.make_async_copy(ref.at[pl.ds(i * 256, 256)], dst, wsems.at[j % 2])

    def part_copy(j):
        ref, i = part_steps[j]
        return pltpu.make_async_copy(ref.at[:, pl.ds(i * 512, 512)], part_buf.at[j % 2], psems.at[j % 2])

    early = [local(h_cot, cot, 0), local(h_second, second, 2)]
    for copy in (row_copy, part_copy, wide_copy):
        copy(0).start()
        copy(1).start()
    early += [
        local(h_middle, middle, 1),
        local(h_gain, gains, 3),
        local(h_context, context, 4),
    ]

    def following(copy, steps, j):
        if j + 2 < len(steps):
            copy(j + 2).start()

    def run(order, work):
        for name in order:
            if "." in name:
                u, k = name.split(".")
                (work["gain"] if u == "g" else functools.partial(stages[int(k)], u))(
                    *([int(k)] if u == "g" else [])
                )
            else:
                short = name.rstrip("0123456789")
                rest = name[len(short) :]
                work[short](*([int(rest)] if rest else []))

    def phase_one(dhid):
        def chunk(i):
            if i == 0:
                early[0].wait()
                early[1].wait()
            slot = i % 2
            s = slice(i * 512, (i + 1) * 512)
            row_copy(i).wait()
            part_copy(i).wait()
            grown = dot(cot[...], rows_buf[slot], 1, 1) * part_buf[slot].astype(jnp.float32)
            dhid[:, s] = grown.astype(jnp.bfloat16)
            following(row_copy, row_steps, i)
            following(part_copy, part_steps, i)
            t = slice((i % 4) * 512, (i % 4 + 1) * 512)
            put("u0" if i < 4 else "u1", t, second, dhid[:, s])

        def grad_second(i):
            wide_copy(i).wait()
            s = slice(i * 256, (i + 1) * 256)
            dmid[:, s] = dot(dhid[...], wide_buf[i % 2], 1, 1)
            following(wide_copy, wide_steps, i)

        def norm_back_two():
            for cp in early[2:]:
                cp.wait()
            gain_sum[...] = jnp.zeros_like(gain_sum)

            def step(r):
                v, dn = middle[r, :], dmid[r, :]
                sc = scale_of(v)
                gain_sum[1:2, :] += jnp.sum(dn * v * sc, axis=0, keepdims=True)
                scaled = dn * gains[1:2, :]
                inner = jnp.mean(scaled * v, axis=-1, keepdims=True)
                total = cot[r, :].astype(jnp.float32) + (sc * scaled - v * (sc * sc * sc) * inner)
                dmid[r, :] = total
                low[r, :] = total.astype(jnp.bfloat16)

            rows_loop(step)

        run(NEAR, {"c": chunk, "ds": grad_second, "nb": norm_back_two})

    f32, bf = jnp.float32, jnp.bfloat16
    pl.run_scoped(phase_one, pltpu.VMEM((512, 4096), bf))

    def phase_two(qkv, dqkv, bias, lse, dk_sum, dv_sum):
        load_qkv = local(h_qkv, qkv, 1)
        load_lse = local(h_lse, lse, 3)
        load_tokens = local(h_tokens, second, 2)
        late = {}

        def grad_out(i):
            s = slice(i * 512, (i + 1) * 512)
            put("o", s, context, low[:, s])

        def grad_context(i):
            j = 8 + i
            row_copy(j).wait()
            s = slice(i * 512, (i + 1) * 512)
            dcontext[:, s] = dot(low[...], rows_buf[j % 2], 1, 1).astype(bf)
            following(row_copy, row_steps, j)

        def attend_back(pair):
            if pair == 0:
                load_qkv.wait()
                load_lse.wait()
                write_bias(lengths, bias)
            lane = lax.broadcasted_iota(jnp.int32, (1, 128), 1)
            lower = lane < HD
            col = pair * 128
            scale = 1.0 / math.sqrt(HD)
            for r0 in (256, 0):
                limit = r0 + 256
                q = qkv[r0:limit, col : col + 128]
                do = dcontext[r0:limit, col : col + 128]
                k = qkv[0:limit, 1024 + col : 1152 + col]
                v = qkv[0:limit, 2048 + col : 2176 + col]
                parts, dk, dv = [], None, None
                for h in range(2):
                    keep_lane = lower if h == 0 else ~lower
                    qh = jnp.where(keep_lane, q, jnp.zeros_like(q))
                    dh = jnp.where(keep_lane, do, jnp.zeros_like(do))
                    sums = jnp.where(lane == pair * 2 + h, lse[r0:limit, :], 0.0)
                    sums = jnp.sum(sums, axis=1, keepdims=True)
                    prob = jnp.exp2(dot(qh, k, 1, 1) * SCALE2 + bias[r0:limit, 0:limit] - sums)
                    scaled = prob * dot(dh, v, 1, 1)
                    inner = jnp.sum(scaled, axis=1, keepdims=True)
                    dlogit = (scaled - prob * inner).astype(bf)
                    parts.append(dot(dlogit, k, 1, 0))
                    dk_h = dot(dlogit, qh, 0, 0)
                    dv_h = dot(prob.astype(bf), dh, 0, 0)
                    dk = dk_h if dk is None else dk + dk_h
                    dv = dv_h if dv is None else dv + dv_h
                dqkv[r0:limit, col : col + 128] = (
                    jnp.where(lower, parts[0], parts[1]) * scale
                ).astype(bf)
                if limit == 512:
                    dk_sum[...] = dk
                    dv_sum[...] = dv
                else:
                    dk_sum[0:limit] += dk
                    dv_sum[0:limit] += dv
            dqkv[:, 1024 + col : 1152 + col] = (dk_sum[...] * scale).astype(bf)
            dqkv[:, 2048 + col : 2176 + col] = dv_sum[...].astype(bf)

        def renorm():
            load_tokens.wait()

            def step(r):
                v = second[r, :].astype(f32)
                context[r, :] = (v * scale_of(v) * gains[0:1, :]).astype(bf)

            rows_loop(step)

        def grad_qkv(j, i):
            s = slice(i * 512, (i + 1) * 512)
            t = slice(j * 1024 + i * 512, j * 1024 + (i + 1) * 512)
            put("qkv"[j], s, context, dqkv[:, t])

        def add_down(i):
            j = 10 + i
            row_copy(j).wait()
            part_copy(8 + i).wait()
            middle[...] = middle[...] + dot(part_buf[i % 2], rows_buf[j % 2], 1, 0)
            following(row_copy, row_steps, j)
            following(part_copy, part_steps, 8 + i)

        def out_end():
            rows_loop(lambda r: dcontext.__setitem__((r, every), middle[r, :].astype(bf)))
            late["out"] = local(dcontext, o_output, 5)

        def grad_normed(i):
            j = 4 + i
            wide_copy(j).wait()
            s = slice(i * 256, (i + 1) * 256)
            middle[:, s] = dot(dqkv[...], wide_buf[j % 2, :, 0:3072], 1, 1)
            following(wide_copy, wide_steps, j)

        def norm_final():
            def step(r):
                v, dn = second[r, :].astype(f32), middle[r, :]
                sc = scale_of(v)
                gain_sum[0:1, :] += jnp.sum(dn * v * sc, axis=0, keepdims=True)
                scaled = dn * gains[0:1, :]
                inner = jnp.mean(scaled * v, axis=-1, keepdims=True)
                total = dmid[r, :] + (sc * scaled - v * (sc * sc * sc) * inner)
                low[r, :] = total.astype(bf)

            rows_loop(step)
            late["tokens"] = local(low, o_tokens, 0)

        partners = (speer, xpeer, ypeer, pair_peer, twin_peer)

        def gain_step(k):
            if k:
                exchange(k - 1).wait()
                gain_sum[...] = gain_sum[...] + got_gain[k - 1]
            if k < 5:
                exchange(k).start()
            else:
                block = pl.multiple_of(me // 4 * 128, 128)
                o_gain[...] = gain_sum[:, pl.ds(block, 128)]

        def exchange(k):
            return remote(gain_sum, got_gain.at[k], gs.at[k], gr.at[k], partners[k])

        F = functools.partial
        run(
            LATE,
            {
                "go": grad_out,
                "dc": grad_context,
                "a": attend_back,
                "rn": renorm,
                "gq": F(grad_qkv, 0),
                "gk": F(grad_qkv, 1),
                "gv": F(grad_qkv, 2),
                "ad": add_down,
                "oe": out_end,
                "dn": grad_normed,
                "nf": norm_final,
                "gain": gain_step,
            },
        )
        for cp in late.values():
            cp.wait()

    pl.run_scoped(
        phase_two,
        pltpu.VMEM((512, 3072), bf),
        pltpu.VMEM((512, 3072), bf),
        pltpu.VMEM((512, 512), f32),
        pltpu.VMEM((512, 128), f32),
        pltpu.VMEM((512, 128), f32),
        pltpu.VMEM((512, 128), f32),
    )
    for u in UNITS:
        for copy in sent[u]:
            copy().wait_send()
    for u in finals:
        result(u).wait()


def backward(whole, saved, tokens, cotangent, lengths):
    gains, qkv, context, lse, middle, second, active, slope, grad_down = saved
    grad_down = grad_down.reshape(4, 2, 2, 128, 1024)
    hbm = pl.BlockSpec(memory_space=pl.ANY)
    vmem = pl.BlockSpec(memory_space=pltpu.VMEM)
    smem = pl.BlockSpec(memory_space=pltpu.SMEM)
    bf, f32, dma = jnp.bfloat16, jnp.float32, pltpu.SemaphoreType.DMA
    per = {u: unit_shape(u) for u in UNITS}
    got1 = [(2, 4, 2, h, n) if u != "dz" else (3, 2, 2, 64, n) for u, (h, n) in per.items()]
    got2 = [(2, 4, h, n) if u != "dz" else (2, 64, n) for u, (h, n) in per.items()]
    got3 = [(3, 2 * h, n) if u != "dz" else (64, n) for u, (h, n) in per.items()]
    scratch = (
        [(v, bf) for v in got1 + got2 + got3]
        + [((2 * h, n), f32) for h, n in per.values()]
        + [
            ((4, 2, 2, 128, 1024), bf),
            ((4, 2, 2, 32, 2048), bf),
            ((4, 2, 2, 32, 2048), bf),
            ((4, 2, 2, 32, 1024), bf),
            ((4, 2, 2, 32, 1024), bf),
            ((4, 2, 2, 32, 1024), bf),
            ((4, 2, 2, 32, 1024), bf),
            ((4, 2, 2, 32, 2048), bf),
            ((4, 2, 2, 32, 2048), bf),
            ((4, 2, 2, 128, 1024), bf),
            ((4, 2, 2, 32, 2048), bf),
            ((512, 1024), bf),
            ((512, 1024), f32),
            ((512, 1024), f32),
            ((2, 512, 1024), bf),
            ((2, 256, 4096), bf),
            ((2, 512, 512), bf),
            ((512, 1024), bf),
            ((512, 1024), bf),
            ((512, 1024), bf),
            ((512, 1024), bf),
            ((8, 1024), f32),
            ((8, 1024), f32),
            ((5, 8, 1024), f32),
        ]
    )
    outs = [
        ((512, 1024), bf),
        ((512, 1024), bf),
        ((32, 3072), f32),
        ((32, 1024), f32),
        ((32, 4096), f32),
        ((128, 1024), f32),
        ((8, 128), f32),
    ]
    nu = len(UNITS)
    return pl.pallas_call(
        backward_kernel,
        out_shape=[jax.ShapeDtypeStruct(*o) for o in outs],
        in_specs=[hbm] * 15 + [smem],
        out_specs=[hbm] * 6 + [vmem],
        scratch_shapes=[pltpu.VMEM(*v) for v in scratch]
        + [
            dma((nu, 8)),
            dma((nu, 8)),
            dma((9,)),
            dma((nu,)),
            dma((2,)),
            dma((2,)),
            dma((2,)),
            dma((5,)),
            dma((5,)),
            pltpu.SemaphoreType.REGULAR,
        ],
        compiler_params=pltpu.CompilerParams(
            collective_id=1, has_side_effects=True, vmem_limit_bytes=63 << 20
        ),
    )(
        *whole, qkv, context, lse, middle, second, active, slope, grad_down, gains, tokens, cotangent, lengths
    )


def project_input(inputs, w_qkv, gain):
    normed, scale_one = normalize(inputs, gain)
    normed_low = normed.astype(jnp.bfloat16)
    mixed = jnp.dot(normed_low, w_qkv, preferred_element_type=jnp.float32).astype(jnp.bfloat16)
    split = mixed.reshape(inputs.shape[0], 3, H, HD)
    return (normed_low, scale_one, split[:, 0], split[:, 1], split[:, 2])


def feed_inputs(inputs, context, w_out, w_up, gain):
    middle = inputs + jnp.dot(context, w_out, preferred_element_type=jnp.float32)
    second, scale_two = normalize(middle, gain)
    second_low = second.astype(jnp.bfloat16)
    hidden = jnp.dot(second_low, w_up, preferred_element_type=jnp.float32)
    active = jax.nn.gelu(hidden, approximate=True).astype(jnp.bfloat16)
    return (middle, scale_two, second_low, hidden, active)


def layer(tokens, lengths, w_qkv, w_out, w_up, w_down, gain_attn, gain_mlp, cotangent, low_type):
    total_rows = tokens.shape[0]
    ends = jnp.cumsum(lengths[0])
    places = jnp.arange(total_rows, dtype=jnp.int32)
    segment = jnp.sum((places[:, None] >= ends[None, :]).astype(jnp.int32), axis=1)
    inputs = tokens.astype(jnp.float32)
    gain_attn, gain_mlp = gain_attn.astype(jnp.float32), gain_mlp.astype(jnp.float32)
    normed_low, scale_one, queries, keys_all, values_all = project_input(inputs, w_qkv, gain_attn)
    context_full, log_sums = attend_forward(queries, keys_all, values_all, segment)
    context = context_full.reshape(total_rows, H * HD).astype(jnp.bfloat16)
    middle, scale_two, second_low, hidden, active = feed_inputs(
        inputs, context, w_out, w_up, gain_mlp
    )
    output = (middle + jnp.dot(active, w_down, preferred_element_type=jnp.float32)).astype(
        jnp.bfloat16
    )
    grad_down = jnp.einsum("rf,rd->fd", active, cotangent, preferred_element_type=low_type)
    grad_active = jnp.einsum("rd,fd->rf", cotangent, w_down, preferred_element_type=jnp.float32)
    unused, gelu_pull = jax.vjp(lambda values: jax.nn.gelu(values, approximate=True), hidden)
    grad_hidden = gelu_pull(grad_active)[0].astype(jnp.bfloat16)
    grad_up = jnp.einsum("rd,rf->df", second_low, grad_hidden, preferred_element_type=low_type)
    grad_second = jnp.einsum("rf,df->rd", grad_hidden, w_up, preferred_element_type=jnp.float32)
    grad_mid_norm, grad_gain_m = norm_back(grad_second, middle, scale_two, gain_mlp)
    grad_middle = cotangent.astype(jnp.float32) + grad_mid_norm
    grad_mid_low = grad_middle.astype(jnp.bfloat16)
    grad_out = jnp.einsum("rc,rd->cd", context, grad_mid_low, preferred_element_type=low_type)
    grad_context = jnp.einsum("rd,cd->rc", grad_mid_low, w_out, preferred_element_type=jnp.float32)
    grad_context = grad_context.astype(jnp.bfloat16).reshape(total_rows, H, HD)
    grad_queries, grad_keys, grad_values = attend_backward(
        queries, keys_all, values_all, segment, log_sums, grad_context
    )
    grad_mixed = (
        jnp.stack([grad_queries, grad_keys, grad_values], axis=1)
        .reshape(total_rows, 3 * H * HD)
        .astype(jnp.bfloat16)
    )
    grad_qkv = jnp.einsum("rd,re->de", normed_low, grad_mixed, preferred_element_type=low_type)
    grad_normed = jnp.einsum("re,de->rd", grad_mixed, w_qkv, preferred_element_type=jnp.float32)
    grad_in_norm, grad_gain_a = norm_back(grad_normed, inputs, scale_one, gain_attn)
    grad_tokens = (grad_middle + grad_in_norm).astype(jnp.bfloat16)
    return (output, grad_tokens, grad_qkv, grad_out, grad_up, grad_down, grad_gain_a, grad_gain_m)


def shards_any(tokens, lengths, w_qkv, w_out, w_up, w_down, gain_attn, gain_mlp, cotangent):
    whole = gather_any(w_qkv, w_out, w_up, w_down, gain_attn, gain_mlp)
    out = layer(tokens, lengths, *whole, cotangent, jnp.float32)
    return out[:2] + sum_any(*out[2:])


def keep_kernel(*refs):
    n = (len(refs) - 2) // 3
    gets, puts = refs[-2:]
    into = [pltpu.make_async_copy(refs[i], refs[2 * n + i], gets.at[i]) for i in range(n)]
    back = [pltpu.make_async_copy(refs[2 * n + i], refs[n + i], puts.at[i]) for i in range(n)]
    for cp in into:
        cp.start()
    for i in range(n):
        into[i].wait()
        back[i].start()
    for cp in back:
        cp.wait()


def keep(arrays):
    hbm = pl.BlockSpec(memory_space=pl.ANY)
    return pl.pallas_call(
        keep_kernel,
        out_shape=[jax.ShapeDtypeStruct(a.shape, a.dtype) for a in arrays],
        in_specs=[hbm] * len(arrays),
        out_specs=[hbm] * len(arrays),
        scratch_shapes=[pltpu.VMEM(a.shape, a.dtype) for a in arrays]
        + [pltpu.SemaphoreType.DMA((len(arrays),))] * 2,
    )(*arrays)


def shards(tokens, lengths, w_qkv, w_out, w_up, w_down, gain_attn, gain_mlp, cotangent):
    me = lax.axis_index("dp") * 4 + lax.axis_index("fsdp")
    lanes = lax.rem(me, 4) * 32
    pair = jnp.stack([gain_attn, gain_mlp]).astype(jnp.float32)
    spot = lax.dynamic_update_slice(jnp.zeros((8, 128), jnp.float32), pair, (0, lanes))
    whole, saved = forward((w_qkv, w_out, w_up, w_down), spot, lengths, tokens, cotangent)
    output, grad_tokens, g_qkv, g_out, g_up, g_down, g_gain = backward(
        whole, saved, tokens, cotangent, lengths
    )
    own = lax.dynamic_slice(g_gain, (0, lanes), (2, 32))
    kept = keep((output, grad_tokens, g_qkv, g_out, g_up, g_down))
    return (*kept, own[0], own[1])


def solution(mesh):
    rows, flat = P(AXES, None), P(AXES)
    known = dict(mesh.shape) == {"dp": 8, "fsdp": 4}
    return jax.shard_map(
        shards if known else shards_any,
        mesh=mesh,
        in_specs=(rows, rows, rows, rows, rows, rows, flat, flat, rows),
        out_specs=(rows, rows, rows, rows, rows, rows, flat, flat),
        check_vma=False,
    )
```

```python
import functools
import math

import jax
import jax.numpy as jnp
from jax import lax
from jax.experimental import pallas as pl
from jax.experimental.pallas import tpu as pltpu
from jax.sharding import PartitionSpec as P

H = 16
HD = 64
MESH = pl.DeviceIdType.MESH
AXES = ("dp", "fsdp")


epsilon = 1e-05


def normalize(values, gain):
    scale_row = lax.rsqrt(jnp.mean(values * values, axis=-1, keepdims=True) + epsilon)
    return (values * scale_row * gain, scale_row)


def norm_back(grad_normed, values, scale_row, gain):
    scaled = grad_normed * gain
    grad_gain = jnp.sum(grad_normed * values * scale_row, axis=0)
    cubed = scale_row * scale_row * scale_row
    grad_values = scale_row * scaled - values * cubed * jnp.mean(
        scaled * values, axis=-1, keepdims=True
    )
    return (grad_values, grad_gain)


def block_logits(query_block, key_rows, segment):
    block_rows = query_block.shape[0]
    key_limit = key_rows.shape[0]
    raw = jnp.einsum("qhd,khd->hqk", query_block, key_rows, preferred_element_type=jnp.float32)
    query_place = jnp.arange(block_rows, dtype=jnp.int32)
    key_place = jnp.arange(key_limit, dtype=jnp.int32)
    allowed = (segment[:, None] == segment[None, :]) & (query_place[:, None] >= key_place[None, :])
    return jnp.where(allowed[None], raw * (1.0 / math.sqrt(HD)), -1e30)


def attend_forward(queries, keys_all, values_all, segment):
    logits = block_logits(queries, keys_all, segment)
    peak = jnp.max(logits, axis=-1, keepdims=True)
    raised = jnp.exp(logits - peak)
    totals = jnp.sum(raised, axis=-1, keepdims=True)
    attn_prob = (raised / totals).astype(jnp.bfloat16)
    contexts = jnp.einsum("hqk,khd->qhd", attn_prob, values_all, preferred_element_type=jnp.float32)
    log_sums = (peak + jnp.log(totals))[:, :, 0]
    return (contexts, log_sums)


def attend_backward(queries, keys_all, values_all, segment, log_sums, grad_context):
    logits = block_logits(queries, keys_all, segment)
    attn_prob = jnp.exp(logits - log_sums[:, :, None])
    rounded = attn_prob.astype(jnp.bfloat16)
    grad_prob = jnp.einsum(
        "qhd,khd->hqk", grad_context, values_all, preferred_element_type=jnp.float32
    )
    inner = jnp.sum(attn_prob * grad_prob, axis=-1, keepdims=True)
    grad_logit = (1.0 / math.sqrt(HD) * attn_prob * (grad_prob - inner)).astype(jnp.bfloat16)
    grad_queries = jnp.einsum(
        "hqk,khd->qhd", grad_logit, keys_all, preferred_element_type=jnp.float32
    )
    grad_keys = jnp.einsum("hqk,qhd->khd", grad_logit, queries, preferred_element_type=jnp.float32)
    grad_values = jnp.einsum(
        "hqk,qhd->khd", rounded, grad_context, preferred_element_type=jnp.float32
    )
    return (grad_queries, grad_keys, grad_values)


def gather_any(*weights):
    return tuple(lax.all_gather(w, AXES, axis=0, tiled=True) for w in weights)


def sum_any(*grads):
    return tuple(lax.psum_scatter(g, AXES, scatter_dimension=0, tiled=True) for g in grads)


NZ = 4


def coords():
    a, b = lax.axis_index("dp"), lax.axis_index("fsdp")
    return a // 2, a % 2, b // 2, b % 2


def device(z, y, x, c):
    return (z * 2 + y, x * 2 + c)


def owner(z, y, x, c):
    return ((z * 2 + y) * 2 + x) * 2 + c


def all_peers(z, y, x, c):
    peers = []
    for d in range(NZ):
        for m in range(2):
            for l in range(2):
                for s in range(2):
                    if d + m + l + s:
                        peers.append(
                            device(
                                lax.rem(z + d, NZ),
                                1 - y if m else y,
                                1 - x if l else x,
                                1 - c if s else c,
                            )
                        )
    return peers


def greet(peers):
    sem = pltpu.get_barrier_semaphore()
    for peer in peers:
        pl.semaphore_signal(sem, inc=1, device_id=peer, device_id_type=MESH)
    pl.semaphore_wait(sem, len(peers))


def remote(src, dst, send_sem, recv_sem, peer):
    return pltpu.make_async_remote_copy(
        src_ref=src, dst_ref=dst, send_sem=send_sem, recv_sem=recv_sem,
        device_id=peer, device_id_type=MESH,
    )


FORWARD = 512
SHARDS = ((32, 3072), (32, 1024), (32, 4096), (128, 1024), (8, 128))
PARTS = (
    (0, 0, 32, 0, 1280, "21yx"),
    (0, 0, 32, 1280, 1280, "21xy"),
    (0, 0, 32, 2560, 512, "xy21"),
    (1, 0, 16, 0, 1024, "21yx"),
    (1, 16, 16, 0, 1024, "21xy"),
    (2, 0, 32, 0, 896, "21yx"),
    (2, 0, 32, 896, 768, "21xy"),
    (2, 0, 32, 1664, 384, "xy21"),
    (2, 0, 32, 2048, 768, "21yx"),
    (2, 0, 32, 2816, 896, "21xy"),
    (2, 0, 32, 3712, 384, "yx21"),
    (3, 0, 48, 0, 1024, "21yx"),
    (3, 48, 48, 0, 1024, "21xy"),
    (3, 96, 32, 0, 1024, "yx21"),
    (4, 0, 8, 0, 128, "21yx"),
)
GROUPS = ((14, 0, 1, 2), (3, 4), (5, 6, 7), (8, 9, 10), (11, 12, 13))
STEPS = 4


def z_twins(z):
    return (z, z + 1 - 2 * lax.rem(z, 2), lax.rem(z + 2, NZ), NZ - 1 - z)


def moved(rel, dim):
    e, m, l = rel
    return {"1": (e ^ 1, m, l), "2": (e ^ 2, m, l), "y": (e, 1 - m, l), "x": (e, m, 1 - l)}[dim]


def routes(stages):
    hold, arrivals, slot = [(0, 0, 0)], [], {}
    for s, dim in enumerate(stages):
        new = []
        for rel in hold:
            slot[rel, s] = len(arrivals)
            arrivals.append((moved(rel, dim), s))
            new.append(arrivals[-1][0])
        hold = hold + new
    return arrivals, slot


class Gather:
    def __init__(self, ins, outs, sems, here):
        self.ins, self.outs, (self.ssem, self.rsem) = ins, outs, sems
        z, y, x, c = here
        self.core = c
        self.zfrom = z_twins(z)
        self.ys, self.xs = (y, 1 - y), (x, 1 - x)
        self.peer = {"1": device(self.zfrom[1], y, x, c), "2": device(self.zfrom[2], y, x, c)}
        self.peer["y"] = device(z, 1 - y, x, c)
        self.peer["x"] = device(z, y, 1 - x, c)
        self.other = device(z, y, x, 1 - c)
        self.plan = [routes(p[5]) for p in PARTS]
        self.sent = []

    def place(self, part, rel, core):
        w, r0, nr, c0, nc, stages = PARTS[part]
        o = owner(self.zfrom[rel[0]], self.ys[rel[1]], self.xs[rel[2]], core)
        n = SHARDS[w][0]
        return self.outs[w].at[pl.ds(pl.multiple_of(o * n + r0, math.gcd(n, r0 or n, 16)), nr), pl.ds(c0, nc)]

    def send(self, part, rel, k, peer, own):
        w, r0, nr, c0, nc, stages = PARTS[part]
        dst = self.place(part, rel, self.core)
        src = self.ins[w].at[pl.ds(r0, nr), pl.ds(c0, nc)] if own else dst
        cp = remote(src, dst, self.ssem.at[part, k], self.rsem.at[part, k], peer)
        cp.start()
        self.sent.append(cp)

    def wait(self, part, rel, core, k):
        ref = self.place(part, rel, core)
        remote(ref, ref, self.ssem.at[part, k], self.rsem.at[part, k], self.other).wait_recv()

    def forward(self, part, rel, s, i):
        stages, slot = PARTS[part][5], self.plan[part][1]
        for t in range(s + 1, STEPS):
            self.send(part, rel, slot[rel, t], self.peer[stages[t]], s < 0)
        self.send(part, rel, 15 + i, self.other, s < 0)

    def start(self, group):
        for part in group:
            self.forward(part, (0, 0, 0), -1, 0)

    def arrive(self, group, s):
        ks = [[k for k, a in enumerate(self.plan[p][0]) if a[1] == s] for p in group]
        steps = []
        for j in range(max(map(len, ks))):
            steps.append([(p, k[j]) for p, k in zip(group, ks) if j < len(k)])

        def one(step):
            for part, k in step:
                rel = self.plan[part][0][k][0]
                self.wait(part, rel, self.core, k)
                self.forward(part, rel, s, 1 + k)

        return [functools.partial(one, step) for step in steps]

    def halves(self, group):
        for part in group:
            for i, rel in enumerate([(0, 0, 0)] + [a[0] for a in self.plan[part][0]]):
                self.wait(part, rel, 1 - self.core, 15 + i)


def dot(a, b, ca, cb):
    return lax.dot_general(
        a, b, (((ca,), (cb,)), ((), ())), preferred_element_type=jnp.float32
    )


def scale_of(values):
    return lax.rsqrt(jnp.mean(values * values, axis=-1, keepdims=True) + epsilon)


def rows_loop(step):
    @pl.loop(0, 8)
    def _(i):
        step(pl.ds(pl.multiple_of(i * 64, 64), 64))


LOG2E = math.log2(math.e)
SCALE2 = LOG2E / math.sqrt(HD)


def write_bias(lengths, bias):
    ends, total = [], jnp.int32(0)
    for j in range(lengths.shape[1]):
        total = total + lengths[0, j]
        ends.append(total)
    key = lax.broadcasted_iota(jnp.int32, (1, 512), 1)
    seg_key = sum((key >= e).astype(jnp.int32) for e in ends)

    @pl.loop(0, 8)
    def _(i):
        query = lax.broadcasted_iota(jnp.int32, (64, 1), 0) + i * 64
        seg_query = sum((query >= e).astype(jnp.int32) for e in ends)
        ok = (seg_query == seg_key) & (query >= key)
        bias[pl.ds(pl.multiple_of(i * 64, 64), 64), :] = jnp.where(ok, 0.0, -1e30)


def attend_pair(pair, qkv, bias, context, lse):
    lane = lax.broadcasted_iota(jnp.int32, (1, 128), 1)
    low = lane < HD
    col = pl.multiple_of(pair * 128, 128)
    q = qkv[:, pl.ds(col, 128)]
    k = qkv[:, pl.ds(1024 + col, 128)]
    v = qkv[:, pl.ds(2048 + col, 128)]
    parts, sums = [], lse[...]
    for h in range(2):
        qh = jnp.where(low if h == 0 else ~low, q, jnp.zeros_like(q))
        logits = dot(qh, k, 1, 1) * SCALE2 + bias[...]
        peak = jnp.max(logits, axis=1, keepdims=True)
        raised = jnp.exp2(logits - peak)
        total = jnp.sum(raised, axis=1, keepdims=True)
        parts.append(dot(raised.astype(jnp.bfloat16), v, 1, 0) * (1.0 / total))
        sums = jnp.where(lane == pair * 2 + h, peak + jnp.log2(total), sums)
    context[:, pl.ds(col, 128)] = jnp.where(low, parts[0], parts[1]).astype(jnp.bfloat16)
    lse[...] = sums


GELU_A = math.sqrt(2.0 / math.pi)


def forward_kernel(*refs):
    ins, gain_in, lengths, tokens, cotangent = refs[:4], *refs[4:8]
    outs = refs[8:12]
    o_gain, o_qkv, o_context, o_lse, o_middle, o_second, o_active, o_slope, o_grad = refs[12:21]
    w_qkv, w_out, w_up, normed, qkv, bias, context, lse, middle, second = refs[21:31]
    hid, act, slope, grad, grad_in, gains, gain_row = refs[31:38]
    lsem, wsem, hsem, gsem, gssem, grsem, ssem, rsem = refs[38:]
    here = coords()
    me = owner(*here)
    g = Gather((*ins, gain_in), (*outs, gains), (ssem, rsem), here)
    greet([*g.peer.values(), g.other])
    g.start(GROUPS[0])
    for w in range(4):
        n = SHARDS[w][0]
        cp = pltpu.make_async_copy(
            ins[w], outs[w].at[pl.ds(pl.multiple_of(me * n, n), n)], lsem.at[w]
        )
        cp.start()
    own = [
        pltpu.make_async_copy(
            ins[w],
            outs[w].at[pl.ds(pl.multiple_of(me * SHARDS[w][0], SHARDS[w][0]), SHARDS[w][0])],
            lsem.at[w],
        )
        for w in range(4)
    ]
    gains[pl.ds(pl.multiple_of(me * 8, 8), 8), :] = gain_in[...]
    write_bias(lengths, bias)
    saves = []

    def save(src, dst, k):
        cp = pltpu.make_async_copy(src, dst, lsem.at[k])
        cp.start()
        saves.append(cp)

    def gain_rows():
        for b in range(8):
            total = gains[32 * b : 32 * b + 8, :]
            for j in range(1, 4):
                total = total + gains[32 * b + 8 * j : 32 * b + 8 * j + 8, :]
            gain_row[:, b * 128 : (b + 1) * 128] = total
        save(gain_row, o_gain, 4)

    def norm_one():
        def step(r):
            v = tokens[r, :].astype(jnp.float32)
            normed[r, :] = (v * scale_of(v) * gain_row[0:1, :]).astype(jnp.bfloat16)

        rows_loop(step)

    def load(group, w, dst, n, blocks):
        width = SHARDS[w][1] // n
        g.halves(GROUPS[group])
        if 0 in blocks:
            own[w].wait()
        for i in blocks:
            s = pl.ds(i * width, width)
            pltpu.make_async_copy(outs[w].at[:, s], dst.at[:, s], wsem.at[w, i]).start()

    def loaded(w, dst, n, i):
        s = pl.ds(i * (SHARDS[w][1] // n), SHARDS[w][1] // n)
        pltpu.make_async_copy(outs[w].at[:, s], dst.at[:, s], wsem.at[w, i]).wait()

    def project(i):
        loaded(0, w_qkv, 6, i)
        s = slice(i * 512, (i + 1) * 512)
        qkv[:, s] = dot(normed[...], w_qkv[:, s], 1, 0).astype(jnp.bfloat16)

    def attend(i):
        attend_pair(i, qkv, bias, context, lse)

    def attended():
        save(qkv, o_qkv, 5)
        save(context, o_context, 6)
        save(lse, o_lse, 7)

    def add_out(i):
        loaded(1, w_out, 2, i)
        s = slice(i * 512, (i + 1) * 512)
        middle[:, s] = tokens[:, s].astype(jnp.float32) + dot(context[...], w_out[:, s], 1, 0)

    def norm_two():
        save(middle, o_middle, 8)

        def step(r):
            v = middle[r, :]
            second[r, :] = (v * scale_of(v) * gain_row[1:2, :]).astype(jnp.bfloat16)

        rows_loop(step)
        save(second, o_second, 9)

    hid_copies = []
    core = here[3]

    def feed(i):
        loaded(2, w_up, 8, i)
        s = slice(i * 512, (i + 1) * 512)
        slot = i % 2
        if i >= 2:
            for cp in hid_copies[i - 2]:
                cp.wait()
        hid[...] = dot(second[...], w_up[:, s], 1, 0)

        def step(r):
            v = hid[r, :]
            sq = v * v
            t = jnp.tanh(GELU_A * (v + 0.044715 * v * sq))
            half = 0.5 * (1.0 + t)
            act[slot, r, :] = (v * half).astype(jnp.bfloat16)
            rise = half + 0.5 * v * (1.0 - t * t) * (GELU_A * (1.0 + 3 * 0.044715 * sq))
            slope[slot, r, :] = rise.astype(jnp.bfloat16)

        rows_loop(step)
        pair = [
            pltpu.make_async_copy(act.at[slot], o_active.at[:, s], hsem.at[slot]),
            pltpu.make_async_copy(slope.at[slot], o_slope.at[:, s], hsem.at[2 + slot]),
        ]
        for cp in pair:
            cp.start()
        hid_copies.append(pair)

    def feed_grad(i):
        slot = i % 2
        s = slice(i * 512, (i + 1) * 512)
        grad[i] = (
            dot(act[slot], cotangent[...], 0, 0).astype(jnp.bfloat16).reshape(2, 2, 128, 1024)
        )
        share(i).start()

    def share(i):
        return remote(grad.at[i, :, 1 - core], grad_in.at[i], gssem.at[i], grsem.at[i], g.other)

    def grad_out(i):
        return pltpu.make_async_copy(grad.at[i, :, core], o_grad.at[pl.ds(2 * i, 2)], gsem.at[i])

    def sum_grad(i):
        share(i).wait_recv()
        for chip in range(2):
            at = grad.at[i, chip, core]
            at[...] = at[...] + grad_in[i, chip]
        grad_out(i).start()

    events = []
    for t in range(1, STEPS + len(GROUPS)):
        if t < len(GROUPS):
            events += [functools.partial(g.start, GROUPS[t])]
        for s in reversed(range(STEPS)):
            if 0 <= t - s - 1 < len(GROUPS):
                events += g.arrive(GROUPS[t - s - 1], s)
                if s == STEPS - 1:
                    events.append("whole%d" % (t - s - 1))
    F = functools.partial
    work = {
        0: [gain_rows, norm_one]
        + [F(project, i) for i in range(6)] + [F(attend, i) for i in range(8)] + [attended],
        1: [F(add_out, i) for i in range(2)] + [norm_two],
        2: [F(f, i) for i in range(4) for f in (feed, feed_grad)] + [F(sum_grad, 0)],
        3: [
            F(f, j)
            for i in range(4, 8)
            for f, j in ((feed, i), (feed_grad, i), (sum_grad, i - 3))
        ]
        + [F(sum_grad, i) for i in (5, 6, 7)],
    }
    ready, since = [], 0
    n_load = {
        0: (0, w_qkv, 6, range(6)),
        1: (1, w_out, 2, range(2)),
        2: (2, w_up, 8, range(4)),
        3: (2, w_up, 8, range(4, 8)),
    }
    lse[...] = jnp.zeros_like(lse)
    for e in events:
        if isinstance(e, str):
            w = int(e[5:])
            if w in n_load:
                ready.append(F(load, w, *n_load[w]))
                ready += work[w]
            continue
        e()
        since += 1
        if ready and since >= EVERY:
            ready.pop(0)()
            since = 0
    for step in ready:
        step()
    g.halves(GROUPS[-1])
    own[3].wait()
    for cp in hid_copies[-2] + hid_copies[-1] + saves:
        cp.wait()
    for i in range(8):
        share(i).wait_send()
        grad_out(i).wait()
    for cp in g.sent:
        cp.wait_send()


EVERY = 1


def forward(weights, gains, lengths, tokens, cotangent):
    hbm = pl.BlockSpec(memory_space=pl.ANY)
    vmem = pl.BlockSpec(memory_space=pltpu.VMEM)
    smem = pl.BlockSpec(memory_space=pltpu.SMEM)
    bf, f32 = jnp.bfloat16, jnp.float32
    saved = [
        ((8, 1024), f32),
        ((512, 3072), bf),
        ((512, 1024), bf),
        ((512, 128), f32),
        ((512, 1024), f32),
        ((512, 1024), bf),
        ((512, 4096), bf),
        ((512, 4096), bf),
        ((16, 128, 1024), bf),
    ]
    scratch = [
        ((1024, 3072), bf),
        ((1024, 1024), bf),
        ((1024, 4096), bf),
        ((512, 1024), bf),
        ((512, 3072), bf),
        ((512, 512), f32),
        ((512, 1024), bf),
        ((512, 128), f32),
        ((512, 1024), f32),
        ((512, 1024), bf),
        ((512, 512), f32),
        ((2, 512, 512), bf),
        ((2, 512, 512), bf),
        ((8, 2, 2, 128, 1024), bf),
        ((8, 2, 128, 1024), bf),
        ((256, 128), f32),
        ((8, 1024), f32),
    ]
    dma = pltpu.SemaphoreType.DMA
    out = pl.pallas_call(
        forward_kernel,
        out_shape=[jax.ShapeDtypeStruct((w.shape[0] * 32, w.shape[1]), w.dtype) for w in weights]
        + [jax.ShapeDtypeStruct(*s) for s in saved],
        in_specs=[vmem] * 5 + [smem, vmem, vmem],
        out_specs=[hbm] * 13,
        scratch_shapes=[pltpu.VMEM(*s) for s in scratch]
        + [
            dma((10,)),
            dma((3, 8)),
            dma((4,)),
            dma((8,)),
            dma((8,)),
            dma((8,)),
            dma((len(PARTS), 31)),
            dma((len(PARTS), 31)),
        ],
        compiler_params=pltpu.CompilerParams(
            collective_id=0, has_side_effects=True, vmem_limit_bytes=60 << 20
        ),
    )(*weights, gains, lengths, tokens, cotangent)
    return out[:4], out[4:]


UNITS = ("dz", "d0", "u0", "u1", "o", "q", "k", "v")
SHAPE = {"dz": (32, 1024), "d0": (32, 1024), "u0": (16, 2048), "u1": (16, 2048)}
NEAR = (
    "d0.1", "dz.1", "c0", "c1", "c2", "c3", "u0.0", "c4", "c5", "c6", "d0.2", "u0.1", "c7", "u1.0",
    "ds0", "ds1", "ds2", "ds3", "d0.3", "nb",
)
LATE = (
    "u1.1", "dz.2", "go0", "go1", "o.0", "dc0", "dc1", "a0", "d0.4", "a1", "o.1", "u0.2", "a2",
    "a3", "a4", "a5", "a6", "u1.2", "a7", "rn", "gq0", "gq1", "q.0", "o.2", "gk0", "gk1", "k.0",
    "dz.3", "gv0", "gv1", "v.0", "ad0", "q.1", "u0.3", "ad1", "k.1", "d0.5", "ad2", "ad3", "ad4",
    "u1.3", "ad5", "ad6", "o.3", "u0.4", "ad7", "oe", "dn0", "dn1", "dn2", "dz.4", "u1.4", "dn3",
    "nf", "g.0", "o.4", "q.2", "v.1", "u0.5", "g.1", "dz.5", "u1.5", "k.2", "o.5", "q.3", "q.4",
    "v.2", "g.2", "k.3", "q.5", "g.3", "v.3", "k.4", "g.4", "v.4", "g.5", "k.5", "v.5",
)


def unit_shape(u):
    return SHAPE.get(u, (16, 1024))


def backward_kernel(*refs):
    f_qkv, f_out, f_up, f_down, h_qkv, h_context, h_lse, h_middle, h_second, h_act, h_slope, h_grad = (
        refs[:12]
    )
    h_gain, h_tokens, h_cot, lengths = refs[12:16]
    o_output, o_tokens, o_gqkv, o_gout, o_gup, o_gdown, o_gain = refs[16:23]
    refs = refs[23:]
    nu = len(UNITS)
    got1, got2, got3, res = (dict(zip(UNITS, refs[i * nu : (i + 1) * nu])) for i in range(4))
    refs = refs[4 * nu :]
    m_d, g_u0, g_u1, g_o, g_q, g_k, g_v, stage_a, stage_b, got0_d, got0_u = refs[:11]
    refs = refs[11:]
    cot, middle, dmid, rows_buf, wide_buf, part_buf, second, low, context, dcontext = refs[:10]
    gains, gain_sum, got_gain = refs[10:13]
    ssem, rsem, lsem, osem, rsems, wsems, psems, gs, gr, credit_u = refs[13:]
    here = coords()
    z, y, x, c = here
    me = owner(*here)
    ypeer, xpeer, speer = device(z, 1 - y, x, c), device(z, y, 1 - x, c), device(z, y, x, 1 - c)
    twin = z_twins(z)
    pair_peer, twin_peer = device(twin[1], y, x, c), device(twin[2], y, x, c)
    greet([xpeer, ypeer, speer, pair_peer, twin_peer])
    index = {u: i for i, u in enumerate(UNITS)}
    sent = {u: [] for u in UNITS}
    left = []
    every = slice(None)
    own = {"u0": g_u0, "u1": g_u1, "o": g_o, "q": g_q, "k": g_k, "v": g_v}
    staged = {
        "u0": (stage_a, 0, None),
        "u1": (stage_b, 0, None),
        "o": (stage_a, 0, "u0"),
        "q": (stage_a, 1024, "u0"),
        "k": (stage_b, 0, "u1"),
        "v": (stage_b, 1024, "u1"),
    }
    down_row = {"d0": 0, "dz": 64}

    def mine(u, k, yy, xx, lo, n):
        if u in down_row:
            return m_d.at[k, yy, xx, pl.ds(down_row[u] + lo, n)]
        return own[u].at[k, yy, xx, pl.ds(lo, n)]

    def first(u):
        if u in ("u0", "u1"):
            return got0_u
        return got0_d.at[:, :, :, pl.ds("oqkv".index(u) * 32, 32)]

    def send(u, k, make, peer):
        def copy():
            src, dst = make()
            return remote(src, dst, ssem.at[index[u], k], rsem.at[index[u], k], peer)

        copy().start()
        sent[u].append(copy)

    def wait(u, k, ref):
        remote(ref, ref, ssem.at[index[u], k], rsem.at[index[u], k], speer).wait_recv()

    def add(dst, src):
        dst[...] = dst[...] + src[...]

    def own_down(u):
        src = h_grad.at[:, :, :, pl.ds(down_row[u], 64)]
        dst = m_d.at[:, :, :, pl.ds(down_row[u], 64)]
        return pltpu.make_async_copy(src, dst, lsem.at[7 if u == "d0" else 8])

    def stage0(u):
        if u in down_row:
            own_down(u).start()
            return
        if u == "u1":
            pl.semaphore_wait(credit_u, 1)
        buf, col, before = staged[u]
        send(u, 0, lambda: (buf.at[:, :, :, :, pl.ds(col, own[u].shape[4])], first(u)), speer)

    def put(u, t, lhs, rhs):
        buf, col, before = staged[u]
        if before and before not in left:
            sent[before].pop(0)().wait_send()
            left.append(before)
        far = slice(t.start + col, t.stop + col)
        for k in range(4):
            v = dot(lhs[:, k * 256 : (k + 1) * 256], rhs, 0, 0).astype(jnp.bfloat16)
            v = v.reshape(2, 2, 64, v.shape[1])
            for core in range(2):

                @pl.when(c == core)
                def _():
                    own[u][k, :, :, :, t] = v[:, :, core * 32 : core * 32 + 32]
                    buf[k, :, :, :, far] = v[:, :, 32 - core * 32 : 64 - core * 32]

    def stage1(u):
        h, n = unit_shape(u)
        if u in down_row:
            own_down(u).wait()
        if u == "dz":
            for j in (1, 3):
                send(
                    u,
                    5 + j // 2,
                    lambda j=j: (mine(u, twin[j], every, every, 0, 64), got1[u].at[j // 2]),
                    pair_peer,
                )
            return

        def send_far():
            send(u, 1, lambda: (mine(u, every, every, 1 - x, 0, h), got1[u].at[0]), xpeer)
            send(u, 2, lambda: (mine(u, every, 1 - y, every, h, h), got1[u].at[1]), ypeer)

        if u == "d0":
            send_far()
            return
        got = first(u)
        wait(u, 0, got)
        for far in (True, False):
            xx, yy = (1 - x, 1 - y) if far else (x, y)

            @pl.loop(0, NZ)
            def _(k):
                for j in range(2):
                    add(mine(u, k, j, xx, 0, h), got.at[k, j, xx, pl.ds(0, h)])
                    add(mine(u, k, yy, j, h, h), got.at[k, yy, j, pl.ds(h, h)])

            if far:
                send_far()
        if u == "u0":
            pl.semaphore_signal(credit_u, inc=1, device_id=speer, device_id_type=MESH)

    def stage2(u):
        h, n = unit_shape(u)
        if u == "dz":
            wait(u, 6, got1[u].at[1])
            for yy in range(2):
                for xx in range(2):
                    add(mine(u, twin[2], yy, xx, 0, 64), got1[u].at[1, yy, xx])
            send(u, 7, lambda: (mine(u, twin[2], every, every, 0, 64), got1[u].at[2]), twin_peer)
            return
        wait(u, 1, got1[u].at[0])
        wait(u, 2, got1[u].at[1])
        for far in (True, False):
            xx, yy = (1 - x, 1 - y) if far else (x, y)

            @pl.loop(0, NZ)
            def _(k):
                add(mine(u, k, yy, x, 0, h), got1[u].at[0, k, yy])
                add(mine(u, k, y, xx, h, h), got1[u].at[1, k, xx])

            if far:
                send(u, 3, lambda: (mine(u, every, 1 - y, x, 0, h), got2[u].at[0]), ypeer)
                send(u, 4, lambda: (mine(u, every, y, 1 - x, h, h), got2[u].at[1]), xpeer)

    def stage3(u):
        h, n = unit_shape(u)
        if u == "dz":
            wait(u, 5, got1[u].at[0])
            wait(u, 7, got1[u].at[2])
            for xx in (1 - x, x):
                for yy in range(2):
                    at = mine(u, z, yy, xx, 0, 64)
                    total = at[...].astype(jnp.float32)
                    for j in (0, 2):
                        total = total + got1[u][j, yy, xx].astype(jnp.float32)
                    at[...] = total.astype(jnp.bfloat16)
                if xx is not x:
                    send(u, 1, lambda: (mine(u, z, every, 1 - x, 0, 64), got2[u]), xpeer)
            return
        wait(u, 3, got2[u].at[0])
        wait(u, 4, got2[u].at[1])

        @pl.loop(0, NZ)
        def _(k):
            add(mine(u, k, y, x, 0, h), got2[u].at[0, k])
            add(mine(u, k, y, x, h, h), got2[u].at[1, k])

        for j in (3, 1):

            def make(j=j):
                return mine(u, twin[j], y, x, 0, 2 * h), got3[u].at[j // 2]

            send(u, 5 + j // 2, make, pair_peer)

    def stage4(u):
        h, n = unit_shape(u)
        if u == "dz":
            wait(u, 1, got2[u])
            for yy in (1 - y, y):
                add(mine(u, z, yy, x, 0, 64), got2[u].at[yy])
                if yy is not y:
                    send(u, 3, lambda: (mine(u, z, 1 - y, x, 0, 64), got3[u]), ypeer)
            return
        wait(u, 6, got3[u].at[1])
        add(mine(u, twin[2], y, x, 0, 2 * h), got3[u].at[1])
        send(u, 7, lambda: (mine(u, twin[2], y, x, 0, 2 * h), got3[u].at[2]), twin_peer)

    finals = []

    def stage5(u):
        h, n = unit_shape(u)
        total = mine(u, z, y, x, 0, 2 * h)[...].astype(jnp.float32)
        if u == "dz":
            wait(u, 3, got3[u])
            total = total + got3[u][...].astype(jnp.float32)
        else:
            wait(u, 5, got3[u].at[0])
            wait(u, 7, got3[u].at[2])
            total = total + got3[u][0].astype(jnp.float32) + got3[u][2].astype(jnp.float32)
        res[u][...] = total
        result(u).start()
        finals.append(u)

    def result(u):
        dst = {
            "d0": o_gdown.at[pl.ds(0, 64)],
            "dz": o_gdown.at[pl.ds(64, 64)],
            "u0": o_gup.at[:, pl.ds(0, 2048)],
            "u1": o_gup.at[:, pl.ds(2048, 2048)],
            "o": o_gout,
            "q": o_gqkv.at[:, pl.ds(0, 1024)],
            "k": o_gqkv.at[:, pl.ds(1024, 1024)],
            "v": o_gqkv.at[:, pl.ds(2048, 1024)],
        }[u]
        return pltpu.make_async_copy(res[u], dst, osem.at[index[u]])

    stages = (stage0, stage1, stage2, stage3, stage4, stage5)
    stage0("d0")
    stage0("dz")

    def local(src, dst, k):
        cp = pltpu.make_async_copy(src, dst, lsem.at[k])
        cp.start()
        return cp

    row_steps = [(f_down, i) for i in range(8)] + [(f_out, i) for i in range(2)]
    row_steps += [(f_down, i) for i in range(8)]
    wide_steps = [(f_up, 4096, i) for i in range(4)] + [(f_qkv, 3072, i) for i in range(4)]
    part_steps = [(h_slope, i) for i in range(8)] + [(h_act, i) for i in range(8)]

    def row_copy(j):
        ref, i = row_steps[j]
        return pltpu.make_async_copy(ref.at[pl.ds(i * 512, 512)], rows_buf.at[j % 2], rsems.at[j % 2])

    def wide_copy(j):
        ref, n, i = wide_steps[j]
        dst = wide_buf.at[j % 2, :, pl.ds(0, n)]
        return pltpu.make_async_copy(ref.at[pl.ds(i * 256, 256)], dst, wsems.at[j % 2])

    def part_copy(j):
        ref, i = part_steps[j]
        return pltpu.make_async_copy(ref.at[:, pl.ds(i * 512, 512)], part_buf.at[j % 2], psems.at[j % 2])

    early = [local(h_cot, cot, 0), local(h_second, second, 2)]
    for copy in (row_copy, part_copy, wide_copy):
        copy(0).start()
        copy(1).start()
    early += [
        local(h_middle, middle, 1),
        local(h_gain, gains, 3),
        local(h_context, context, 4),
    ]

    def following(copy, steps, j):
        if j + 2 < len(steps):
            copy(j + 2).start()

    def run(order, work):
        for name in order:
            if "." in name:
                u, k = name.split(".")
                (work["gain"] if u == "g" else functools.partial(stages[int(k)], u))(
                    *([int(k)] if u == "g" else [])
                )
            else:
                short = name.rstrip("0123456789")
                rest = name[len(short) :]
                work[short](*([int(rest)] if rest else []))

    def phase_one(dhid):
        def chunk(i):
            if i == 0:
                early[0].wait()
                early[1].wait()
            slot = i % 2
            s = slice(i * 512, (i + 1) * 512)
            row_copy(i).wait()
            part_copy(i).wait()
            grown = dot(cot[...], rows_buf[slot], 1, 1) * part_buf[slot].astype(jnp.float32)
            dhid[:, s] = grown.astype(jnp.bfloat16)
            following(row_copy, row_steps, i)
            following(part_copy, part_steps, i)
            t = slice((i % 4) * 512, (i % 4 + 1) * 512)
            put("u0" if i < 4 else "u1", t, second, dhid[:, s])

        def grad_second(i):
            wide_copy(i).wait()
            s = slice(i * 256, (i + 1) * 256)
            dmid[:, s] = dot(dhid[...], wide_buf[i % 2], 1, 1)
            following(wide_copy, wide_steps, i)

        def norm_back_two():
            for cp in early[2:]:
                cp.wait()
            gain_sum[...] = jnp.zeros_like(gain_sum)

            def step(r):
                v, dn = middle[r, :], dmid[r, :]
                sc = scale_of(v)
                gain_sum[1:2, :] += jnp.sum(dn * v * sc, axis=0, keepdims=True)
                scaled = dn * gains[1:2, :]
                inner = jnp.mean(scaled * v, axis=-1, keepdims=True)
                total = cot[r, :].astype(jnp.float32) + (sc * scaled - v * (sc * sc * sc) * inner)
                dmid[r, :] = total
                low[r, :] = total.astype(jnp.bfloat16)

            rows_loop(step)

        run(NEAR, {"c": chunk, "ds": grad_second, "nb": norm_back_two})

    f32, bf = jnp.float32, jnp.bfloat16
    pl.run_scoped(phase_one, pltpu.VMEM((512, 4096), bf))

    def phase_two(qkv, dqkv, bias, lse, dk_sum, dv_sum):
        load_qkv = local(h_qkv, qkv, 1)
        load_lse = local(h_lse, lse, 3)
        load_tokens = local(h_tokens, second, 2)
        late = {}

        def grad_out(i):
            s = slice(i * 512, (i + 1) * 512)
            put("o", s, context, low[:, s])

        def grad_context(i):
            j = 8 + i
            row_copy(j).wait()
            s = slice(i * 512, (i + 1) * 512)
            dcontext[:, s] = dot(low[...], rows_buf[j % 2], 1, 1).astype(bf)
            following(row_copy, row_steps, j)

        def attend_back(pair):
            if pair == 0:
                load_qkv.wait()
                load_lse.wait()
                write_bias(lengths, bias)
            lane = lax.broadcasted_iota(jnp.int32, (1, 128), 1)
            lower = lane < HD
            col = pair * 128
            scale = 1.0 / math.sqrt(HD)
            for r0 in (256, 0):
                limit = r0 + 256
                q = qkv[r0:limit, col : col + 128]
                do = dcontext[r0:limit, col : col + 128]
                k = qkv[0:limit, 1024 + col : 1152 + col]
                v = qkv[0:limit, 2048 + col : 2176 + col]
                parts, dk, dv = [], None, None
                for h in range(2):
                    keep_lane = lower if h == 0 else ~lower
                    qh = jnp.where(keep_lane, q, jnp.zeros_like(q))
                    dh = jnp.where(keep_lane, do, jnp.zeros_like(do))
                    sums = jnp.where(lane == pair * 2 + h, lse[r0:limit, :], 0.0)
                    sums = jnp.sum(sums, axis=1, keepdims=True)
                    prob = jnp.exp2(dot(qh, k, 1, 1) * SCALE2 + bias[r0:limit, 0:limit] - sums)
                    scaled = prob * dot(dh, v, 1, 1)
                    inner = jnp.sum(scaled, axis=1, keepdims=True)
                    dlogit = (scaled - prob * inner).astype(bf)
                    parts.append(dot(dlogit, k, 1, 0))
                    dk_h = dot(dlogit, qh, 0, 0)
                    dv_h = dot(prob.astype(bf), dh, 0, 0)
                    dk = dk_h if dk is None else dk + dk_h
                    dv = dv_h if dv is None else dv + dv_h
                dqkv[r0:limit, col : col + 128] = (
                    jnp.where(lower, parts[0], parts[1]) * scale
                ).astype(bf)
                if limit == 512:
                    dk_sum[...] = dk
                    dv_sum[...] = dv
                else:
                    dk_sum[0:limit] += dk
                    dv_sum[0:limit] += dv
            dqkv[:, 1024 + col : 1152 + col] = (dk_sum[...] * scale).astype(bf)
            dqkv[:, 2048 + col : 2176 + col] = dv_sum[...].astype(bf)

        def renorm():
            load_tokens.wait()

            def step(r):
                v = second[r, :].astype(f32)
                context[r, :] = (v * scale_of(v) * gains[0:1, :]).astype(bf)

            rows_loop(step)

        def grad_qkv(j, i):
            s = slice(i * 512, (i + 1) * 512)
            t = slice(j * 1024 + i * 512, j * 1024 + (i + 1) * 512)
            put("qkv"[j], s, context, dqkv[:, t])

        def add_down(i):
            j = 10 + i
            row_copy(j).wait()
            part_copy(8 + i).wait()
            middle[...] = middle[...] + dot(part_buf[i % 2], rows_buf[j % 2], 1, 0)
            following(row_copy, row_steps, j)
            following(part_copy, part_steps, 8 + i)

        def out_end():
            rows_loop(lambda r: dcontext.__setitem__((r, every), middle[r, :].astype(bf)))
            late["out"] = local(dcontext, o_output, 5)

        def grad_normed(i):
            j = 4 + i
            wide_copy(j).wait()
            s = slice(i * 256, (i + 1) * 256)
            middle[:, s] = dot(dqkv[...], wide_buf[j % 2, :, 0:3072], 1, 1)
            following(wide_copy, wide_steps, j)

        def norm_final():
            def step(r):
                v, dn = second[r, :].astype(f32), middle[r, :]
                sc = scale_of(v)
                gain_sum[0:1, :] += jnp.sum(dn * v * sc, axis=0, keepdims=True)
                scaled = dn * gains[0:1, :]
                inner = jnp.mean(scaled * v, axis=-1, keepdims=True)
                total = dmid[r, :] + (sc * scaled - v * (sc * sc * sc) * inner)
                low[r, :] = total.astype(bf)

            rows_loop(step)
            late["tokens"] = local(low, o_tokens, 0)

        partners = (speer, xpeer, ypeer, pair_peer, twin_peer)

        def gain_step(k):
            if k:
                exchange(k - 1).wait()
                gain_sum[...] = gain_sum[...] + got_gain[k - 1]
            if k < 5:
                exchange(k).start()
            else:
                block = pl.multiple_of(me // 4 * 128, 128)
                o_gain[...] = gain_sum[:, pl.ds(block, 128)]

        def exchange(k):
            return remote(gain_sum, got_gain.at[k], gs.at[k], gr.at[k], partners[k])

        F = functools.partial
        run(
            LATE,
            {
                "go": grad_out,
                "dc": grad_context,
                "a": attend_back,
                "rn": renorm,
                "gq": F(grad_qkv, 0),
                "gk": F(grad_qkv, 1),
                "gv": F(grad_qkv, 2),
                "ad": add_down,
                "oe": out_end,
                "dn": grad_normed,
                "nf": norm_final,
                "gain": gain_step,
            },
        )
        for cp in late.values():
            cp.wait()

    pl.run_scoped(
        phase_two,
        pltpu.VMEM((512, 3072), bf),
        pltpu.VMEM((512, 3072), bf),
        pltpu.VMEM((512, 512), f32),
        pltpu.VMEM((512, 128), f32),
        pltpu.VMEM((512, 128), f32),
        pltpu.VMEM((512, 128), f32),
    )
    for u in UNITS:
        for copy in sent[u]:
            copy().wait_send()
    for u in finals:
        result(u).wait()


def backward(whole, saved, tokens, cotangent, lengths):
    gains, qkv, context, lse, middle, second, active, slope, grad_down = saved
    grad_down = grad_down.reshape(4, 2, 2, 128, 1024)
    hbm = pl.BlockSpec(memory_space=pl.ANY)
    vmem = pl.BlockSpec(memory_space=pltpu.VMEM)
    smem = pl.BlockSpec(memory_space=pltpu.SMEM)
    bf, f32, dma = jnp.bfloat16, jnp.float32, pltpu.SemaphoreType.DMA
    per = {u: unit_shape(u) for u in UNITS}
    got1 = [(2, 4, 2, h, n) if u != "dz" else (3, 2, 2, 64, n) for u, (h, n) in per.items()]
    got2 = [(2, 4, h, n) if u != "dz" else (2, 64, n) for u, (h, n) in per.items()]
    got3 = [(3, 2 * h, n) if u != "dz" else (64, n) for u, (h, n) in per.items()]
    scratch = (
        [(v, bf) for v in got1 + got2 + got3]
        + [((2 * h, n), f32) for h, n in per.values()]
        + [
            ((4, 2, 2, 128, 1024), bf),
            ((4, 2, 2, 32, 2048), bf),
            ((4, 2, 2, 32, 2048), bf),
            ((4, 2, 2, 32, 1024), bf),
            ((4, 2, 2, 32, 1024), bf),
            ((4, 2, 2, 32, 1024), bf),
            ((4, 2, 2, 32, 1024), bf),
            ((4, 2, 2, 32, 2048), bf),
            ((4, 2, 2, 32, 2048), bf),
            ((4, 2, 2, 128, 1024), bf),
            ((4, 2, 2, 32, 2048), bf),
            ((512, 1024), bf),
            ((512, 1024), f32),
            ((512, 1024), f32),
            ((2, 512, 1024), bf),
            ((2, 256, 4096), bf),
            ((2, 512, 512), bf),
            ((512, 1024), bf),
            ((512, 1024), bf),
            ((512, 1024), bf),
            ((512, 1024), bf),
            ((8, 1024), f32),
            ((8, 1024), f32),
            ((5, 8, 1024), f32),
        ]
    )
    outs = [
        ((512, 1024), bf),
        ((512, 1024), bf),
        ((32, 3072), f32),
        ((32, 1024), f32),
        ((32, 4096), f32),
        ((128, 1024), f32),
        ((8, 128), f32),
    ]
    nu = len(UNITS)
    return pl.pallas_call(
        backward_kernel,
        out_shape=[jax.ShapeDtypeStruct(*o) for o in outs],
        in_specs=[hbm] * 15 + [smem],
        out_specs=[hbm] * 6 + [vmem],
        scratch_shapes=[pltpu.VMEM(*v) for v in scratch]
        + [
            dma((nu, 8)),
            dma((nu, 8)),
            dma((9,)),
            dma((nu,)),
            dma((2,)),
            dma((2,)),
            dma((2,)),
            dma((5,)),
            dma((5,)),
            pltpu.SemaphoreType.REGULAR,
        ],
        compiler_params=pltpu.CompilerParams(
            collective_id=1, has_side_effects=True, vmem_limit_bytes=63 << 20
        ),
    )(
        *whole, qkv, context, lse, middle, second, active, slope, grad_down, gains, tokens, cotangent, lengths
    )


def project_input(inputs, w_qkv, gain):
    normed, scale_one = normalize(inputs, gain)
    normed_low = normed.astype(jnp.bfloat16)
    mixed = jnp.dot(normed_low, w_qkv, preferred_element_type=jnp.float32).astype(jnp.bfloat16)
    split = mixed.reshape(inputs.shape[0], 3, H, HD)
    return (normed_low, scale_one, split[:, 0], split[:, 1], split[:, 2])


def feed_inputs(inputs, context, w_out, w_up, gain):
    middle = inputs + jnp.dot(context, w_out, preferred_element_type=jnp.float32)
    second, scale_two = normalize(middle, gain)
    second_low = second.astype(jnp.bfloat16)
    hidden = jnp.dot(second_low, w_up, preferred_element_type=jnp.float32)
    active = jax.nn.gelu(hidden, approximate=True).astype(jnp.bfloat16)
    return (middle, scale_two, second_low, hidden, active)


def layer(tokens, lengths, w_qkv, w_out, w_up, w_down, gain_attn, gain_mlp, cotangent, low_type):
    total_rows = tokens.shape[0]
    ends = jnp.cumsum(lengths[0])
    places = jnp.arange(total_rows, dtype=jnp.int32)
    segment = jnp.sum((places[:, None] >= ends[None, :]).astype(jnp.int32), axis=1)
    inputs = tokens.astype(jnp.float32)
    gain_attn, gain_mlp = gain_attn.astype(jnp.float32), gain_mlp.astype(jnp.float32)
    normed_low, scale_one, queries, keys_all, values_all = project_input(inputs, w_qkv, gain_attn)
    context_full, log_sums = attend_forward(queries, keys_all, values_all, segment)
    context = context_full.reshape(total_rows, H * HD).astype(jnp.bfloat16)
    middle, scale_two, second_low, hidden, active = feed_inputs(
        inputs, context, w_out, w_up, gain_mlp
    )
    output = (middle + jnp.dot(active, w_down, preferred_element_type=jnp.float32)).astype(
        jnp.bfloat16
    )
    grad_down = jnp.einsum("rf,rd->fd", active, cotangent, preferred_element_type=low_type)
    grad_active = jnp.einsum("rd,fd->rf", cotangent, w_down, preferred_element_type=jnp.float32)
    unused, gelu_pull = jax.vjp(lambda values: jax.nn.gelu(values, approximate=True), hidden)
    grad_hidden = gelu_pull(grad_active)[0].astype(jnp.bfloat16)
    grad_up = jnp.einsum("rd,rf->df", second_low, grad_hidden, preferred_element_type=low_type)
    grad_second = jnp.einsum("rf,df->rd", grad_hidden, w_up, preferred_element_type=jnp.float32)
    grad_mid_norm, grad_gain_m = norm_back(grad_second, middle, scale_two, gain_mlp)
    grad_middle = cotangent.astype(jnp.float32) + grad_mid_norm
    grad_mid_low = grad_middle.astype(jnp.bfloat16)
    grad_out = jnp.einsum("rc,rd->cd", context, grad_mid_low, preferred_element_type=low_type)
    grad_context = jnp.einsum("rd,cd->rc", grad_mid_low, w_out, preferred_element_type=jnp.float32)
    grad_context = grad_context.astype(jnp.bfloat16).reshape(total_rows, H, HD)
    grad_queries, grad_keys, grad_values = attend_backward(
        queries, keys_all, values_all, segment, log_sums, grad_context
    )
    grad_mixed = (
        jnp.stack([grad_queries, grad_keys, grad_values], axis=1)
        .reshape(total_rows, 3 * H * HD)
        .astype(jnp.bfloat16)
    )
    grad_qkv = jnp.einsum("rd,re->de", normed_low, grad_mixed, preferred_element_type=low_type)
    grad_normed = jnp.einsum("re,de->rd", grad_mixed, w_qkv, preferred_element_type=jnp.float32)
    grad_in_norm, grad_gain_a = norm_back(grad_normed, inputs, scale_one, gain_attn)
    grad_tokens = (grad_middle + grad_in_norm).astype(jnp.bfloat16)
    return (output, grad_tokens, grad_qkv, grad_out, grad_up, grad_down, grad_gain_a, grad_gain_m)


def shards_any(tokens, lengths, w_qkv, w_out, w_up, w_down, gain_attn, gain_mlp, cotangent):
    whole = gather_any(w_qkv, w_out, w_up, w_down, gain_attn, gain_mlp)
    out = layer(tokens, lengths, *whole, cotangent, jnp.float32)
    return out[:2] + sum_any(*out[2:])


def keep_kernel(*refs):
    n = (len(refs) - 2) // 3
    gets, puts = refs[-2:]
    into = [pltpu.make_async_copy(refs[i], refs[2 * n + i], gets.at[i]) for i in range(n)]
    back = [pltpu.make_async_copy(refs[2 * n + i], refs[n + i], puts.at[i]) for i in range(n)]
    for cp in into:
        cp.start()
    for i in range(n):
        into[i].wait()
        back[i].start()
    for cp in back:
        cp.wait()


def keep(arrays):
    hbm = pl.BlockSpec(memory_space=pl.ANY)
    return pl.pallas_call(
        keep_kernel,
        out_shape=[jax.ShapeDtypeStruct(a.shape, a.dtype) for a in arrays],
        in_specs=[hbm] * len(arrays),
        out_specs=[hbm] * len(arrays),
        scratch_shapes=[pltpu.VMEM(a.shape, a.dtype) for a in arrays]
        + [pltpu.SemaphoreType.DMA((len(arrays),))] * 2,
    )(*arrays)


def shards(tokens, lengths, w_qkv, w_out, w_up, w_down, gain_attn, gain_mlp, cotangent):
    me = lax.axis_index("dp") * 4 + lax.axis_index("fsdp")
    lanes = lax.rem(me, 4) * 32
    pair = jnp.stack([gain_attn, gain_mlp]).astype(jnp.float32)
    spot = lax.dynamic_update_slice(jnp.zeros((8, 128), jnp.float32), pair, (0, lanes))
    whole, saved = forward((w_qkv, w_out, w_up, w_down), spot, lengths, tokens, cotangent)
    output, grad_tokens, g_qkv, g_out, g_up, g_down, g_gain = backward(
        whole, saved, tokens, cotangent, lengths
    )
    own = lax.dynamic_slice(g_gain, (0, lanes), (2, 32))
    kept = keep((output, grad_tokens, g_qkv, g_out, g_up, g_down))
    return (*kept, own[0], own[1])


def solution(mesh):
    rows, flat = P(AXES, None), P(AXES)
    known = dict(mesh.shape) == {"dp": 8, "fsdp": 4}
    return jax.shard_map(
        shards if known else shards_any,
        mesh=mesh,
        in_specs=(rows, rows, rows, rows, rows, rows, flat, flat, rows),
        out_specs=(rows, rows, rows, rows, rows, rows, flat, flat),
        check_vma=False,
    )
```
